32 devices in a mesh: entries: 16 (over z, x, core), feat: 2 (over y).
Axes of the slice: x: 2, y: 2, z: 4, core: 2. Of those that a mesh axis runs over, the one named last changes fastest.
Arguments:
- pieces: bfloat16 [4672, 7, 512], P(('entries', 'feat')), may hold values from -6 to 6
- lengths: int32 [4672], P(('entries', 'feat')), may hold values from 1 to 7
- entry_group: int32 [4672], P(('entries', 'feat')), may hold values from 0 to 3
- group_table: bfloat16 [4, 512], P(None, ('entries', 'feat')), may hold values from -6 to 6
- ln1_gain: bfloat16 [512], P(('entries', 'feat')), may hold values from 0.099609375 to 1.8984375
- w_qkv: bfloat16 [512, 1536], P(('entries', 'feat')), may hold values from -0.25 to 0.25
- w_out: bfloat16 [512, 512], P(('entries', 'feat')), may hold values from -0.5 to 0.5
- ln2_gain: bfloat16 [512], P(('entries', 'feat')), may hold values from 0.099609375 to 1.8984375
- w_up: bfloat16 [512, 2048], P(('entries', 'feat')), may hold values from -0.25 to 0.25
- w_down: bfloat16 [2048, 512], P(('entries', 'feat')), may hold values from -0.1875 to 0.1875
- w_proj: bfloat16 [512, 2048], P(('entries', 'feat')), may hold values from -0.25 to 0.25
- text_ids: int32 [9344], replicated, may hold values from 0 to 4671, as said below
- text_mask: int32 [9344], replicated, may hold values from 0 to 1
- grad_embed: bfloat16 [2048, 9344], P(('entries', 'feat')), may hold values from -6 to 6
Outputs:
- embeddings: bfloat16 [2048, 9344], P(('entries', 'feat'))
- grad_pieces: bfloat16 [4672, 7, 512], P(('entries', 'feat'))
- grad_group_table: float32 [4, 512], P(None, ('entries', 'feat'))
- grad_ln1_gain: float32 [512], P(('entries', 'feat'))
- grad_w_qkv: float32 [512, 1536], P(('entries', 'feat'))
- grad_w_out: float32 [512, 512], P(('entries', 'feat'))
- grad_ln2_gain: float32 [512], P(('entries', 'feat'))
- grad_w_up: float32 [512, 2048], P(('entries', 'feat'))
- grad_w_down: float32 [2048, 512], P(('entries', 'feat'))
- grad_w_proj: float32 [512, 2048], P(('entries', 'feat'))
The draws below stay inside these ranges and needn't reach their ends.
Inputs may be any that keep to these rules, and one draw needn't show every extreme that they name: `text_ids`: every entry is read by at least one text row whose text_mask is 1.
All inputs are finite; a program needn't handle non-finite values.
Results may differ from the reference program's by a relative error of at most 0.012.
Values may be sent and summed in bfloat16 or wider, within the bound.
A program may use at most 128 MiB of HBM per device.

```python
import jax
import jax.numpy as jnp
from jax import lax

D = 512
HEADS = 8
HEAD = 64
FF = 2048
FOUT = 2048
PIECES = 7
NG = 4
E_DEV = 146
ENTRIES = 4672
TEXT = 9344


def text_layout(key):
    order = jax.random.permutation(jax.random.fold_in(key, 11), TEXT)
    extra_ids = jax.random.randint(jax.random.fold_in(key, 12), (TEXT,), 0, ENTRIES, dtype=jnp.int32)
    extra_live = (jax.random.randint(jax.random.fold_in(key, 13), (TEXT,), 0, 8, dtype=jnp.int32) < 7).astype(jnp.int32)
    position = jnp.arange(TEXT, dtype=jnp.int32)
    covering = position < ENTRIES
    base_ids = jnp.where(covering, position, extra_ids)
    base_keep = jnp.where(covering, jnp.ones_like(extra_live), extra_live)
    placed_ids = jnp.zeros((TEXT,), jnp.int32).at[order].set(base_ids)
    placed_keep = jnp.zeros((TEXT,), jnp.int32).at[order].set(base_keep)
    return (placed_ids, placed_keep)


def draw_text_ids(key, part):
    placed_ids, placed_keep = text_layout(key)
    return placed_ids


def draw_text_mask(key, part):
    placed_ids, placed_keep = text_layout(key)
    return placed_keep


def touch_ends(result, stream_key, least, high):
    longest = result.shape.index(max(result.shape))
    spots = []
    for shift in (0, 1):
        where = [jax.random.randint(jax.random.fold_in(stream_key, axis), (), 0, length) for axis, length in enumerate(result.shape)]
        where[longest] = (where[longest] + shift) % result.shape[longest]
        spots.append(tuple(where))
    return result.at[spots[0]].set(least).at[spots[1]].set(high)


def block_levels(key, extent, split, least, largest):
    gain = 1.0
    for dim, shards_of in split:
        steps = jax.random.uniform(jax.random.fold_in(jax.random.fold_in(key, 6), dim), (shards_of,), jnp.float32, least / len(split), largest / len(split))
        gain = gain * jnp.repeat(jnp.exp(steps), extent[dim] // shards_of).reshape((-1,) + (1,) * (len(extent) - 1 - dim))
    return gain


def centred(own_key, extent, scale, limit, cuts=(), kind=jnp.bfloat16):
    values = jax.random.normal(own_key, extent, jnp.float32) * scale
    if len(cuts) > 0:
        values = block_levels(own_key, extent, cuts, -0.22, 0.18) * values
    return jnp.clip(values, min=-limit, max=limit).astype(kind)


def setup_inputs(seed: int = 0) -> dict:
    arg_keys = jax.random.split(jax.random.key(seed), 15)
    pieces = centred(arg_keys[0], (ENTRIES, PIECES, D), 1.0, 6.0, ((0, 32),))
    lengths = touch_ends(jax.random.randint(arg_keys[1], (ENTRIES,), 1, PIECES + 1), jax.random.fold_in(arg_keys[1], 1), 1, PIECES).astype(jnp.int32)
    entry_group = touch_ends(jax.random.randint(arg_keys[2], (ENTRIES,), 0, NG), jax.random.fold_in(arg_keys[2], 1), 0, NG - 1).astype(jnp.int32)
    group_table = centred(arg_keys[3], (NG, D), 1.0, 6.0, ((1, 32),))
    ln1_gain = jnp.clip(1.0 + 0.18 * jax.random.normal(arg_keys[4], (D,), jnp.float32), 0.099609375, 1.8984375).astype(jnp.bfloat16)
    w_qkv = centred(arg_keys[5], (D, 3 * D), D ** -0.5, 0.25, ((0, 32),))
    w_out = centred(arg_keys[6], (D, D), (D // 4) ** -0.5, 0.5, ((0, 32),))
    ln2_gain = jnp.clip(1.0 + 0.18 * jax.random.normal(arg_keys[7], (D,), jnp.float32), 0.099609375, 1.8984375).astype(jnp.bfloat16)
    w_up = centred(arg_keys[8], (D, FF), D ** -0.5, 0.25, ((0, 32),))
    w_down = centred(arg_keys[9], (FF, D), (FF // 2) ** -0.5, 0.1875, ((0, 32),))
    w_proj = centred(arg_keys[10], (D, FOUT), D ** -0.5, 0.25, ((0, 32),))
    text_ids = draw_text_ids(jax.random.fold_in(arg_keys[14], 71), 0)
    text_mask = draw_text_mask(jax.random.fold_in(arg_keys[14], 71), 0)
    grad_embed = centred(arg_keys[13], (FOUT, TEXT), 1.0, 6.0, ((0, 32),))
    return {"pieces": pieces, "lengths": lengths, "entry_group": entry_group, "group_table": group_table, "ln1_gain": ln1_gain, "w_qkv": w_qkv, "w_out": w_out, "ln2_gain": ln2_gain, "w_up": w_up, "w_down": w_down, "w_proj": w_proj, "text_ids": text_ids, "text_mask": text_mask, "grad_embed": grad_embed}


@jax.custom_vjp
def low(v):
    return lax.optimization_barrier(v.astype(jnp.bfloat16)).astype(jnp.float32)

@jax.custom_vjp
def low_back(v):
    return v

def low_keep(v):
    return (low(v), None)

def low_pass(kept, grad):
    return (grad,)

def back_keep(v):
    return (v, None)

def back_low(kept, grad):
    return (low(grad),)
low.defvjp(low_keep, low_pass)
low_back.defvjp(back_keep, back_low)
highest_precision = lax.Precision.HIGHEST
epsilon = 1e-05

def normalize(tensor, gain_vec):
    average = lax.optimization_barrier(jnp.mean(tensor, axis=-1, keepdims=True))
    centered = tensor - average
    spread = lax.optimization_barrier(jnp.mean(centered * centered, axis=-1, keepdims=True))
    return centered * lax.rsqrt(spread + epsilon) * gain_vec

def matmul(left_side, right_side):
    return jnp.dot(left_side, right_side, precision=highest_precision)

def encode_block(pieces, lengths, groups, group_table, gain_one, w_qkv, w_out, gain_two, w_up, w_down, w_proj):
    number = pieces.shape[0]
    slot_ids = jnp.arange(PIECES)
    start_mask = (slot_ids == 0).astype(jnp.float32)
    states = pieces + start_mask[None, :, None] * group_table[groups][:, None, :]
    normed = low(normalize(states, gain_one))
    mixed = low_back(low(jnp.einsum('epd,df->epf', normed, w_qkv, precision=highest_precision)))
    query_heads = mixed[:, 0, :D].reshape(number, HEADS, HEAD)
    key_heads = mixed[:, :, D:2 * D].reshape(number, PIECES, HEADS, HEAD)
    value_heads = mixed[:, :, 2 * D:].reshape(number, PIECES, HEADS, HEAD)
    scale_factor = HEAD ** (-0.5)
    scores = low_back(jnp.einsum('ehd,ephd->ehp', query_heads, key_heads, precision=highest_precision) * scale_factor)
    live_slot = slot_ids[None, :] < lengths[:, None]
    masked = jnp.where(live_slot[:, None, :], scores, -1e+30)
    highest = lax.optimization_barrier(jnp.max(masked, axis=-1, keepdims=True))
    raised = jnp.exp(masked - highest)
    attn_prob = raised / lax.optimization_barrier(jnp.sum(raised, axis=-1, keepdims=True))
    attended = jnp.einsum('ehp,ephd->ehd', low(attn_prob), value_heads, precision=highest_precision)
    attended = low_back(low(attended.reshape(number, D)))
    hidden = states[:, 0] + low_back(matmul(attended, w_out))
    normed_two = low(normalize(hidden, gain_two))
    upward = low_back(matmul(normed_two, w_up))
    activated = low(jax.nn.gelu(upward, approximate=False))
    output = hidden + low_back(matmul(activated, w_down))
    return matmul(low(output), w_proj)

def forward(pieces, group_table, gain_one, w_qkv, w_out, gain_two, w_up, w_down, w_proj, lengths, groups, text_ids, text_keep):
    block_count = ENTRIES // E_DEV

    def encode_one(block_args):
        return encode_block(block_args[0], block_args[1], block_args[2], group_table, gain_one, w_qkv, w_out, gain_two, w_up, w_down, w_proj)
    projected = lax.map(jax.checkpoint(encode_one), (pieces.reshape(block_count, E_DEV, PIECES, D), lengths.reshape(block_count, E_DEV), groups.reshape(block_count, E_DEV)))
    embed_table = low_back(low(projected.reshape(ENTRIES, FOUT)))
    looked = embed_table[text_ids] * text_keep[:, None]
    return looked.T

def reference(pieces, lengths, entry_group, group_table, ln1_gain, w_qkv, w_out, ln2_gain, w_up, w_down, w_proj, text_ids, text_mask, grad_embed):
    as_float = tuple((item.astype(jnp.float32) for item in (pieces, group_table, ln1_gain, w_qkv, w_out, ln2_gain, w_up, w_down, w_proj)))
    text_keep = text_mask.astype(jnp.float32)

    def forward_all(*inputs):
        return forward(*inputs, lengths, entry_group, text_ids, text_keep)
    looked, pullback = jax.vjp(forward_all, *as_float)
    gradients = pullback(grad_embed.astype(jnp.float32))
    return (looked.astype(jnp.bfloat16), gradients[0].astype(jnp.bfloat16), gradients[1], gradients[2], gradients[3], gradients[4], gradients[5], gradients[6], gradients[7], gradients[8])
```

```python
import functools

import jax
import jax.numpy as jnp
from jax import lax
from jax.experimental import pallas as pl
from jax.experimental.pallas import tpu as pltpu
from jax.sharding import PartitionSpec as P

HEADS = 8
HEAD = 64
PIECES = 7
LANES = 128
TBLOCK = 512
AXES = ("entries", "feat")
MESH = pl.DeviceIdType.MESH
VMEM = pltpu.VMEM
BF16 = jnp.bfloat16
F32 = jnp.float32

epsilon = 1e-05


def contract(left_side, right_side, left_dim, right_dim):
    return lax.dot_general(
        left_side,
        right_side,
        (((left_dim,), (right_dim,)), ((), ())),
        preferred_element_type=jnp.float32,
    )


class Place:
    def __init__(self, n_entries):
        entry = lax.axis_index("entries")
        self.n_z = n_entries // 4
        self.n = n_entries * 2
        self.y = lax.axis_index("feat")
        self.c = lax.rem(entry, 2)
        self.x = lax.rem(lax.div(entry, 2), 2)
        self.z = lax.div(entry, 4)
        self.line = entry * 2 + self.y
        first = self.c == 0
        self.x1 = jnp.where(first, 1 - self.x, self.x)
        self.y1 = jnp.where(first, self.y, 1 - self.y)
        self.x2 = jnp.where(first, self.x, 1 - self.x)
        self.y2 = jnp.where(first, 1 - self.y, self.y)

    def at(self, z, x, c, y):
        return ((z * 2 + x) * 2 + c, y)

    def along_z(self, step):
        return lax.rem(self.z + step, self.n_z)


def meet(place):
    barrier = pltpu.get_barrier_semaphore()

    def greet(step, carry):
        other = lax.rem(place.line + step, place.n)
        pl.semaphore_signal(
            barrier,
            inc=1,
            device_id=(lax.div(other, 2), lax.rem(other, 2)),
            device_id_type=MESH,
        )
        return carry

    lax.fori_loop(1, place.n, greet, 0)
    pl.semaphore_wait(barrier, place.n - 1)


def remote(src, dst, send, recv, to):
    return pltpu.make_async_remote_copy(
        src_ref=src, dst_ref=dst, send_sem=send, recv_sem=recv, device_id=to, device_id_type=MESH
    )


class Gather:
    def __init__(self, place, whole, send, recv):
        p = self.place = place
        nz = p.n_z
        self.nz = nz
        mine = whole.at[p.z, p.x, p.c, p.y]
        self.along = [
            remote(mine, mine, send.at[k - 1], recv.at[k - 1], p.at(p.along_z(k), p.x, p.c, p.y))
            for k in range(1, nz)
        ]
        col = [
            whole.at[:, p.x, p.c, p.y],
            whole.at[:, p.x1, p.c, p.y1],
            whole.at[:, p.x2, p.c, p.y2],
            whole.at[:, 1 - p.x, p.c, 1 - p.y],
        ]
        to_one = p.at(p.z, p.x1, p.c, p.y1)
        to_two = p.at(p.z, p.x2, p.c, p.y2)
        to_core = p.at(p.z, p.x, 1 - p.c, p.y)
        s = nz - 1
        self.one = remote(col[0], col[0], send.at[s], recv.at[s], to_one)
        self.two = remote(col[0], col[0], send.at[s + 1], recv.at[s + 1], to_two)
        self.three = remote(col[1], col[1], send.at[s + 2], recv.at[s + 2], to_two)
        self.core = [
            remote(col[k], col[k], send.at[s + 3 + k], recv.at[s + 3 + k], to_core)
            for k in range(4)
        ]

    def step(self, stage):
        if stage == 0:
            for copy in self.along:
                copy.start()
        elif stage == 1:
            for copy in self.along:
                copy.wait_recv()
            self.one.start()
            self.two.start()
            self.core[0].start()
        elif stage == 2:
            self.one.wait_recv()
            self.three.start()
            self.core[1].start()
        elif stage == 3:
            self.two.wait_recv()
            self.core[2].start()
        elif stage == 4:
            self.three.wait_recv()
            self.core[3].start()
        elif stage == 5:
            for copy in self.core:
                copy.wait_recv()

    def finish(self):
        for copy in self.along + [self.one, self.two, self.three] + self.core:
            copy.wait_send()


class Reduce:
    def __init__(self, place, parts, held_core, held_one, held_two, held_z, send, recv):
        p = self.place = place
        nz = p.n_z
        self.parts, self.held_core = parts, held_core
        self.held_one, self.held_two, self.held_z = held_one, held_two, held_z
        self.cols = [(p.x, p.y), (p.x1, p.y1), (p.x2, p.y2), (1 - p.x, 1 - p.y)]
        to_one = p.at(p.z, p.x1, p.c, p.y1)
        to_two = p.at(p.z, p.x2, p.c, p.y2)
        to_core = p.at(p.z, p.x, 1 - p.c, p.y)

        def col(k):
            return parts.at[:, self.cols[k][0], p.c, self.cols[k][1]]

        self.core = remote(parts.at[:, :, 1 - p.c], held_core, send.at[0], recv.at[0], to_core)
        self.one = [
            remote(col(1), held_one.at[0], send.at[1], recv.at[1], to_one),
            remote(col(3), held_one.at[1], send.at[2], recv.at[2], to_one),
        ]
        self.two = remote(col(2), held_two, send.at[3], recv.at[3], to_two)
        self.along = [
            remote(
                parts.at[p.along_z(k), p.x, p.c, p.y],
                held_z.at[k - 1],
                send.at[3 + k],
                recv.at[3 + k],
                p.at(p.along_z(k), p.x, p.c, p.y),
            )
            for k in range(1, nz)
        ]

    def add(self, k, other):
        p, (x, y) = self.place, self.cols[k]
        self.parts[:, x, p.c, y] = (
            self.parts[:, x, p.c, y].astype(F32) + other.astype(F32)
        ).astype(BF16)

    def step(self, stage, out=None):
        if stage == 0:
            self.core.start()
        elif stage == 1:
            self.core.wait_recv()
            for k in (3, 1, 2, 0):
                x, y = self.cols[k]
                self.add(k, self.held_core[:, x, y])
                if k == 3:
                    self.one[1].start()
                if k == 1:
                    self.one[0].start()
        elif stage == 2:
            self.one[1].wait_recv()
            self.add(2, self.held_one[1])
            self.two.start()
            self.one[0].wait_recv()
            self.add(0, self.held_one[0])
        elif stage == 3:
            self.two.wait_recv()
            self.add(0, self.held_two[...])
            for copy in self.along:
                copy.start()
        elif stage == 4:
            p = self.place
            total = self.parts[p.z, p.x, p.c, p.y].astype(F32)
            for k, copy in enumerate(self.along):
                copy.wait_recv()
                total = total + self.held_z[k].astype(F32)
            out[...] = total

    def finish(self):
        for copy in [self.core] + self.one + [self.two] + self.along:
            copy.wait_send()


def exchange(place, src, dst, send, recv):
    dst[place.line] = src[place.line]

    def begin(step, carry):
        other = lax.rem(place.line + step, place.n)
        remote(
            src.at[other],
            dst.at[place.line],
            send.at[step],
            recv.at[step],
            (lax.div(other, 2), lax.rem(other, 2)),
        ).start()
        return carry

    lax.fori_loop(1, place.n, begin, 0)


def exchange_wait(place, src, dst, send, recv, sends):
    def end(step, carry):
        other = lax.rem(place.line + step, place.n)
        copy = remote(
            src.at[other],
            dst.at[place.line],
            send.at[step],
            recv.at[step],
            (lax.div(other, 2), lax.rem(other, 2)),
        )
        if sends:
            copy.wait_send()
        else:
            copy.wait_recv()
        return carry

    lax.fori_loop(1, place.n, end, 0)


def text_blocks(length):
    whole = length // TBLOCK
    return whole, length - whole * TBLOCK


def one_hot(keys, depth):
    width = keys.shape[1]
    return (lax.broadcasted_iota(jnp.int32, (depth, width), 0) == keys).astype(F32).astype(BF16)


def scatter_block(start, width, row_ref, seg_ref, cot_ref, acc_ref):
    span = pl.ds(start, width)
    hot = one_hot(row_ref[:, span], acc_ref.shape[0])
    seg = seg_ref[:, span]
    cot = cot_ref[:, span].astype(F32)
    segments = acc_ref.shape[1] // cot.shape[0]
    spread = jnp.concatenate(
        [jnp.where(seg == q, cot, 0.0).astype(BF16) for q in range(segments)], axis=0
    )
    acc_ref[...] += contract(hot, spread, 1, 1)


def lookup_block(start, width, row_ref, seg_ref, table_ref, out_ref):
    span = pl.ds(start, width)
    hot = one_hot(row_ref[:, span], table_ref.shape[1])
    seg = seg_ref[:, span]
    wide = jnp.dot(table_ref[...], hot, preferred_element_type=F32)
    feats = out_ref.shape[0]
    found = jnp.zeros((feats, width), F32)
    for q in range(table_ref.shape[0] // feats):
        found = found + jnp.where(seg == q, wide[q * feats : (q + 1) * feats], 0.0)
    out_ref[:, span] = found.astype(BF16)


N_WEIGHTS = 5


def gather_kernel(n_entries, *refs):
    shards = refs[:N_WEIGHTS]
    row_ref, seg_ref, cot_ref = refs[N_WEIGHTS : N_WEIGHTS + 3]
    wholes = refs[N_WEIGHTS + 3 : 2 * N_WEIGHTS + 3]
    back_ref = refs[2 * N_WEIGHTS + 3]
    acc_ref, sent_ref, g_send, g_recv, x_send, x_recv = refs[2 * N_WEIGHTS + 4 :]
    place = Place(n_entries)
    n = place.n
    gathers = [
        Gather(place, whole, g_send.at[i], g_recv.at[i]) for i, whole in enumerate(wholes)
    ]
    for shard, whole in zip(shards, wholes):
        whole[place.z, place.x, place.c, place.y] = shard[...]
    acc_ref[...] = jnp.zeros_like(acc_ref)
    meet(place)
    slots = N_WEIGHTS + 5
    whole_blocks, tail = text_blocks(row_ref.shape[1])
    for slot in range(slots):
        for i in range(N_WEIGHTS):
            if 0 <= slot - i <= 5:
                gathers[i].step(slot - i)
        low, high = slot * whole_blocks // slots, (slot + 1) * whole_blocks // slots

        def block(i, carry):
            scatter_block(
                pl.multiple_of(i * TBLOCK, TBLOCK), TBLOCK, row_ref, seg_ref, cot_ref, acc_ref
            )
            return carry

        lax.fori_loop(low, high, block, 0)
    if tail:
        scatter_block(whole_blocks * TBLOCK, tail, row_ref, seg_ref, cot_ref, acc_ref)
    half, rows = n // 2, sent_ref.shape[1]

    def pack(i, carry):
        span = pl.ds(pl.multiple_of(i * rows, rows), rows)
        sent_ref[i] = acc_ref[span, :LANES].astype(BF16)
        sent_ref[i + half] = acc_ref[span, LANES:].astype(BF16)
        return carry

    lax.fori_loop(0, half, pack, 0)
    exchange(place, sent_ref, back_ref, x_send, x_recv)
    exchange_wait(place, sent_ref, back_ref, x_send, x_recv, False)
    exchange_wait(place, sent_ref, back_ref, x_send, x_recv, True)
    for gather in gathers:
        gather.finish()


def reduce_kernel(n_entries, *refs):
    grads = refs[:N_WEIGHTS]
    sent_ref, row_ref, seg_ref = refs[N_WEIGHTS : N_WEIGHTS + 3]
    outs = refs[N_WEIGHTS + 3 : 2 * N_WEIGHTS + 3]
    found_ref = refs[2 * N_WEIGHTS + 3]
    scratch = refs[2 * N_WEIGHTS + 4 :]
    held = scratch[: 4 * N_WEIGHTS]
    came_ref, table_ref, r_send, r_recv, x_send, x_recv = scratch[4 * N_WEIGHTS :]
    place = Place(n_entries)
    n = place.n
    reduces = [
        Reduce(place, grads[i], *held[4 * i : 4 * i + 4], r_send.at[i], r_recv.at[i])
        for i in range(N_WEIGHTS)
    ]
    meet(place)
    for reduce in reduces:
        reduce.step(0)
    exchange(place, sent_ref, came_ref, x_send, x_recv)
    order = (4, 3, 2, 1, 0)
    for i in order:
        reduces[i].step(1)
    exchange_wait(place, sent_ref, came_ref, x_send, x_recv, False)
    half, rows = n // 2, sent_ref.shape[1]
    for side in range(2):
        part = came_ref[side * half : (side + 1) * half].reshape(half * rows, LANES)
        table_ref[side * LANES : (side + 1) * LANES, :] = part.astype(F32).T.astype(BF16)
    slots = N_WEIGHTS + 2
    whole_blocks, tail = text_blocks(row_ref.shape[1])
    for slot in range(slots):
        for k, i in enumerate(order):
            if 2 <= slot - k + 2 <= 4:
                reduces[i].step(slot - k + 2, outs[i])
        low, high = slot * whole_blocks // slots, (slot + 1) * whole_blocks // slots

        def block(i, carry):
            lookup_block(
                pl.multiple_of(i * TBLOCK, TBLOCK), TBLOCK, row_ref, seg_ref, table_ref, found_ref
            )
            return carry

        lax.fori_loop(low, high, block, 0)
    if tail:
        lookup_block(whole_blocks * TBLOCK, tail, row_ref, seg_ref, table_ref, found_ref)
    exchange_wait(place, sent_ref, came_ref, x_send, x_recv, True)
    for reduce in reduces:
        reduce.finish()


def normalize_parts(tensor, gain_vec):
    average = jnp.mean(tensor, axis=-1, keepdims=True)
    centered = tensor - average
    scaled_inv = lax.rsqrt(jnp.mean(centered * centered, axis=-1, keepdims=True) + epsilon)
    unit_form = centered * scaled_inv
    return (unit_form * gain_vec, unit_form, scaled_inv)


def normalize_back(grad_out, gain_vec, unit_form, scaled_inv):
    grad_unit = grad_out * gain_vec
    first_mean = jnp.mean(grad_unit, axis=-1, keepdims=True)
    second_mean = jnp.mean(grad_unit * unit_form, axis=-1, keepdims=True)
    return scaled_inv * (grad_unit - first_mean - unit_form * second_mean)


def forward_part(weights, pieces, lengths, groups):
    group_table, gain_one, w_qkv, w_out, gain_two, w_up, w_down, w_proj = weights
    number = pieces.shape[0]
    model_width = w_out.shape[0]
    group_pick = (groups[:, None] == jnp.arange(group_table.shape[0])[None, :]).astype(jnp.float32)
    start_add = jnp.dot(
        group_pick.astype(jnp.bfloat16), group_table, preferred_element_type=jnp.float32
    )
    states = pieces.astype(jnp.float32).at[:, 0, :].add(start_add)
    normed, unit_one, inv_one = normalize_parts(states, gain_one.astype(jnp.float32))
    normed = normed.astype(jnp.bfloat16)
    key_value = jnp.einsum(
        "epd,df->epf", normed, w_qkv[:, model_width:], preferred_element_type=jnp.float32
    ).astype(jnp.bfloat16)
    query_flat = jnp.dot(
        normed[:, 0], w_qkv[:, :model_width], preferred_element_type=jnp.float32
    ).astype(jnp.bfloat16)
    query_heads = query_flat.reshape(number, HEADS, HEAD)
    key_heads = key_value[:, :, :model_width].reshape(number, PIECES, HEADS, HEAD)
    value_heads = key_value[:, :, model_width:].reshape(number, PIECES, HEADS, HEAD)
    scale_factor = HEAD ** (-0.5)
    scores = (
        jnp.einsum("ehd,ephd->ehp", query_heads, key_heads, preferred_element_type=jnp.float32)
        * scale_factor
    )
    live_slot = jnp.arange(PIECES)[None, :] < lengths[:, None]
    masked = jnp.where(live_slot[:, None, :], scores, -1e30)
    highest = jnp.max(masked, axis=-1, keepdims=True)
    raised = jnp.exp(masked - highest)
    attn_prob = raised / jnp.sum(raised, axis=-1, keepdims=True)
    prob_low = attn_prob.astype(jnp.bfloat16)
    attended = jnp.einsum(
        "ehp,ephd->ehd", prob_low, value_heads, preferred_element_type=jnp.float32
    )
    attended = attended.reshape(number, model_width).astype(jnp.bfloat16)
    hidden = states[:, 0] + jnp.dot(attended, w_out, preferred_element_type=jnp.float32)
    normed_two, unit_two, inv_two = normalize_parts(hidden, gain_two.astype(jnp.float32))
    normed_two = normed_two.astype(jnp.bfloat16)
    upward = jnp.dot(normed_two, w_up, preferred_element_type=jnp.float32)
    activated = jax.nn.gelu(upward, approximate=False).astype(jnp.bfloat16)
    output = hidden + jnp.dot(activated, w_down, preferred_element_type=jnp.float32)
    output_low = output.astype(jnp.bfloat16)
    projected = jnp.dot(output_low, w_proj, preferred_element_type=jnp.float32).astype(jnp.bfloat16)
    stored = (
        group_pick,
        normed,
        unit_one,
        inv_one,
        query_heads,
        key_heads,
        value_heads,
        attn_prob,
        prob_low,
        attended,
        unit_two,
        inv_two,
        normed_two,
        upward,
        activated,
        output_low,
    )
    return (projected, stored)


def backward_part(weights, stored, grad_proj):
    group_table, gain_one, w_qkv, w_out, gain_two, w_up, w_down, w_proj = weights
    (
        group_pick,
        normed,
        unit_one,
        inv_one,
        query_heads,
        key_heads,
        value_heads,
        attn_prob,
        prob_low,
        attended,
        unit_two,
        inv_two,
        normed_two,
        upward,
        activated,
        output_low,
    ) = stored
    number = normed.shape[0]
    model_width = w_out.shape[0]
    scale_factor = HEAD ** (-0.5)
    grad_wproj = contract(output_low, grad_proj, 0, 0)
    grad_output = contract(grad_proj, w_proj, 1, 1)
    grad_branch = grad_output.astype(jnp.bfloat16)
    grad_wdown = contract(activated, grad_branch, 0, 0)
    grad_act = contract(grad_branch, w_down, 1, 1)
    gelu_value, gelu_pull = jax.vjp(lambda tensor: jax.nn.gelu(tensor, approximate=False), upward)
    grad_upward = gelu_pull(grad_act)[0].astype(jnp.bfloat16)
    grad_wup = contract(normed_two, grad_upward, 0, 0)
    grad_normed_two = contract(grad_upward, w_up, 1, 1)
    gain_two_f = gain_two.astype(jnp.float32)
    grad_gain_two = jnp.sum(grad_normed_two * unit_two, axis=0)
    grad_hidden = grad_output + normalize_back(grad_normed_two, gain_two_f, unit_two, inv_two)
    grad_attn = grad_hidden.astype(jnp.bfloat16)
    grad_wout = contract(attended, grad_attn, 0, 0)
    grad_attended = (
        contract(grad_attn, w_out, 1, 1).astype(jnp.bfloat16).reshape(number, HEADS, HEAD)
    )
    grad_prob = jnp.einsum(
        "ehd,ephd->ehp", grad_attended, value_heads, preferred_element_type=jnp.float32
    )
    grad_value = jnp.einsum(
        "ehp,ehd->ephd", prob_low, grad_attended, preferred_element_type=jnp.float32
    )
    grad_scores = attn_prob * (grad_prob - jnp.sum(attn_prob * grad_prob, axis=-1, keepdims=True))
    grad_scores = grad_scores.astype(jnp.bfloat16)
    grad_query = (
        jnp.einsum("ehp,ephd->ehd", grad_scores, key_heads, preferred_element_type=jnp.float32)
        * scale_factor
    )
    grad_key = (
        jnp.einsum("ehp,ehd->ephd", grad_scores, query_heads, preferred_element_type=jnp.float32)
        * scale_factor
    )
    grad_query = grad_query.reshape(number, model_width).astype(jnp.bfloat16)
    grad_kv = jnp.concatenate(
        [
            grad_key.reshape(number, PIECES, model_width),
            grad_value.reshape(number, PIECES, model_width),
        ],
        axis=-1,
    ).astype(jnp.bfloat16)
    grad_wq = contract(normed[:, 0], grad_query, 0, 0)
    grad_wkv = jnp.einsum("epd,epf->df", normed, grad_kv, preferred_element_type=jnp.float32)
    grad_wqkv = jnp.concatenate([grad_wq, grad_wkv], axis=1)
    grad_normed = jnp.einsum(
        "epf,df->epd", grad_kv, w_qkv[:, model_width:], preferred_element_type=jnp.float32
    )
    grad_normed = grad_normed.at[:, 0].add(contract(grad_query, w_qkv[:, :model_width], 1, 1))
    grad_gain_one = jnp.sum(grad_normed * unit_one, axis=(0, 1))
    grad_states = normalize_back(grad_normed, gain_one.astype(jnp.float32), unit_one, inv_one)
    grad_states = grad_states.at[:, 0].add(grad_hidden)
    grad_groups = lax.dot_general(
        group_pick, grad_states[:, 0], (((0,), (0,)), ((), ())), precision=lax.Precision.HIGHEST
    )
    grad_terms = (
        grad_groups,
        grad_gain_one,
        grad_wqkv,
        grad_wout,
        grad_gain_two,
        grad_wup,
        grad_wdown,
        grad_wproj,
    )
    return (grad_states.astype(jnp.bfloat16), grad_terms)


def full(shape, dtype):
    return jax.ShapeDtypeStruct(shape, dtype)


def body(
    mesh_shape,
    pieces,
    lengths,
    entry_group,
    group_table,
    ln1_gain,
    w_qkv,
    w_out,
    ln2_gain,
    w_up,
    w_down,
    w_proj,
    text_ids,
    text_mask,
    grad_embed,
):
    n_entries = mesh_shape["entries"]
    n = n_entries * mesh_shape["feat"]
    n_z = n_entries // 4
    number, width = pieces.shape[0], pieces.shape[2]
    shard = ln1_gain.shape[0]
    groups_n = group_table.shape[0]
    feats = grad_embed.shape[0]
    text_len = text_ids.shape[0]
    segs = LANES // feats
    seg_rows = -(-number // segs)
    rows = -(-seg_rows // 16) * 16
    half = n // 2

    small = jnp.concatenate(
        [ln1_gain[:, None], ln2_gain[:, None], group_table.T], axis=1
    )
    w_out_more = jnp.concatenate(
        [w_out, jnp.pad(small, ((0, 0), (0, LANES - small.shape[1])))], axis=1
    )
    source = text_ids // number
    within = text_ids - source * number
    segment = within // seg_rows
    row_key = (source % half) * rows + within - segment * seg_rows
    seg_key = jnp.where(text_mask != 0, (source // half) * segs + segment, -1)
    row_key, seg_key = row_key[None, :], seg_key[None, :]

    vmem = pl.BlockSpec(memory_space=VMEM)
    shards = (w_qkv, w_out_more, w_up, w_down, w_proj)
    lead = (n_z, 2, 2, 2)
    gathered = pl.pallas_call(
        functools.partial(gather_kernel, n_entries),
        out_shape=tuple(full(lead + s.shape, BF16) for s in shards)
        + (full((n, rows, LANES), BF16),),
        in_specs=[vmem] * 8,
        out_specs=(vmem,) * 6,
        scratch_shapes=[
            VMEM((half * rows, 2 * LANES), F32),
            VMEM((n, rows, LANES), BF16),
            pltpu.SemaphoreType.DMA((N_WEIGHTS, n_z + 6)),
            pltpu.SemaphoreType.DMA((N_WEIGHTS, n_z + 6)),
            pltpu.SemaphoreType.DMA((n,)),
            pltpu.SemaphoreType.DMA((n,)),
        ],
        compiler_params=pltpu.CompilerParams(
            collective_id=0, has_side_effects=True, vmem_limit_bytes=56 * 2**20
        ),
    )(*shards, row_key, seg_key, grad_embed)
    g_qkv, g_out, g_up, g_down, g_proj, came = gathered
    g_qkv = g_qkv.reshape(width, -1)
    g_out = g_out.reshape(width, -1)
    g_small = g_out[:, width:]
    weights = (
        g_small[:, 2 : 2 + groups_n].T,
        g_small[:, 0],
        g_qkv,
        g_out[:, :width],
        g_small[:, 1],
        g_up.reshape(width, -1),
        g_down.reshape(-1, width),
        g_proj.reshape(width, -1),
    )
    projected, stored = forward_part(weights, pieces, lengths, entry_group)
    blocks = jnp.pad(projected, ((0, segs * seg_rows - number), (0, 0)))
    blocks = blocks.reshape(segs, seg_rows, n, feats).transpose(2, 1, 0, 3)
    blocks = jnp.pad(
        blocks.reshape(n, seg_rows, LANES), ((0, 0), (0, rows - seg_rows), (0, 0))
    )
    grad_back = came[:, :seg_rows].reshape(n, seg_rows, segs, feats).transpose(2, 1, 0, 3)
    grad_back = grad_back.reshape(segs * seg_rows, n * feats)[:number]
    grad_pieces, terms = backward_part(weights, stored, grad_back)
    d_small = jnp.concatenate([terms[1][:, None], terms[4][:, None], terms[0].T], axis=1)
    d_out = jnp.concatenate(
        [terms[3], jnp.pad(d_small, ((0, 0), (0, LANES - d_small.shape[1])))], axis=1
    )
    grads = tuple(
        g.astype(BF16).reshape(lead + s.shape)
        for g, s in zip((terms[2], d_out, terms[5], terms[6], terms[7]), shards)
    )
    held = []
    for s in shards:
        held += [
            VMEM((n_z, 2, 2) + s.shape, BF16),
            VMEM((2, n_z) + s.shape, BF16),
            VMEM((n_z,) + s.shape, BF16),
            VMEM((n_z - 1,) + s.shape, BF16),
        ]
    summed = pl.pallas_call(
        functools.partial(reduce_kernel, n_entries),
        out_shape=tuple(full(s.shape, F32) for s in shards) + (full((feats, text_len), BF16),),
        in_specs=[vmem] * 8,
        out_specs=(vmem,) * 6,
        scratch_shapes=held
        + [
            VMEM((n, rows, LANES), BF16),
            VMEM((2 * LANES, half * rows), BF16),
            pltpu.SemaphoreType.DMA((N_WEIGHTS, n_z + 4)),
            pltpu.SemaphoreType.DMA((N_WEIGHTS, n_z + 4)),
            pltpu.SemaphoreType.DMA((n,)),
            pltpu.SemaphoreType.DMA((n,)),
        ],
        compiler_params=pltpu.CompilerParams(
            collective_id=1, has_side_effects=True, vmem_limit_bytes=56 * 2**20
        ),
    )(*grads, blocks, row_key, seg_key)
    s_qkv, s_out, s_up, s_down, s_proj, embeddings = summed
    s_small = s_out[:, width:]
    return (
        embeddings,
        grad_pieces,
        s_small[:, 2 : 2 + groups_n].T,
        s_small[:, 0],
        s_qkv,
        s_out[:, :width],
        s_small[:, 1],
        s_up,
        s_down,
        s_proj,
    )


def solution(mesh):
    both = P(AXES)
    rows = P(AXES, None)
    return jax.shard_map(
        functools.partial(body, dict(mesh.shape)),
        mesh=mesh,
        in_specs=(
            P(AXES, None, None),
            both,
            both,
            P(None, AXES),
            both,
            rows,
            rows,
            both,
            rows,
            rows,
            rows,
            P(),
            P(),
            rows,
        ),
        out_specs=(
            rows,
            P(AXES, None, None),
            P(None, AXES),
            both,
            rows,
            rows,
            both,
            rows,
            rows,
            rows,
        ),
        check_vma=False,
    )
```

```python
import functools
import types

import jax
import jax.numpy as jnp
from jax import lax
from jax.experimental import pallas as pl
from jax.experimental.pallas import tpu as pltpu
from jax.sharding import PartitionSpec as P

HEADS = 8
HEAD = 64
PIECES = 7
LANES = 128
TBLOCK = 512
AXES = ("entries", "feat")
MESH = pl.DeviceIdType.MESH
VMEM = pltpu.VMEM
BF16 = jnp.bfloat16
F32 = jnp.float32

epsilon = 1e-05


def contract(left_side, right_side, left_dim, right_dim):
    return lax.dot_general(
        left_side,
        right_side,
        (((left_dim,), (right_dim,)), ((), ())),
        preferred_element_type=jnp.float32,
    )


class Place:
    def __init__(self, n_entries):
        entry = lax.axis_index("entries")
        self.n_z = n_entries // 4
        self.n = n_entries * 2
        self.y = lax.axis_index("feat")
        self.c = lax.rem(entry, 2)
        self.x = lax.rem(lax.div(entry, 2), 2)
        self.z = lax.div(entry, 4)
        self.line = entry * 2 + self.y
        first = self.c == 0
        self.x1 = jnp.where(first, 1 - self.x, self.x)
        self.y1 = jnp.where(first, self.y, 1 - self.y)
        self.x2 = jnp.where(first, self.x, 1 - self.x)
        self.y2 = jnp.where(first, 1 - self.y, self.y)

    def at(self, z, x, c, y):
        return ((z * 2 + x) * 2 + c, y)

    def along_z(self, step):
        return lax.rem(self.z + step, self.n_z)


def meet(place):
    barrier = pltpu.get_barrier_semaphore()

    def greet(step, carry):
        other = lax.rem(place.line + step, place.n)
        pl.semaphore_signal(
            barrier,
            inc=1,
            device_id=(lax.div(other, 2), lax.rem(other, 2)),
            device_id_type=MESH,
        )
        return carry

    lax.fori_loop(1, place.n, greet, 0)
    pl.semaphore_wait(barrier, place.n - 1)


def remote(src, dst, send, recv, to):
    return pltpu.make_async_remote_copy(
        src_ref=src, dst_ref=dst, send_sem=send, recv_sem=recv, device_id=to, device_id_type=MESH
    )


class Gather:
    def __init__(self, place, whole, send, recv):
        p = self.place = place
        nz = p.n_z
        self.nz = nz
        mine = whole.at[p.z, p.x, p.c, p.y]
        self.along = [
            remote(mine, mine, send.at[k - 1], recv.at[k - 1], p.at(p.along_z(k), p.x, p.c, p.y))
            for k in range(1, nz)
        ]
        col = [
            whole.at[:, p.x, p.c, p.y],
            whole.at[:, p.x1, p.c, p.y1],
            whole.at[:, p.x2, p.c, p.y2],
            whole.at[:, 1 - p.x, p.c, 1 - p.y],
        ]
        to_one = p.at(p.z, p.x1, p.c, p.y1)
        to_two = p.at(p.z, p.x2, p.c, p.y2)
        to_core = p.at(p.z, p.x, 1 - p.c, p.y)
        s = nz - 1
        self.one = remote(col[0], col[0], send.at[s], recv.at[s], to_one)
        self.two = remote(col[0], col[0], send.at[s + 1], recv.at[s + 1], to_two)
        self.three = remote(col[1], col[1], send.at[s + 2], recv.at[s + 2], to_two)
        self.core = [
            remote(col[k], col[k], send.at[s + 3 + k], recv.at[s + 3 + k], to_core)
            for k in range(4)
        ]

    def step(self, stage):
        if stage == 0:
            for copy in self.along:
                copy.start()
        elif stage == 1:
            for copy in self.along:
                copy.wait_recv()
            self.one.start()
            self.two.start()
            self.core[0].start()
        elif stage == 2:
            self.one.wait_recv()
            self.three.start()
            self.core[1].start()
        elif stage == 3:
            self.two.wait_recv()
            self.core[2].start()
        elif stage == 4:
            self.three.wait_recv()
            self.core[3].start()
        elif stage == 5:
            for copy in self.core:
                copy.wait_recv()

    def finish(self):
        for copy in self.along + [self.one, self.two, self.three] + self.core:
            copy.wait_send()


class Reduce:
    def __init__(self, place, parts, held_core, held_one, held_two, held_z, send, recv):
        p = self.place = place
        nz = p.n_z
        self.parts, self.held_core = parts, held_core
        self.held_one, self.held_two, self.held_z = held_one, held_two, held_z
        self.cols = [(p.x, p.y), (p.x1, p.y1), (p.x2, p.y2), (1 - p.x, 1 - p.y)]
        to_one = p.at(p.z, p.x1, p.c, p.y1)
        to_two = p.at(p.z, p.x2, p.c, p.y2)
        to_core = p.at(p.z, p.x, 1 - p.c, p.y)

        def col(k):
            return parts.at[:, self.cols[k][0], p.c, self.cols[k][1]]

        self.core = remote(parts.at[:, :, 1 - p.c], held_core, send.at[0], recv.at[0], to_core)
        self.one = [
            remote(col(1), held_one.at[0], send.at[1], recv.at[1], to_one),
            remote(col(3), held_one.at[1], send.at[2], recv.at[2], to_one),
        ]
        self.two = remote(col(2), held_two, send.at[3], recv.at[3], to_two)
        self.along = [
            remote(
                parts.at[p.along_z(k), p.x, p.c, p.y],
                held_z.at[k - 1],
                send.at[3 + k],
                recv.at[3 + k],
                p.at(p.along_z(k), p.x, p.c, p.y),
            )
            for k in range(1, nz)
        ]

    def add(self, k, other):
        p, (x, y) = self.place, self.cols[k]
        self.parts[:, x, p.c, y] = (
            self.parts[:, x, p.c, y].astype(F32) + other.astype(F32)
        ).astype(BF16)

    def step(self, stage, out=None):
        if stage == 0:
            self.core.start()
        elif stage == 1:
            self.core.wait_recv()
            for k in (3, 1, 2, 0):
                x, y = self.cols[k]
                self.add(k, self.held_core[:, x, y])
                if k == 3:
                    self.one[1].start()
                if k == 1:
                    self.one[0].start()
        elif stage == 2:
            self.one[1].wait_recv()
            self.add(2, self.held_one[1])
            self.two.start()
            self.one[0].wait_recv()
            self.add(0, self.held_one[0])
        elif stage == 3:
            self.two.wait_recv()
            self.add(0, self.held_two[...])
            for copy in self.along:
                copy.start()
        elif stage == 4:
            p = self.place
            total = self.parts[p.z, p.x, p.c, p.y].astype(F32)
            for k, copy in enumerate(self.along):
                copy.wait_recv()
                total = total + self.held_z[k].astype(F32)
            out[...] = total

    def finish(self):
        for copy in [self.core] + self.one + [self.two] + self.along:
            copy.wait_send()


def exchange(place, src, dst, send, recv):
    dst[place.line] = src[place.line]

    def begin(step, carry):
        other = lax.rem(place.line + step, place.n)
        remote(
            src.at[other],
            dst.at[place.line],
            send.at[step],
            recv.at[step],
            (lax.div(other, 2), lax.rem(other, 2)),
        ).start()
        return carry

    lax.fori_loop(1, place.n, begin, 0)


def exchange_wait(place, src, dst, send, recv, sends):
    def end(step, carry):
        other = lax.rem(place.line + step, place.n)
        copy = remote(
            src.at[other],
            dst.at[place.line],
            send.at[step],
            recv.at[step],
            (lax.div(other, 2), lax.rem(other, 2)),
        )
        if sends:
            copy.wait_send()
        else:
            copy.wait_recv()
        return carry

    lax.fori_loop(1, place.n, end, 0)


def text_blocks(length):
    whole = length // TBLOCK
    return whole, length - whole * TBLOCK


def one_hot(keys, depth):
    width = keys.shape[1]
    return (lax.broadcasted_iota(jnp.int32, (depth, width), 0) == keys).astype(F32).astype(BF16)


def scatter_block(start, width, row_ref, seg_ref, cot_ref, acc_ref):
    span = pl.ds(start, width)
    hot = one_hot(row_ref[:, span], acc_ref.shape[0])
    seg = seg_ref[:, span]
    cot = cot_ref[:, span].astype(F32)
    segments = acc_ref.shape[1] // cot.shape[0]
    spread = jnp.concatenate(
        [jnp.where(seg == q, cot, 0.0).astype(BF16) for q in range(segments)], axis=0
    )
    acc_ref[...] += contract(hot, spread, 1, 1)


def lookup_block(start, width, row_ref, seg_ref, table_ref, out_ref):
    span = pl.ds(start, width)
    hot = one_hot(row_ref[:, span], table_ref.shape[1])
    seg = seg_ref[:, span]
    wide = jnp.dot(table_ref[...], hot, preferred_element_type=F32)
    feats = out_ref.shape[0]
    found = jnp.zeros((feats, width), F32)
    for q in range(table_ref.shape[0] // feats):
        found = found + jnp.where(seg == q, wide[q * feats : (q + 1) * feats], 0.0)
    out_ref[:, span] = found.astype(BF16)


N_WEIGHTS = 5


def gather_kernel(n_entries, *refs):
    shards = refs[:N_WEIGHTS]
    row_ref, seg_ref, cot_ref = refs[N_WEIGHTS : N_WEIGHTS + 3]
    wholes = refs[N_WEIGHTS + 3 : 2 * N_WEIGHTS + 3]
    back_ref = refs[2 * N_WEIGHTS + 3]
    acc_ref, sent_ref, g_send, g_recv, x_send, x_recv = refs[2 * N_WEIGHTS + 4 :]
    place = Place(n_entries)
    n = place.n
    gathers = [
        Gather(place, whole, g_send.at[i], g_recv.at[i]) for i, whole in enumerate(wholes)
    ]
    for shard, whole in zip(shards, wholes):
        whole[place.z, place.x, place.c, place.y] = shard[...]
    acc_ref[...] = jnp.zeros_like(acc_ref)
    meet(place)
    slots = N_WEIGHTS + 5
    whole_blocks, tail = text_blocks(row_ref.shape[1])
    for slot in range(slots):
        for i in range(N_WEIGHTS):
            if 0 <= slot - i <= 5:
                gathers[i].step(slot - i)
        low, high = slot * whole_blocks // slots, (slot + 1) * whole_blocks // slots

        def block(i, carry):
            scatter_block(
                pl.multiple_of(i * TBLOCK, TBLOCK), TBLOCK, row_ref, seg_ref, cot_ref, acc_ref
            )
            return carry

        lax.fori_loop(low, high, block, 0)
    if tail:
        scatter_block(whole_blocks * TBLOCK, tail, row_ref, seg_ref, cot_ref, acc_ref)
    half, rows = n // 2, sent_ref.shape[1]

    def pack(i, carry):
        span = pl.ds(pl.multiple_of(i * rows, rows), rows)
        sent_ref[i] = acc_ref[span, :LANES].astype(BF16)
        sent_ref[i + half] = acc_ref[span, LANES:].astype(BF16)
        return carry

    lax.fori_loop(0, half, pack, 0)
    exchange(place, sent_ref, back_ref, x_send, x_recv)
    exchange_wait(place, sent_ref, back_ref, x_send, x_recv, False)
    exchange_wait(place, sent_ref, back_ref, x_send, x_recv, True)
    for gather in gathers:
        gather.finish()


def reduce_kernel(n_entries, *refs):
    grads = refs[:N_WEIGHTS]
    sent_ref, row_ref, seg_ref = refs[N_WEIGHTS : N_WEIGHTS + 3]
    outs = refs[N_WEIGHTS + 3 : 2 * N_WEIGHTS + 3]
    found_ref = refs[2 * N_WEIGHTS + 3]
    scratch = refs[2 * N_WEIGHTS + 4 :]
    held = scratch[: 4 * N_WEIGHTS]
    came_ref, table_ref, r_send, r_recv, x_send, x_recv = scratch[4 * N_WEIGHTS :]
    place = Place(n_entries)
    n = place.n
    reduces = [
        Reduce(place, grads[i], *held[4 * i : 4 * i + 4], r_send.at[i], r_recv.at[i])
        for i in range(N_WEIGHTS)
    ]
    meet(place)
    for reduce in reduces:
        reduce.step(0)
    exchange(place, sent_ref, came_ref, x_send, x_recv)
    order = (4, 3, 2, 1, 0)
    for i in order:
        reduces[i].step(1)
    exchange_wait(place, sent_ref, came_ref, x_send, x_recv, False)
    half, rows = n // 2, sent_ref.shape[1]
    for side in range(2):
        part = came_ref[side * half : (side + 1) * half].reshape(half * rows, LANES)
        table_ref[side * LANES : (side + 1) * LANES, :] = part.astype(F32).T.astype(BF16)
    slots = N_WEIGHTS + 2
    whole_blocks, tail = text_blocks(row_ref.shape[1])
    for slot in range(slots):
        for k, i in enumerate(order):
            if 2 <= slot - k + 2 <= 4:
                reduces[i].step(slot - k + 2, outs[i])
        low, high = slot * whole_blocks // slots, (slot + 1) * whole_blocks // slots

        def block(i, carry):
            lookup_block(
                pl.multiple_of(i * TBLOCK, TBLOCK), TBLOCK, row_ref, seg_ref, table_ref, found_ref
            )
            return carry

        lax.fori_loop(low, high, block, 0)
    if tail:
        lookup_block(whole_blocks * TBLOCK, tail, row_ref, seg_ref, table_ref, found_ref)
    exchange_wait(place, sent_ref, came_ref, x_send, x_recv, True)
    for reduce in reduces:
        reduce.finish()


def cast_pair(value):
    high = value.astype(BF16)
    return high, (value - high.astype(F32)).astype(BF16)


def head_ones():
    head_row = lax.broadcasted_iota(jnp.int32, (4 * HEAD, 4 * HEAD), 0) // HEAD
    head_col = lax.broadcasted_iota(jnp.int32, (4 * HEAD, 4 * HEAD), 1) // HEAD
    return (head_row == head_col).astype(F32).astype(BF16)


def head_sum(value, ones):
    high, low = cast_pair(value)
    step = 4 * HEAD
    return jnp.concatenate(
        [
            jnp.dot(high[:, j : j + step], ones, preferred_element_type=F32)
            + jnp.dot(low[:, j : j + step], ones, preferred_element_type=F32)
            for j in range(0, value.shape[1], step)
        ],
        axis=1,
    )


def flat(ref, low=None, high=None):
    value = ref[...] if low is None else ref[:, :, :, :, :, low:high]
    return value.reshape(-1, value.shape[-1])


def spread_segments(blocks, feats, segs):
    lane = lax.broadcasted_iota(jnp.int32, blocks[0].shape, 1) // feats
    out = []
    for h in range(segs):
        whole = None
        for j in range(segs):
            shift = ((j - h) * feats) % LANES
            moved = blocks[j] if shift == 0 else pltpu.roll(blocks[j], shift, 1)
            whole = moved if whole is None else jnp.where(lane == j, moved, whole)
        out.append(whole)
    return out


class Block:
    def __init__(self, m, segs, seg_rows, rows, feats):
        self.m, self.segs, self.seg_rows, self.rows, self.feats = m, segs, seg_rows, rows, feats
        self.number = m.pieces.shape[0]
        self.width = m.pieces.shape[2]
        self.total = segs * rows

    def pieces_of(self, h):
        return min(self.seg_rows, max(self.number - h * self.seg_rows, 0))

    def load(self):
        m = self.m
        for k in range(self.width // LANES):
            lanes = slice(k * LANES, (k + 1) * LANES)
            m.layout[k, 0 : self.number, 0:PIECES, :] = m.pieces[:, :, lanes].astype(F32)
            lines = m.layout.at[k].reshape(self.total * 8, LANES)
            for h in range(self.segs):
                count = self.pieces_of(h)
                base = h * self.rows
                for p in range(PIECES):
                    m.unit[p, base : base + count, lanes] = lines[
                        pl.ds(h * self.seg_rows * 8 + p, count, stride=8), :
                    ]
                    if count < self.rows:
                        m.unit[p, base + count : base + self.rows, lanes] = jnp.zeros(
                            (self.rows - count, LANES), F32
                        )

    def norm_one(self):
        m, width = self.m, self.width
        small = flat(m.w_qkv, 3 * width, 3 * width + LANES).astype(F32).T
        m.small[...] = small[:8]
        start = m.unit[0]
        for g in range(m.n_groups):
            start = start + jnp.where(m.groups[...] == g, small[2 + g : 3 + g, :], 0.0)
        m.unit[0] = start
        m.first[...] = start

        def one(p, carry):
            value = m.unit[p]
            centered = value - jnp.mean(value, axis=1, keepdims=True)
            inv = lax.rsqrt(jnp.mean(centered * centered, axis=1, keepdims=True) + epsilon)
            unit = centered * inv
            m.unit[p] = unit
            m.inv_one[p] = jnp.broadcast_to(inv, (self.total, LANES))
            m.normed[p] = (unit * m.small[0:1, :]).astype(BF16)
            return carry

        lax.fori_loop(0, PIECES, one, 0)

    def project_qkv(self):
        m, width = self.m, self.width
        step = 2 * LANES
        m.query[...] = jnp.dot(
            m.normed[0], flat(m.w_qkv, 0, width), preferred_element_type=F32
        ).astype(BF16)

        def one(j, carry):
            span = pl.ds(pl.multiple_of(j * step, step), step)
            source = pl.ds(pl.multiple_of(width + j * step, step), step)
            weight = m.w_qkv[:, :, :, :, :, source].reshape(width, step)
            m.key_value[:, :, span] = (
                jnp.dot(
                    m.normed[...].reshape(PIECES * self.total, width),
                    weight,
                    preferred_element_type=F32,
                )
                .astype(BF16)
                .reshape(PIECES, self.total, step)
            )
            return carry

        lax.fori_loop(0, 2 * width // step, one, 0)

    def attend(self):
        m, width = self.m, self.width
        ones = head_ones()

        def score(p, carry):
            product = m.query[...].astype(F32) * m.key_value[p, :, :width].astype(F32)
            m.prob[p] = head_sum(product, ones) * (HEAD**-0.5)
            return carry

        lax.fori_loop(0, PIECES, score, 0)

        def soft(i, carry):
            span = pl.ds(pl.multiple_of(i * 16, 16), 16)
            length = m.lengths[span, :]
            scores = [
                jnp.where(p < length, m.prob[p, span, :], -1e30) for p in range(PIECES)
            ]
            highest = functools.reduce(jnp.maximum, scores)
            raised = [jnp.exp(s - highest) for s in scores]
            inv = 1.0 / functools.reduce(jnp.add, raised)
            total = jnp.zeros((16, width), F32)
            for p in range(PIECES):
                prob = raised[p] * inv
                m.prob[p, span, :] = prob
                total = total + prob.astype(BF16).astype(F32) * m.key_value[
                    p, span, width:
                ].astype(F32)
            m.attended[span, :] = total.astype(BF16)
            return carry

        lax.fori_loop(0, self.total // 16, soft, 0)

    def norm_two(self):
        m, width = self.m, self.width
        hidden = m.first[...] + jnp.dot(
            m.attended[...], flat(m.w_out), preferred_element_type=F32
        )
        m.hidden[...] = hidden
        centered = hidden - jnp.mean(hidden, axis=1, keepdims=True)
        inv = lax.rsqrt(jnp.mean(centered * centered, axis=1, keepdims=True) + epsilon)
        unit = centered * inv
        m.unit_two[...] = unit
        m.inv_two[...] = jnp.broadcast_to(inv, (self.total, LANES))
        m.normed_two[...] = (unit * m.small[1:2, :]).astype(BF16)

    def up(self):
        m, step = self.m, 2 * LANES

        def one(j, carry):
            span = pl.ds(pl.multiple_of(j * step, step), step)
            weight = m.w_up[:, :, :, :, :, span].reshape(self.width, step)
            upward = jnp.dot(m.normed_two[...], weight, preferred_element_type=F32)
            normal = 0.5 * (1.0 + lax.erf(upward * (0.5**0.5)))
            m.activated[:, span] = (upward * normal).astype(BF16)
            m.slope[:, span] = normal + upward * (
                jnp.exp(-0.5 * upward * upward) * 0.3989422804014327
            )
            return carry

        lax.fori_loop(0, m.activated.shape[1] // step, one, 0)

    def down(self):
        m = self.m
        m.output[...] = (
            m.hidden[...]
            + jnp.dot(m.activated[...], flat(m.w_down), preferred_element_type=F32)
        ).astype(BF16)

    def table(self):
        m, segs, rows = self.m, self.segs, self.rows

        def one(g, carry):
            span = pl.ds(pl.multiple_of(g * LANES, LANES), LANES)
            weight = m.w_proj[:, :, :, :, :, span].reshape(self.width, LANES)
            value = jnp.dot(m.output[...], weight, preferred_element_type=F32)
            parts = [value[h * rows : (h + 1) * rows] for h in range(segs)]
            for j, part in enumerate(spread_segments(parts, self.feats, segs)):
                m.sent[g * segs + j] = part.astype(BF16)
            return carry

        lax.fori_loop(0, m.w_proj.shape[-1] // LANES, one, 0)


    def table_back(self):
        m, segs, rows = self.m, self.segs, self.rows

        def one(g, carry):
            span = pl.ds(pl.multiple_of(g * LANES, LANES), LANES)
            parts = [m.came[g * segs + j].astype(F32) for j in range(segs)]
            for h, part in enumerate(spread_segments(parts, self.feats, segs)):
                m.grad_table[h * rows : (h + 1) * rows, span] = part.astype(BF16)
            return carry

        lax.fori_loop(0, m.grad_table.shape[1] // LANES, one, 0)

    def put(self, ref, value):
        ref[...] = value.astype(BF16).reshape(ref.shape)

    def proj_back(self):
        m = self.m
        self.put(m.d_proj, contract(m.output[...], m.grad_table[...], 0, 0))
        grad_output = contract(m.grad_table[...], flat(m.w_proj), 1, 1)
        m.grad_output[...] = grad_output
        m.grad_branch[...] = grad_output.astype(BF16)

    def down_back(self):
        m = self.m
        self.put(m.d_down, contract(m.activated[...], m.grad_branch[...], 0, 0))
        grad_act = contract(m.grad_branch[...], flat(m.w_down), 1, 1)
        m.grad_up[...] = (grad_act * m.slope[...]).astype(BF16)

    def up_back(self):
        m = self.m
        self.put(m.d_up, contract(m.normed_two[...], m.grad_up[...], 0, 0))
        grad = contract(m.grad_up[...], flat(m.w_up), 1, 1)
        m.d_small[...] = jnp.zeros_like(m.d_small)
        unit = m.unit_two[...]
        m.d_small[1:2, :] = jnp.sum(grad * unit, axis=0, keepdims=True)
        grad = grad * m.small[1:2, :]
        first = jnp.mean(grad, axis=1, keepdims=True)
        second = jnp.mean(grad * unit, axis=1, keepdims=True)
        hidden = m.grad_output[...] + m.inv_two[:, 0:1] * (grad - first - unit * second)
        m.hidden[...] = hidden
        m.grad_branch[...] = hidden.astype(BF16)

    def out_back(self):
        m = self.m
        self.put(m.d_out, contract(m.attended[...], m.grad_branch[...], 0, 0))
        m.grad_att[...] = contract(m.grad_branch[...], flat(m.w_out), 1, 1).astype(BF16)

    def attend_back(self):
        m, width = self.m, self.width
        ones = head_ones()
        scale = HEAD**-0.5

        def score(p, carry):
            product = m.grad_att[...].astype(F32) * m.key_value[p, :, width:].astype(F32)
            m.grad_prob[p] = head_sum(product, ones)
            return carry

        lax.fori_loop(0, PIECES, score, 0)

        def soft(i, carry):
            span = pl.ds(pl.multiple_of(i * 16, 16), 16)
            inner = jnp.zeros((16, width), F32)
            for p in range(PIECES):
                inner = inner + m.prob[p, span, :] * m.grad_prob[p, span, :]
            query = m.query[span, :].astype(F32)
            grad_att = m.grad_att[span, :].astype(F32)
            grad_query = jnp.zeros((16, width), F32)
            for p in range(PIECES):
                prob = m.prob[p, span, :]
                low = prob.astype(BF16).astype(F32)
                grad = (prob * (m.grad_prob[p, span, :] - inner)).astype(BF16).astype(F32)
                grad_query = grad_query + grad * m.key_value[p, span, :width].astype(F32)
                m.grad_kv[p, span, :width] = (grad * query * scale).astype(BF16)
                m.grad_kv[p, span, width:] = (low * grad_att).astype(BF16)
            m.grad_query[span, :] = (grad_query * scale).astype(BF16)
            return carry

        lax.fori_loop(0, self.total // 16, soft, 0)

    def qkv_back(self):
        m, width = self.m, self.width
        lead = m.d_qkv.shape[:-1]
        step = 2 * LANES
        m.d_qkv[:, :, :, :, :, :width] = (
            contract(m.normed[0], m.grad_query[...], 0, 0).astype(BF16).reshape(lead + (width,))
        )

        def one(j, carry):
            target = pl.ds(pl.multiple_of(width + j * step, step), step)
            span = pl.ds(pl.multiple_of(j * step, step), step)
            grad = m.grad_kv[:, :, span].reshape(PIECES * self.total, step)
            m.d_qkv[:, :, :, :, :, target] = (
                contract(m.normed[...].reshape(PIECES * self.total, width), grad, 0, 0)
                .astype(BF16)
                .reshape(lead + (step,))
            )
            return carry

        lax.fori_loop(0, 2 * width // step, one, 0)

    def normed_back(self):
        m, width = self.m, self.width
        m.grad_prob[...] = contract(
            m.grad_kv[...].reshape(PIECES * self.total, 2 * width),
            flat(m.w_qkv, width, 3 * width),
            1,
            1,
        ).reshape(PIECES, self.total, width)
        m.grad_prob[0] += contract(m.grad_query[...], flat(m.w_qkv, 0, width), 1, 1)

    def norm_back(self):
        m, width = self.m, self.width
        gain = m.small[0:1, :]

        def back(p):
            grad = m.grad_prob[p]
            unit = m.unit[p]
            m.d_small[0:1, :] += jnp.sum(grad * unit, axis=0, keepdims=True)
            grad = grad * gain
            first = jnp.mean(grad, axis=1, keepdims=True)
            second = jnp.mean(grad * unit, axis=1, keepdims=True)
            grad = m.inv_one[p][:, 0:1] * (grad - first - unit * second)
            if p == 0:
                grad = grad + m.hidden[...]
                for g in range(m.n_groups):
                    m.d_small[2 + g : 3 + g, :] = jnp.sum(
                        jnp.where(m.groups[...] == g, grad, 0.0), axis=0, keepdims=True
                    )
            for k in range(width // LANES):
                lines = m.layout.at[k].reshape(self.total * 8, LANES)
                for h in range(self.segs):
                    count = self.pieces_of(h)
                    lines[pl.ds(h * self.seg_rows * 8 + p, count, stride=8), :] = grad[
                        h * self.rows : h * self.rows + count, k * LANES : (k + 1) * LANES
                    ]

        for p in range(PIECES):
            back(p)
        for k in range(width // LANES):
            m.grad_pieces[:, :, k * LANES : (k + 1) * LANES] = m.layout[
                k, 0 : self.number, 0:PIECES, :
            ].astype(BF16)
        lead = m.d_qkv.shape[:-1]
        small = jnp.concatenate(
            [m.d_small[...], jnp.zeros((LANES - 8, width), F32)], axis=0
        ).T
        m.d_qkv[:, :, :, :, :, 3 * width :] = small.astype(BF16).reshape(lead + (LANES,))


def block_scratch(n, rows, total, width, hidden, out_width):
    return dict(
        layout=((width // LANES, total, 8, LANES), F32),
        unit=((PIECES, total, width), F32),
        inv_one=((PIECES, total, LANES), F32),
        first=((total, width), F32),
        small=((8, width), F32),
        normed=((PIECES, total, width), BF16),
        query=((total, width), BF16),
        key_value=((PIECES, total, 2 * width), BF16),
        prob=((PIECES, total, width), F32),
        attended=((total, width), BF16),
        hidden=((total, width), F32),
        unit_two=((total, width), F32),
        inv_two=((total, LANES), F32),
        normed_two=((total, width), BF16),
        activated=((total, hidden), BF16),
        slope=((total, hidden), F32),
        output=((total, width), BF16),
        grad_table=((total, out_width), BF16),
        grad_output=((total, width), F32),
        grad_branch=((total, width), BF16),
        grad_up=((total, hidden), BF16),
        d_small=((8, width), F32),
        grad_att=((total, width), BF16),
        grad_prob=((PIECES, total, width), F32),
        grad_kv=((PIECES, total, 2 * width), BF16),
        grad_query=((total, width), BF16),
    )


def middle_kernel(names, consts, *refs):
    m = types.SimpleNamespace(**dict(zip(names, refs)), n_groups=consts[0])
    block = Block(m, *consts[1:])
    block.load()
    block.norm_one()
    block.project_qkv()
    block.attend()
    block.norm_two()
    block.up()
    block.down()
    block.table()
    block.table_back()
    block.proj_back()
    block.down_back()
    block.up_back()
    block.out_back()
    block.attend_back()
    block.qkv_back()
    block.normed_back()
    block.norm_back()


def full(shape, dtype):
    return jax.ShapeDtypeStruct(shape, dtype)


def body(
    mesh_shape,
    pieces,
    lengths,
    entry_group,
    group_table,
    ln1_gain,
    w_qkv,
    w_out,
    ln2_gain,
    w_up,
    w_down,
    w_proj,
    text_ids,
    text_mask,
    grad_embed,
):
    n_entries = mesh_shape["entries"]
    n = n_entries * mesh_shape["feat"]
    n_z = n_entries // 4
    number, width = pieces.shape[0], pieces.shape[2]
    shard = ln1_gain.shape[0]
    groups_n = group_table.shape[0]
    feats = grad_embed.shape[0]
    text_len = text_ids.shape[0]
    segs = LANES // feats
    seg_rows = -(-number // segs)
    rows = -(-seg_rows // 16) * 16
    half = n // 2

    small = jnp.concatenate([ln1_gain[:, None], ln2_gain[:, None], group_table.T], axis=1)
    w_qkv_more = jnp.concatenate(
        [w_qkv, jnp.pad(small, ((0, 0), (0, LANES - small.shape[1])))], axis=1
    )
    total = segs * rows

    def column(values):
        values = jnp.pad(values, (0, segs * seg_rows - number)).reshape(segs, seg_rows)
        return jnp.pad(values, ((0, 0), (0, rows - seg_rows))).reshape(total, 1)

    source = text_ids // number
    within = text_ids - source * number
    segment = within // seg_rows
    row_key = (source % half) * rows + within - segment * seg_rows
    seg_key = jnp.where(text_mask != 0, (source // half) * segs + segment, -1)
    row_key, seg_key = row_key[None, :], seg_key[None, :]

    vmem = pl.BlockSpec(memory_space=VMEM)
    shards = (w_qkv_more, w_out, w_up, w_down, w_proj)
    lead = (n_z, 2, 2, 2)
    gathered = pl.pallas_call(
        functools.partial(gather_kernel, n_entries),
        out_shape=tuple(full(lead + s.shape, BF16) for s in shards)
        + (full((n, rows, LANES), BF16),),
        in_specs=[vmem] * 8,
        out_specs=(vmem,) * 6,
        scratch_shapes=[
            VMEM((half * rows, 2 * LANES), F32),
            VMEM((n, rows, LANES), BF16),
            pltpu.SemaphoreType.DMA((N_WEIGHTS, n_z + 6)),
            pltpu.SemaphoreType.DMA((N_WEIGHTS, n_z + 6)),
            pltpu.SemaphoreType.DMA((n,)),
            pltpu.SemaphoreType.DMA((n,)),
        ],
        compiler_params=pltpu.CompilerParams(
            collective_id=0, has_side_effects=True, vmem_limit_bytes=56 * 2**20
        ),
    )(*shards, row_key, seg_key, grad_embed)
    *wholes, came = gathered
    ins = dict(
        pieces=pieces,
        lengths=column(lengths),
        groups=column(entry_group),
        w_qkv=wholes[0],
        w_out=wholes[1],
        w_up=wholes[2],
        w_down=wholes[3],
        w_proj=wholes[4],
        came=came,
    )
    outs = dict(
        d_qkv=full(lead + w_qkv_more.shape, BF16),
        d_out=full(lead + w_out.shape, BF16),
        d_up=full(lead + w_up.shape, BF16),
        d_down=full(lead + w_down.shape, BF16),
        d_proj=full(lead + w_proj.shape, BF16),
        sent=full((n, rows, LANES), BF16),
        grad_pieces=full(pieces.shape, BF16),
    )
    scratch = block_scratch(n, rows, total, width, w_up.shape[1], w_proj.shape[1])
    *grads, blocks, grad_pieces = pl.pallas_call(
        functools.partial(
            middle_kernel,
            tuple(ins) + tuple(outs) + tuple(scratch),
            (groups_n, segs, seg_rows, rows, feats),
        ),
        out_shape=tuple(outs.values()),
        in_specs=[vmem] * len(ins),
        out_specs=(vmem,) * len(outs),
        scratch_shapes=[VMEM(*item) for item in scratch.values()],
        compiler_params=pltpu.CompilerParams(vmem_limit_bytes=60 * 2**20),
    )(*ins.values())
    held = []
    for s in shards:
        held += [
            VMEM((n_z, 2, 2) + s.shape, BF16),
            VMEM((2, n_z) + s.shape, BF16),
            VMEM((n_z,) + s.shape, BF16),
            VMEM((n_z - 1,) + s.shape, BF16),
        ]
    summed = pl.pallas_call(
        functools.partial(reduce_kernel, n_entries),
        out_shape=tuple(full(s.shape, F32) for s in shards) + (full((feats, text_len), BF16),),
        in_specs=[vmem] * 8,
        out_specs=(vmem,) * 6,
        scratch_shapes=held
        + [
            VMEM((n, rows, LANES), BF16),
            VMEM((2 * LANES, half * rows), BF16),
            pltpu.SemaphoreType.DMA((N_WEIGHTS, n_z + 4)),
            pltpu.SemaphoreType.DMA((N_WEIGHTS, n_z + 4)),
            pltpu.SemaphoreType.DMA((n,)),
            pltpu.SemaphoreType.DMA((n,)),
        ],
        compiler_params=pltpu.CompilerParams(
            collective_id=1, has_side_effects=True, vmem_limit_bytes=56 * 2**20
        ),
    )(*grads, blocks, row_key, seg_key)
    s_qkv, s_out, s_up, s_down, s_proj, embeddings = summed
    s_small = s_qkv[:, 3 * width :]
    return (
        embeddings,
        grad_pieces,
        s_small[:, 2 : 2 + groups_n].T,
        s_small[:, 0],
        s_qkv[:, : 3 * width],
        s_out,
        s_small[:, 1],
        s_up,
        s_down,
        s_proj,
    )


def solution(mesh):
    both = P(AXES)
    rows = P(AXES, None)
    return jax.shard_map(
        functools.partial(body, dict(mesh.shape)),
        mesh=mesh,
        in_specs=(
            P(AXES, None, None),
            both,
            both,
            P(None, AXES),
            both,
            rows,
            rows,
            both,
            rows,
            rows,
            rows,
            P(),
            P(),
            rows,
        ),
        out_specs=(
            rows,
            P(AXES, None, None),
            P(None, AXES),
            both,
            rows,
            rows,
            both,
            rows,
            rows,
            rows,
        ),
        check_vma=False,
    )
```

```python
import functools
import types

import jax
import jax.numpy as jnp
from jax import lax
from jax.experimental import pallas as pl
from jax.experimental.pallas import tpu as pltpu
from jax.sharding import PartitionSpec as P

HEADS = 8
HEAD = 64
PIECES = 7
LANES = 128
TBLOCK = 512
AXES = ("entries", "feat")
MESH = pl.DeviceIdType.MESH
VMEM = pltpu.VMEM
BF16 = jnp.bfloat16
F32 = jnp.float32

epsilon = 1e-05


def contract(left_side, right_side, left_dim, right_dim):
    return lax.dot_general(
        left_side,
        right_side,
        (((left_dim,), (right_dim,)), ((), ())),
        preferred_element_type=jnp.float32,
    )


class Place:
    def __init__(self, n_entries):
        entry = lax.axis_index("entries")
        self.n_z = n_entries // 4
        self.n = n_entries * 2
        self.y = lax.axis_index("feat")
        self.c = lax.rem(entry, 2)
        self.x = lax.rem(lax.div(entry, 2), 2)
        self.z = lax.div(entry, 4)
        self.line = entry * 2 + self.y
        first = self.c == 0
        self.x1 = jnp.where(first, 1 - self.x, self.x)
        self.y1 = jnp.where(first, self.y, 1 - self.y)
        self.x2 = jnp.where(first, self.x, 1 - self.x)
        self.y2 = jnp.where(first, 1 - self.y, self.y)

    def at(self, z, x, c, y):
        return ((z * 2 + x) * 2 + c, y)

    def along_z(self, step):
        return lax.rem(self.z + step, self.n_z)


def meet(place):
    p = place
    barrier = pltpu.get_barrier_semaphore()
    peers = [p.at(p.along_z(k), p.x, p.c, p.y) for k in range(1, p.n_z)]
    peers += [
        p.at(p.z, p.x, 1 - p.c, p.y),
        p.at(p.z, p.x1, p.c, p.y1),
        p.at(p.z, p.x2, p.c, p.y2),
    ]
    for peer in peers:
        pl.semaphore_signal(barrier, inc=1, device_id=peer, device_id_type=MESH)
    pl.semaphore_wait(barrier, len(peers))


def remote(src, dst, send, recv, to):
    return pltpu.make_async_remote_copy(
        src_ref=src, dst_ref=dst, send_sem=send, recv_sem=recv, device_id=to, device_id_type=MESH
    )


class Gather:
    def __init__(self, place, whole, send, recv):
        p = self.place = place
        nz = p.n_z
        self.nz = nz
        mine = whole.at[p.z, p.x, p.c, p.y]
        self.along = [
            remote(mine, mine, send.at[k - 1], recv.at[k - 1], p.at(p.along_z(k), p.x, p.c, p.y))
            for k in range(1, nz)
        ]
        col = [
            whole.at[:, p.x, p.c, p.y],
            whole.at[:, p.x1, p.c, p.y1],
            whole.at[:, p.x2, p.c, p.y2],
            whole.at[:, 1 - p.x, p.c, 1 - p.y],
        ]
        to_one = p.at(p.z, p.x1, p.c, p.y1)
        to_two = p.at(p.z, p.x2, p.c, p.y2)
        to_core = p.at(p.z, p.x, 1 - p.c, p.y)
        s = nz - 1
        self.one = remote(col[0], col[0], send.at[s], recv.at[s], to_one)
        self.two = remote(col[0], col[0], send.at[s + 1], recv.at[s + 1], to_two)
        self.three = remote(col[1], col[1], send.at[s + 2], recv.at[s + 2], to_two)
        self.core = [
            remote(col[k], col[k], send.at[s + 3 + k], recv.at[s + 3 + k], to_core)
            for k in range(4)
        ]

    def z_start(self):
        for copy in self.along:
            copy.start()

    def z_wait(self):
        for copy in self.along:
            copy.wait_recv()
        self.one.start()
        self.two.start()
        self.core[0].start()

    def one_wait(self):
        self.one.wait_recv()
        self.three.start()
        self.core[1].start()

    def two_wait(self):
        self.two.wait_recv()
        self.core[2].start()

    def three_wait(self):
        self.three.wait_recv()
        self.core[3].start()

    def core_wait(self):
        for copy in self.core:
            copy.wait_recv()

    def finish(self):
        for copy in self.along + [self.one, self.two, self.three] + self.core:
            copy.wait_send()


class Reduce:
    def __init__(self, place, parts, held_core, held_one, held_two, held_z, send, recv):
        p = self.place = place
        nz = p.n_z
        self.parts, self.held_core = parts, held_core
        self.held_one, self.held_two, self.held_z = held_one, held_two, held_z
        self.cols = [(p.x, p.y), (p.x1, p.y1), (p.x2, p.y2), (1 - p.x, 1 - p.y)]
        to_one = p.at(p.z, p.x1, p.c, p.y1)
        to_two = p.at(p.z, p.x2, p.c, p.y2)
        to_core = p.at(p.z, p.x, 1 - p.c, p.y)

        def col(k):
            return parts.at[:, self.cols[k][0], p.c, self.cols[k][1]]

        self.core = remote(parts.at[:, :, 1 - p.c], held_core, send.at[0], recv.at[0], to_core)
        self.one = [
            remote(col(1), held_one.at[0], send.at[1], recv.at[1], to_one),
            remote(col(3), held_one.at[1], send.at[2], recv.at[2], to_one),
        ]
        self.two = remote(col(2), held_two, send.at[3], recv.at[3], to_two)
        self.along = [
            remote(
                parts.at[p.along_z(k), p.x, p.c, p.y],
                held_z.at[k - 1],
                send.at[3 + k],
                recv.at[3 + k],
                p.at(p.along_z(k), p.x, p.c, p.y),
            )
            for k in range(1, nz)
        ]

    def add(self, k, other):
        p, (x, y) = self.place, self.cols[k]
        self.parts[:, x, p.c, y] = (
            self.parts[:, x, p.c, y].astype(F32) + other.astype(F32)
        ).astype(BF16)

    def core_start(self):
        self.core.start()

    def core_wait(self):
        self.core.wait_recv()
        for k in (3, 1, 2, 0):
            x, y = self.cols[k]
            self.add(k, self.held_core[:, x, y])
            if k == 3:
                self.one[1].start()
            if k == 1:
                self.one[0].start()

    def one_wait(self):
        self.one[1].wait_recv()
        self.add(2, self.held_one[1])
        self.two.start()
        self.one[0].wait_recv()
        self.add(0, self.held_one[0])

    def two_wait(self):
        self.two.wait_recv()
        self.add(0, self.held_two[...])
        for copy in self.along:
            copy.start()

    def z_wait(self, out):
        p = self.place
        total = self.parts[p.z, p.x, p.c, p.y].astype(F32)
        for k, copy in enumerate(self.along):
            copy.wait_recv()
            total = total + self.held_z[k].astype(F32)
        out[...] = total

    def finish(self):
        for copy in [self.core] + self.one + [self.two] + self.along:
            copy.wait_send()


def exchange(place, src, dst, send, recv):
    dst[place.line] = src[place.line]

    def begin(step, carry):
        other = lax.rem(place.line + step, place.n)
        remote(
            src.at[other],
            dst.at[place.line],
            send.at[step],
            recv.at[step],
            (lax.div(other, 2), lax.rem(other, 2)),
        ).start()
        return carry

    lax.fori_loop(1, place.n, begin, 0)


def exchange_wait(place, src, dst, send, recv, sends):
    def end(step, carry):
        other = lax.rem(place.line + step, place.n)
        copy = remote(
            src.at[other],
            dst.at[place.line],
            send.at[step],
            recv.at[step],
            (lax.div(other, 2), lax.rem(other, 2)),
        )
        if sends:
            copy.wait_send()
        else:
            copy.wait_recv()
        return carry

    lax.fori_loop(1, place.n, end, 0)


def text_keys(number, seg_rows, rows, segs, half, ids, mask, row_key, seg_key):
    length = ids.shape[0]
    entry = ids[...].reshape(1, length)
    source = ((entry.astype(F32) + 0.5) * (1.0 / number)).astype(jnp.int32)
    within = entry - source * number
    segment = jnp.zeros_like(entry)
    for h in range(1, segs):
        segment = segment + (within >= h * seg_rows).astype(jnp.int32)
    upper = (source >= half).astype(jnp.int32)
    row_key[...] = (source - half * upper) * rows + within - segment * seg_rows
    seg_key[...] = jnp.where(mask[...].reshape(1, length) != 0, upper * segs + segment, -1)


def text_blocks(length):
    whole = length // TBLOCK
    return whole, length - whole * TBLOCK


def one_hot(keys, depth):
    width = keys.shape[1]
    return (lax.broadcasted_iota(jnp.int32, (depth, width), 0) == keys).astype(F32).astype(BF16)


def scatter_block(start, width, row_ref, seg_ref, cot_ref, acc_ref):
    span = pl.ds(start, width)
    depth, side = acc_ref.shape[0], acc_ref.shape[1] // 2
    seg = seg_ref[:, span]
    cot = cot_ref[:, span].astype(F32)
    spread = jnp.concatenate(
        [jnp.where(seg == q, cot, 0.0).astype(BF16) for q in range(side // cot.shape[0])], axis=0
    )
    for k in range(2):
        hot = one_hot(row_ref[:, span] - k * depth, depth)
        acc_ref[:, k * side : (k + 1) * side] += contract(hot, spread, 1, 1)


class Sweep:
    def __init__(self, length, block):
        self.block, self.done = block, 0
        self.whole, self.tail = text_blocks(length)

    def go(self, count=None):
        low = self.done
        high = self.whole if count is None else min(self.whole, low + count)
        self.done = high

        def step(i, carry):
            self.block(pl.multiple_of(i * TBLOCK, TBLOCK), TBLOCK)
            return carry

        if high > low:
            lax.fori_loop(low, high, step, 0)
        if count is None and self.tail:
            self.block(self.whole * TBLOCK, self.tail)


def lookup_block(start, width, row_ref, seg_ref, table_ref, out_ref):
    span = pl.ds(start, width)
    hot = one_hot(row_ref[:, span], table_ref.shape[1])
    seg = seg_ref[:, span]
    wide = jnp.dot(table_ref[...], hot, preferred_element_type=F32)
    feats = out_ref.shape[0]
    found = jnp.zeros((feats, width), F32)
    for q in range(table_ref.shape[0] // feats):
        found = found + jnp.where(seg == q, wide[q * feats : (q + 1) * feats], 0.0)
    out_ref[:, span] = found.astype(BF16)


def cast_pair(value):
    high = value.astype(BF16)
    return high, (value - high.astype(F32)).astype(BF16)


def head_ones():
    head_row = lax.broadcasted_iota(jnp.int32, (4 * HEAD, 4 * HEAD), 0) // HEAD
    head_col = lax.broadcasted_iota(jnp.int32, (4 * HEAD, 4 * HEAD), 1) // HEAD
    return (head_row == head_col).astype(F32).astype(BF16)


def head_sum(value, ones):
    high, low = cast_pair(value)
    step = 4 * HEAD
    return jnp.concatenate(
        [
            jnp.dot(high[:, j : j + step], ones, preferred_element_type=F32)
            + jnp.dot(low[:, j : j + step], ones, preferred_element_type=F32)
            for j in range(0, value.shape[1], step)
        ],
        axis=1,
    )


def flat(ref, low=None, high=None):
    value = ref[...] if low is None else ref[:, :, :, :, :, low:high]
    return value.reshape(-1, value.shape[-1])


def spread_segments(blocks, feats, segs):
    lane = lax.broadcasted_iota(jnp.int32, blocks[0].shape, 1) // feats
    out = []
    for h in range(segs):
        whole = None
        for j in range(segs):
            shift = ((j - h) * feats) % LANES
            moved = blocks[j] if shift == 0 else pltpu.roll(blocks[j], shift, 1)
            whole = moved if whole is None else jnp.where(lane == j, moved, whole)
        out.append(whole)
    return out


class Block:
    def __init__(self, m, segs, seg_rows, rows, feats):
        self.m, self.segs, self.seg_rows, self.rows, self.feats = m, segs, seg_rows, rows, feats
        self.number = m.pieces.shape[1]
        self.width = m.pieces.shape[2]
        self.total = segs * rows

    def pieces_of(self, h):
        return min(self.seg_rows, max(self.number - h * self.seg_rows, 0))

    def column(self, ref):
        line = lax.broadcasted_iota(jnp.int32, (self.total, 1), 0)
        segment, within = line // self.rows, line % self.rows
        entry = jnp.where(within < self.seg_rows, segment * self.seg_rows + within, -1)
        values = ref[...].reshape(1, self.number)
        lane = lax.broadcasted_iota(jnp.int32, (self.total, self.number), 1)
        return jnp.sum(jnp.where(lane == entry, values, 0), axis=1, keepdims=True)

    def load(self):
        m = self.m
        m.length_col[...] = self.column(m.lengths)
        m.group_col[...] = self.column(m.groups)
        for p in range(PIECES):
            value = m.pieces[p].astype(F32)
            for h in range(self.segs):
                low, base, count = h * self.seg_rows, h * self.rows, self.pieces_of(h)
                m.unit[p, base : base + count, :] = value[low : low + count]
                m.unit[p, base + count : base + self.rows, :] = jnp.zeros(
                    (self.rows - count, self.width), F32
                )

    def norm_one(self):
        m, width = self.m, self.width
        small = flat(m.w_qkv, 3 * width, 3 * width + LANES).astype(F32).T
        m.small[...] = small[:8]
        start = m.unit[0]
        for g in range(m.n_groups):
            start = start + jnp.where(m.group_col[...] == g, small[2 + g : 3 + g, :], 0.0)
        m.unit[0] = start
        m.hidden[...] = start

        def one(p, carry):
            value = m.unit[p]
            centered = value - jnp.mean(value, axis=1, keepdims=True)
            inv = lax.rsqrt(jnp.mean(centered * centered, axis=1, keepdims=True) + epsilon)
            unit = centered * inv
            m.unit[p] = unit
            m.inv_one[p] = jnp.broadcast_to(inv, (self.total, LANES))
            m.normed[p] = (unit * m.small[0:1, :]).astype(BF16)
            return carry

        lax.fori_loop(0, PIECES, one, 0)

    def project_qkv(self):
        m, width = self.m, self.width
        step = 2 * LANES
        m.query[...] = jnp.dot(
            m.normed[0], flat(m.w_qkv, 0, width), preferred_element_type=F32
        ).astype(BF16)

        def one(j, carry):
            span = pl.ds(pl.multiple_of(j * step, step), step)
            source = pl.ds(pl.multiple_of(width + j * step, step), step)
            weight = m.w_qkv[:, :, :, :, :, source].reshape(width, step)
            m.key_value[:, :, span] = (
                jnp.dot(
                    m.normed[...].reshape(PIECES * self.total, width),
                    weight,
                    preferred_element_type=F32,
                )
                .astype(BF16)
                .reshape(PIECES, self.total, step)
            )
            return carry

        lax.fori_loop(0, 2 * width // step, one, 0)

    def attend(self):
        m, width = self.m, self.width
        ones = head_ones()

        def score(p, carry):
            product = m.query[...].astype(F32) * m.key_value[p, :, :width].astype(F32)
            m.prob[p] = head_sum(product, ones) * (HEAD**-0.5)
            return carry

        lax.fori_loop(0, PIECES, score, 0)

        def soft(i, carry):
            span = pl.ds(pl.multiple_of(i * 16, 16), 16)
            length = m.length_col[span, :]
            scores = [
                jnp.where(p < length, m.prob[p, span, :], -1e30) for p in range(PIECES)
            ]
            highest = functools.reduce(jnp.maximum, scores)
            raised = [jnp.exp(s - highest) for s in scores]
            inv = 1.0 / functools.reduce(jnp.add, raised)
            total = jnp.zeros((16, width), F32)
            for p in range(PIECES):
                prob = raised[p] * inv
                m.prob[p, span, :] = prob
                total = total + prob.astype(BF16).astype(F32) * m.key_value[
                    p, span, width:
                ].astype(F32)
            m.attended[span, :] = total.astype(BF16)
            return carry

        lax.fori_loop(0, self.total // 16, soft, 0)

    def norm_two(self):
        m, width = self.m, self.width
        hidden = m.hidden[...] + jnp.dot(
            m.attended[...], flat(m.w_out), preferred_element_type=F32
        )
        m.hidden[...] = hidden
        centered = hidden - jnp.mean(hidden, axis=1, keepdims=True)
        inv = lax.rsqrt(jnp.mean(centered * centered, axis=1, keepdims=True) + epsilon)
        unit = centered * inv
        m.unit_two[...] = unit
        m.inv_two[...] = jnp.broadcast_to(inv, (self.total, LANES))
        m.normed_two[...] = (unit * m.small[1:2, :]).astype(BF16)

    def up(self):
        m, step = self.m, 2 * LANES

        def one(j, carry):
            span = pl.ds(pl.multiple_of(j * step, step), step)
            weight = m.w_up[:, :, :, :, :, span].reshape(self.width, step)
            upward = jnp.dot(m.normed_two[...], weight, preferred_element_type=F32)
            normal = 0.5 * (1.0 + lax.erf(upward * (0.5**0.5)))
            m.activated[:, span] = (upward * normal).astype(BF16)
            m.slope[:, span] = normal + upward * (
                jnp.exp(-0.5 * upward * upward) * 0.3989422804014327
            )
            return carry

        lax.fori_loop(0, m.activated.shape[1] // step, one, 0)

    def down(self):
        m = self.m
        m.output[...] = (
            m.hidden[...]
            + jnp.dot(m.activated[...], flat(m.w_down), preferred_element_type=F32)
        ).astype(BF16)

    def table(self):
        m, segs, rows = self.m, self.segs, self.rows

        def one(g, carry):
            span = pl.ds(pl.multiple_of(g * LANES, LANES), LANES)
            weight = m.w_proj[:, :, :, :, :, span].reshape(self.width, LANES)
            value = jnp.dot(m.output[...], weight, preferred_element_type=F32)
            parts = [value[h * rows : (h + 1) * rows] for h in range(segs)]
            for j, part in enumerate(spread_segments(parts, self.feats, segs)):
                m.came_grad[g * segs + j] = part.astype(BF16)
            return carry

        lax.fori_loop(0, m.w_proj.shape[-1] // LANES, one, 0)


    def table_back(self):
        m, segs, rows = self.m, self.segs, self.rows

        def one(g, carry):
            span = pl.ds(pl.multiple_of(g * LANES, LANES), LANES)
            parts = [m.came_grad[g * segs + j].astype(F32) for j in range(segs)]
            for h, part in enumerate(spread_segments(parts, self.feats, segs)):
                m.grad_table[h * rows : (h + 1) * rows, span] = part.astype(BF16)
            return carry

        lax.fori_loop(0, m.grad_table.shape[1] // LANES, one, 0)

    def put(self, ref, value):
        ref[...] = value.astype(BF16).reshape(ref.shape)

    def proj_grad(self):
        m = self.m
        self.put(m.d_proj, contract(m.output[...], m.grad_table[...], 0, 0))

    def proj_back(self):
        m = self.m
        grad_output = contract(m.grad_table[...], flat(m.w_proj), 1, 1)
        m.grad_output[...] = grad_output
        m.grad_branch[...] = grad_output.astype(BF16)

    def down_grad(self):
        m = self.m
        self.put(m.d_down, contract(m.activated[...], m.grad_branch[...], 0, 0))

    def down_back(self):
        m = self.m
        grad_act = contract(m.grad_branch[...], flat(m.w_down), 1, 1)
        m.activated[...] = (grad_act * m.slope[...]).astype(BF16)

    def up_grad(self):
        m = self.m
        self.put(m.d_up, contract(m.normed_two[...], m.activated[...], 0, 0))

    def up_back(self):
        m = self.m
        grad = contract(m.activated[...], flat(m.w_up), 1, 1)
        m.d_small[...] = jnp.zeros_like(m.d_small)
        unit = m.unit_two[...]
        m.d_small[1:2, :] = jnp.sum(grad * unit, axis=0, keepdims=True)
        grad = grad * m.small[1:2, :]
        first = jnp.mean(grad, axis=1, keepdims=True)
        second = jnp.mean(grad * unit, axis=1, keepdims=True)
        hidden = m.grad_output[...] + m.inv_two[:, 0:1] * (grad - first - unit * second)
        m.hidden[...] = hidden
        m.grad_branch[...] = hidden.astype(BF16)

    def out_back(self):
        m = self.m
        self.put(m.d_out, contract(m.attended[...], m.grad_branch[...], 0, 0))
        m.attended[...] = contract(m.grad_branch[...], flat(m.w_out), 1, 1).astype(BF16)

    def attend_back(self):
        m, width = self.m, self.width
        ones = head_ones()
        scale = HEAD**-0.5

        def score(p, carry):
            product = m.attended[...].astype(F32) * m.key_value[p, :, width:].astype(F32)
            m.grad_prob[p] = head_sum(product, ones)
            return carry

        lax.fori_loop(0, PIECES, score, 0)

        def soft(i, carry):
            span = pl.ds(pl.multiple_of(i * 16, 16), 16)
            inner = jnp.zeros((16, width), F32)
            for p in range(PIECES):
                inner = inner + m.prob[p, span, :] * m.grad_prob[p, span, :]
            query = m.query[span, :].astype(F32)
            grad_att = m.attended[span, :].astype(F32)
            grad_query = jnp.zeros((16, width), F32)
            for p in range(PIECES):
                prob = m.prob[p, span, :]
                low = prob.astype(BF16).astype(F32)
                grad = (prob * (m.grad_prob[p, span, :] - inner)).astype(BF16).astype(F32)
                grad_query = grad_query + grad * m.key_value[p, span, :width].astype(F32)
                m.key_value[p, span, :width] = (grad * query * scale).astype(BF16)
                m.key_value[p, span, width:] = (low * grad_att).astype(BF16)
            m.query[span, :] = (grad_query * scale).astype(BF16)
            return carry

        lax.fori_loop(0, self.total // 16, soft, 0)

    def qkv_back(self):
        m, width = self.m, self.width
        lead = m.d_qkv.shape[:-1]
        step = 2 * LANES
        m.d_qkv[:, :, :, :, :, :width] = (
            contract(m.normed[0], m.query[...], 0, 0).astype(BF16).reshape(lead + (width,))
        )

        def one(j, carry):
            target = pl.ds(pl.multiple_of(width + j * step, step), step)
            span = pl.ds(pl.multiple_of(j * step, step), step)
            grad = m.key_value[:, :, span].reshape(PIECES * self.total, step)
            m.d_qkv[:, :, :, :, :, target] = (
                contract(m.normed[...].reshape(PIECES * self.total, width), grad, 0, 0)
                .astype(BF16)
                .reshape(lead + (step,))
            )
            return carry

        lax.fori_loop(0, 2 * width // step, one, 0)

    def normed_back(self):
        m, width = self.m, self.width
        m.grad_prob[...] = contract(
            m.key_value[...].reshape(PIECES * self.total, 2 * width),
            flat(m.w_qkv, width, 3 * width),
            1,
            1,
        ).reshape(PIECES, self.total, width)
        m.grad_prob[0] += contract(m.query[...], flat(m.w_qkv, 0, width), 1, 1)

    def norm_back(self):
        m, width = self.m, self.width
        gain = m.small[0:1, :]

        def back(p):
            grad = m.grad_prob[p]
            unit = m.unit[p]
            m.d_small[0:1, :] += jnp.sum(grad * unit, axis=0, keepdims=True)
            grad = grad * gain
            first = jnp.mean(grad, axis=1, keepdims=True)
            second = jnp.mean(grad * unit, axis=1, keepdims=True)
            grad = m.inv_one[p][:, 0:1] * (grad - first - unit * second)
            if p == 0:
                grad = grad + m.hidden[...]
                for g in range(m.n_groups):
                    m.d_small[2 + g : 3 + g, :] = jnp.sum(
                        jnp.where(m.group_col[...] == g, grad, 0.0), axis=0, keepdims=True
                    )
            for h in range(self.segs):
                low, base, count = h * self.seg_rows, h * self.rows, self.pieces_of(h)
                m.grad_output[low : low + count, :] = grad[base : base + count]
            m.grad_pieces[p] = m.grad_output[0 : self.number, :].astype(BF16)

        for p in range(PIECES):
            back(p)
        lead = m.d_qkv.shape[:-1]
        small = jnp.concatenate(
            [m.d_small[...], jnp.zeros((LANES - 8, width), F32)], axis=0
        ).T
        m.d_qkv[:, :, :, :, :, 3 * width :] = small.astype(BF16).reshape(lead + (LANES,))


def block_scratch(n, rows, total, width, hidden, out_width):
    return dict(
        length_col=((total, 1), jnp.int32),
        group_col=((total, 1), jnp.int32),
        unit=((PIECES, total, width), F32),
        inv_one=((PIECES, total, LANES), F32),
        small=((8, width), F32),
        normed=((PIECES, total, width), BF16),
        query=((total, width), BF16),
        key_value=((PIECES, total, 2 * width), BF16),
        prob=((PIECES, total, width), F32),
        attended=((total, width), BF16),
        hidden=((total, width), F32),
        unit_two=((total, width), F32),
        inv_two=((total, LANES), F32),
        normed_two=((total, width), BF16),
        activated=((total, hidden), BF16),
        slope=((total, hidden), F32),
        output=((total, width), BF16),
        grad_table=((total, out_width), BF16),
        grad_output=((total, width), F32),
        grad_branch=((total, width), BF16),
        d_small=((8, width), F32),
        grad_prob=((PIECES, total, width), F32),
    )


NAMES = ("qkv", "out", "up", "down", "proj")


def main_kernel(n_entries, names, segs, seg_rows, rows, *refs):
    m = types.SimpleNamespace(**dict(zip(names, refs)))
    place = Place(n_entries)
    n, half = place.n, place.n // 2
    shard = m.ln1_gain.shape[0]
    m.n_groups = m.group_table.shape[0]
    feats = m.grad_embed.shape[0]
    block = Block(m, segs, seg_rows, rows, feats)
    width = block.width
    gather, reduce = types.SimpleNamespace(), types.SimpleNamespace()
    for i, name in enumerate(NAMES):
        whole, parts = getattr(m, "w_" + name), getattr(m, "d_" + name)
        setattr(gather, name, Gather(place, whole, m.g_send.at[i], m.g_recv.at[i]))
        held = [getattr(m, f"{kind}_{name}") for kind in ("core", "one", "two", "along")]
        setattr(reduce, name, Reduce(place, parts, *held, m.r_send.at[i], m.r_recv.at[i]))
        if name != "qkv":
            whole[place.z, place.x, place.c, place.y] = getattr(m, "s_" + name)[...]
    mine = m.w_qkv.at[place.z, place.x, place.c, place.y]
    mine[:, : 3 * width] = m.s_qkv[...]
    small = jnp.concatenate(
        [
            m.ln1_gain[...].astype(F32).reshape(1, shard),
            m.ln2_gain[...].astype(F32).reshape(1, shard),
            m.group_table[...].astype(F32),
            jnp.zeros((6 - m.n_groups, shard), F32),
        ],
        axis=0,
    )
    small = jnp.concatenate([small, jnp.zeros((8, LANES - shard), F32)], axis=1).T
    small = jnp.concatenate([small[:shard], jnp.zeros((shard, LANES - 8), F32)], axis=1)
    mine[:, 3 * width :] = small.astype(BF16)
    meet(place)
    gather.out.z_start()
    gather.qkv.z_start()

    text_len = m.text_ids.shape[0]
    text_keys(
        block.number, seg_rows, rows, segs, half, m.text_ids, m.text_mask, m.row_key, m.seg_key
    )
    acc = m.grad_prob.reshape(PIECES * block.total, width)
    acc = acc.at[pl.ds(0, half * rows // 2), pl.ds(0, 4 * LANES)]
    acc[...] = jnp.zeros(acc.shape, F32)
    scatter = Sweep(
        text_len,
        lambda start, count: scatter_block(
            start, count, m.row_key, m.seg_key, m.grad_embed, acc
        ),
    )
    scatter.go(2)
    gather.out.z_wait()
    gather.up.z_start()
    scatter.go(3)
    gather.qkv.z_wait()
    block.load()
    gather.out.one_wait()
    gather.out.two_wait()
    scatter.go(3)
    gather.out.three_wait()
    gather.qkv.one_wait()
    gather.down.z_start()
    scatter.go(3)
    gather.qkv.two_wait()
    gather.up.z_wait()
    gather.proj.z_start()
    scatter.go(3)
    gather.qkv.three_wait()
    gather.out.core_wait()
    scatter.go()

    def pack(i, carry):
        span = pl.ds(pl.multiple_of(i * rows, rows), rows)
        for k in range(4):
            value = acc[span, k * LANES : (k + 1) * LANES]
            m.sent_grad[i + (k // 2) * (half // 2) + (k % 2) * half] = value.astype(BF16)
        return carry

    lax.fori_loop(0, half // 2, pack, 0)
    gather.qkv.core_wait()
    block.norm_one()
    gather.up.one_wait()
    gather.up.two_wait()
    block.project_qkv()
    gather.down.z_wait()
    exchange(place, m.sent_grad, m.came_grad, m.xg_send, m.xg_recv)
    gather.up.three_wait()
    block.attend()
    block.norm_two()
    gather.down.one_wait()
    gather.down.two_wait()
    gather.up.core_wait()
    block.up()
    gather.proj.z_wait()
    gather.down.three_wait()
    gather.proj.one_wait()
    gather.proj.two_wait()
    gather.down.core_wait()
    block.down()
    exchange_wait(place, m.sent_grad, m.came_grad, m.xg_send, m.xg_recv, False)
    block.table_back()
    block.proj_grad()
    reduce.proj.core_start()
    gather.proj.three_wait()
    reduce.proj.core_wait()
    gather.proj.core_wait()
    block.proj_back()
    block.down_grad()
    reduce.down.core_start()
    block.table()
    exchange(place, m.came_grad, m.came_table, m.xt_send, m.xt_recv)
    block.down_back()
    block.up_grad()
    reduce.up.core_start()
    reduce.down.core_wait()
    block.up_back()
    block.out_back()
    reduce.out.core_start()
    reduce.proj.one_wait()
    block.attend_back()
    reduce.up.core_wait()
    block.qkv_back()
    reduce.proj.two_wait()
    block.normed_back()
    reduce.down.one_wait()
    block.norm_back()
    reduce.qkv.core_start()
    pieces_out = pltpu.make_async_copy(m.grad_pieces, m.o_pieces, m.o_sem.at[0])
    pieces_out.start()
    reduce.qkv.core_wait()
    reduce.down.two_wait()
    exchange_wait(place, m.came_grad, m.came_table, m.xt_send, m.xt_recv, False)
    for side in range(2):
        part = m.came_table[side * half : (side + 1) * half].reshape(half * rows, LANES)
        m.table[side * LANES : (side + 1) * LANES, :] = part.astype(F32).T.astype(BF16)
    lookup = Sweep(
        text_len,
        lambda start, count: lookup_block(
            start, count, m.row_key, m.seg_key, m.table, m.found
        ),
    )
    outs = []

    def finish(i, name):
        stage = getattr(m, "t_" + name)
        getattr(reduce, name).z_wait(stage)
        source = stage.at[:, : 3 * width] if name == "qkv" else stage
        outs.append(pltpu.make_async_copy(source, getattr(m, "o_" + name), m.o_sem.at[i]))
        outs[-1].start()

    lookup.go(3)
    reduce.up.one_wait()
    lookup.go(2)
    finish(1, "proj")
    lookup.go(2)
    reduce.out.core_wait()
    reduce.up.two_wait()
    lookup.go(2)
    reduce.qkv.one_wait()
    lookup.go(2)
    finish(2, "down")
    lookup.go(2)
    reduce.qkv.two_wait()
    lookup.go(2)
    reduce.out.one_wait()
    finish(3, "up")
    lookup.go()
    found_out = pltpu.make_async_copy(m.found, m.o_found, m.o_sem.at[4])
    found_out.start()
    reduce.out.two_wait()
    finish(5, "qkv")
    small = m.t_qkv[:, 3 * width :]
    small = jnp.concatenate([small, jnp.zeros((LANES - shard, LANES), F32)], axis=0).T
    m.o_ln1[...] = small[0:1, :shard].reshape(shard)
    m.o_ln2[...] = small[1:2, :shard].reshape(shard)
    m.o_group[...] = small[2 : 2 + m.n_groups, :shard]
    finish(6, "out")
    exchange_wait(place, m.sent_grad, m.came_grad, m.xg_send, m.xg_recv, True)
    exchange_wait(place, m.came_grad, m.came_table, m.xt_send, m.xt_recv, True)
    for name in NAMES:
        getattr(gather, name).finish()
        getattr(reduce, name).finish()
    pieces_out.wait()
    found_out.wait()
    for copy in outs:
        copy.wait()


def copy_kernel(count, *refs):
    ins, outs, held = refs[:count], refs[count : 2 * count], refs[2 * count : 3 * count]
    come, go = refs[3 * count :]
    inward = [pltpu.make_async_copy(ins[i], held[i], come.at[i]) for i in range(count)]
    outward = [pltpu.make_async_copy(held[i], outs[i], go.at[i]) for i in range(count)]
    for copy in inward:
        copy.start()
    for i in range(count):
        inward[i].wait()
        outward[i].start()
    for copy in outward:
        copy.wait()


def full(shape, dtype):
    return jax.ShapeDtypeStruct(shape, dtype)


def body(
    mesh_shape,
    pieces,
    lengths,
    entry_group,
    group_table,
    ln1_gain,
    w_qkv,
    w_out,
    ln2_gain,
    w_up,
    w_down,
    w_proj,
    text_ids,
    text_mask,
    grad_embed,
):
    n_entries = mesh_shape["entries"]
    n = n_entries * mesh_shape["feat"]
    n_z = n_entries // 4
    number, width = pieces.shape[0], pieces.shape[2]
    feats = grad_embed.shape[0]
    text_len = text_ids.shape[0]
    segs = LANES // feats
    seg_rows = -(-number // segs)
    rows = -(-seg_rows // 16) * 16
    half, total = n // 2, segs * rows
    pieces = jnp.transpose(pieces, (1, 0, 2))
    vmem = pl.BlockSpec(memory_space=VMEM)
    hbm = pl.BlockSpec(memory_space=pl.ANY)
    dma = pltpu.SemaphoreType.DMA

    ins = dict(
        pieces=pieces,
        lengths=lengths,
        groups=entry_group,
        group_table=group_table,
        ln1_gain=ln1_gain,
        s_qkv=w_qkv,
        s_out=w_out,
        ln2_gain=ln2_gain,
        s_up=w_up,
        s_down=w_down,
        s_proj=w_proj,
        text_ids=text_ids,
        text_mask=text_mask,
        grad_embed=grad_embed,
    )
    outs = dict(
        o_found=full((feats, text_len), BF16),
        o_pieces=full(pieces.shape, BF16),
        o_group=full(group_table.shape, F32),
        o_ln1=full(ln1_gain.shape, F32),
        o_qkv=full(w_qkv.shape, F32),
        o_out=full(w_out.shape, F32),
        o_ln2=full(ln2_gain.shape, F32),
        o_up=full(w_up.shape, F32),
        o_down=full(w_down.shape, F32),
        o_proj=full(w_proj.shape, F32),
    )
    tiny = ("o_group", "o_ln1", "o_ln2")
    scratch = {
        name: VMEM(*item)
        for name, item in block_scratch(
            n, rows, total, width, w_up.shape[1], w_proj.shape[1]
        ).items()
    }
    lead = (n_z, 2, 2, 2)
    shapes = dict(
        qkv=(w_qkv.shape[0], w_qkv.shape[1] + LANES),
        out=w_out.shape,
        up=w_up.shape,
        down=w_down.shape,
        proj=w_proj.shape,
    )
    for name, shape in shapes.items():
        scratch["w_" + name] = VMEM(lead + shape, BF16)
        scratch["d_" + name] = VMEM(lead + shape, BF16)
        scratch["t_" + name] = VMEM(shape, F32)
        scratch["core_" + name] = VMEM((n_z, 2, 2) + shape, BF16)
        scratch["one_" + name] = VMEM((2, n_z) + shape, BF16)
        scratch["two_" + name] = VMEM((n_z,) + shape, BF16)
        scratch["along_" + name] = VMEM((n_z - 1,) + shape, BF16)
    for name in ("sent_grad", "came_grad", "came_table"):
        scratch[name] = VMEM((n, rows, LANES), BF16)
    scratch.update(
        row_key=VMEM((1, text_len), jnp.int32),
        seg_key=VMEM((1, text_len), jnp.int32),
        table=VMEM((2 * LANES, half * rows), BF16),
        found=VMEM((feats, text_len), BF16),
        grad_pieces=VMEM(pieces.shape, BF16),
        g_send=dma((len(NAMES), n_z + 6)),
        g_recv=dma((len(NAMES), n_z + 6)),
        r_send=dma((len(NAMES), n_z + 4)),
        r_recv=dma((len(NAMES), n_z + 4)),
        xg_send=dma((n,)),
        xg_recv=dma((n,)),
        xt_send=dma((n,)),
        xt_recv=dma((n,)),
        o_sem=dma((7,)),
    )
    results = pl.pallas_call(
        functools.partial(
            main_kernel,
            n_entries,
            tuple(ins) + tuple(outs) + tuple(scratch),
            segs,
            seg_rows,
            rows,
        ),
        out_shape=tuple(outs.values()),
        in_specs=[vmem] * len(ins),
        out_specs=tuple(vmem if name in tiny else hbm for name in outs),
        scratch_shapes=list(scratch.values()),
        compiler_params=pltpu.CompilerParams(
            collective_id=0, has_side_effects=True, vmem_limit_bytes=VMEM_BYTES
        ),
    )(*ins.values())
    results = pl.pallas_call(
        functools.partial(copy_kernel, len(results)),
        out_shape=tuple(outs.values()),
        in_specs=[hbm] * len(results),
        out_specs=(hbm,) * len(results),
        scratch_shapes=[VMEM(leaf.shape, leaf.dtype) for leaf in outs.values()]
        + [dma((len(results),)), dma((len(results),))],
    )(*results)
    found, grad_pieces, *others = results
    return (found, jnp.transpose(grad_pieces, (1, 0, 2)), *others)


VMEM_BYTES = 63 * 2**20


def solution(mesh):
    both = P(AXES)
    rows = P(AXES, None)
    return jax.shard_map(
        functools.partial(body, dict(mesh.shape)),
        mesh=mesh,
        in_specs=(
            P(AXES, None, None),
            both,
            both,
            P(None, AXES),
            both,
            rows,
            rows,
            both,
            rows,
            rows,
            rows,
            P(),
            P(),
            rows,
        ),
        out_specs=(
            rows,
            P(AXES, None, None),
            P(None, AXES),
            both,
            rows,
            rows,
            both,
            rows,
            rows,
            rows,
        ),
        check_vma=False,
    )
```

```python
import functools
import types

import jax
import jax.numpy as jnp
from jax import lax
from jax.experimental import pallas as pl
from jax.experimental.pallas import tpu as pltpu
from jax.sharding import PartitionSpec as P

HEADS = 8
HEAD = 64
PIECES = 7
LANES = 128
TBLOCK = 512
AXES = ("entries", "feat")
MESH = pl.DeviceIdType.MESH
VMEM = pltpu.VMEM
BF16 = jnp.bfloat16
F32 = jnp.float32

epsilon = 1e-05


def contract(left_side, right_side, left_dim, right_dim):
    return lax.dot_general(
        left_side,
        right_side,
        (((left_dim,), (right_dim,)), ((), ())),
        preferred_element_type=jnp.float32,
    )


class Place:
    def __init__(self, n_entries):
        entry = lax.axis_index("entries")
        self.n_z = n_entries // 4
        self.n = n_entries * 2
        self.y = lax.axis_index("feat")
        self.c = lax.rem(entry, 2)
        self.x = lax.rem(lax.div(entry, 2), 2)
        self.z = lax.div(entry, 4)
        self.line = entry * 2 + self.y
        first = self.c == 0
        self.x1 = jnp.where(first, 1 - self.x, self.x)
        self.y1 = jnp.where(first, self.y, 1 - self.y)
        self.x2 = jnp.where(first, self.x, 1 - self.x)
        self.y2 = jnp.where(first, 1 - self.y, self.y)

    def at(self, z, x, c, y):
        return ((z * 2 + x) * 2 + c, y)

    def along_z(self, step):
        return lax.rem(self.z + step, self.n_z)


def partners(place):
    p = place
    return [p.at(p.along_z(k), p.x, p.c, p.y) for k in range(1, p.n_z)] + [
        p.at(p.z, p.x, 1 - p.c, p.y),
        p.at(p.z, p.x1, p.c, p.y1),
        p.at(p.z, p.x2, p.c, p.y2),
    ]


def remote(src, dst, send, recv, to):
    return pltpu.make_async_remote_copy(
        src_ref=src, dst_ref=dst, send_sem=send, recv_sem=recv, device_id=to, device_id_type=MESH
    )


def thirds(n_z):
    others = list(range(1, n_z))
    return [others[i * len(others) // 3 : (i + 1) * len(others) // 3] for i in range(3)]


class Gather:
    def __init__(self, place, whole, send, recv):
        p = self.place = place
        nz = p.n_z
        self.groups = thirds(nz)
        to_one = p.at(p.z, p.x1, p.c, p.y1)
        to_two = p.at(p.z, p.x2, p.c, p.y2)
        to_core = p.at(p.z, p.x, 1 - p.c, p.y)

        def shard(k, x, y):
            return whole.at[p.along_z(nz - k), x, p.c, y]

        def copy(ref, index, to):
            return remote(ref, ref, send, recv.at[index], to)

        self.along = {
            k: copy(shard(0, p.x, p.y), k - 1, p.at(p.along_z(k), p.x, p.c, p.y))
            for k in range(1, nz)
        }
        self.one = [copy(shard(k, p.x, p.y), nz - 1 + k, to_one) for k in range(nz)]
        base = 2 * nz - 1
        self.two = [copy(shard(k, p.x, p.y), base, to_two) for k in range(nz)]
        self.three = [copy(shard(k, p.x1, p.y1), base + 1, to_two) for k in range(nz)]
        cols = [(p.x, p.y), (p.x1, p.y1), (p.x2, p.y2), (1 - p.x, 1 - p.y)]
        self.core = [copy(whole.at[:, x, p.c, y], base + 2, to_core) for x, y in cols]
        self.all_two = copy(whole.at[:, p.x, p.c, p.y], base, to_two)
        self.all_three = copy(whole.at[:, p.x1, p.c, p.y1], base + 1, to_two)
        self.all_core = copy(whole.at[:, :, p.c], base + 2, to_core)
        lines = whole.reshape((p.n,) + whole.shape[4:])
        self.all_sent = copy(lines.at[pl.ds(0, p.n - 1)], base, to_two)

    def start(self):
        for copy in self.along.values():
            copy.start()
        self.one[0].start()
        self.two[0].start()

    def z_wait(self, i):
        for k in self.groups[i]:
            self.along[k].wait_recv()
            self.one[k].start()
            self.two[k].start()
        if i == 2:
            self.core[0].start()

    def one_wait(self, i):
        for k in [0] if i == 0 else self.groups[i - 1]:
            self.one[k].wait_recv()
            self.three[k].start()
        if i == 3:
            self.core[1].start()

    def two_wait(self):
        self.all_two.wait_recv()
        self.core[2].start()

    def three_wait(self):
        self.all_three.wait_recv()
        self.core[3].start()

    def core_wait(self):
        self.all_core.wait_recv()

    def finish(self):
        self.all_sent.wait_send()


class Reduce:
    def __init__(self, place, parts, held_core, held_one, held_two, held_z, send, recv):
        p = self.place = place
        nz = p.n_z
        self.parts, self.held_core = parts, held_core
        self.held_one, self.held_two, self.held_z = held_one, held_two, held_z
        self.cols = [(p.x, p.y), (p.x1, p.y1), (p.x2, p.y2), (1 - p.x, 1 - p.y)]
        to_one = p.at(p.z, p.x1, p.c, p.y1)
        to_two = p.at(p.z, p.x2, p.c, p.y2)
        to_core = p.at(p.z, p.x, 1 - p.c, p.y)

        def col(k):
            return parts.at[:, self.cols[k][0], p.c, self.cols[k][1]]

        self.core = remote(parts.at[:, :, 1 - p.c], held_core, send, recv.at[0], to_core)
        self.one = [
            remote(col(1), held_one.at[0], send, recv.at[1], to_one),
            remote(col(3), held_one.at[1], send, recv.at[2], to_one),
        ]
        self.two = remote(col(2), held_two, send, recv.at[3], to_two)
        self.along = [
            remote(
                parts.at[p.along_z(k), p.x, p.c, p.y],
                held_z.at[k - 1],
                send,
                recv.at[4],
                p.at(p.along_z(k), p.x, p.c, p.y),
            )
            for k in range(1, nz)
        ]

        landed = held_z.at[pl.ds(0, nz - 1)]
        self.all_along = remote(landed, landed, send, recv.at[4], to_two)
        lines = parts.reshape((p.n,) + parts.shape[4:]).at[pl.ds(0, p.n - 1)]
        self.all_sent = remote(lines, lines, send, recv.at[4], to_two)

    def add(self, k, other):
        p, (x, y) = self.place, self.cols[k]
        self.parts[:, x, p.c, y] = (
            self.parts[:, x, p.c, y].astype(F32) + other.astype(F32)
        ).astype(BF16)

    def core_start(self):
        self.core.start()

    def core_wait(self):
        self.core.wait_recv()
        for k in (3, 1, 2, 0):
            x, y = self.cols[k]
            self.add(k, self.held_core[:, x, y])
            if k == 3:
                self.one[1].start()
            if k == 1:
                self.one[0].start()

    def one_wait(self):
        self.one[1].wait_recv()
        self.add(2, self.held_one[1])
        self.two.start()

    def one_more_wait(self):
        self.one[0].wait_recv()
        self.add(0, self.held_one[0])

    def two_wait(self):
        self.two.wait_recv()
        self.add(0, self.held_two[...])
        for copy in self.along:
            copy.start()

    def z_wait(self, out):
        p = self.place
        total = self.parts[p.z, p.x, p.c, p.y].astype(F32)
        self.all_along.wait_recv()
        for k in range(len(self.along)):
            total = total + self.held_z[k].astype(F32)
        out[...] = total

    def finish(self):
        self.all_sent.wait_send()


def exchange(place, src, dst, send, recv):
    dst[place.line] = src[place.line]

    def begin(step, carry):
        other = lax.rem(place.line + step, place.n)
        to = (lax.div(other, 2), lax.rem(other, 2))
        remote(src.at[other], dst.at[place.line], send, recv, to).start()
        return carry

    lax.fori_loop(1, place.n, begin, 0)


def exchange_wait(place, src, dst, send, recv, sends):
    blocks = pl.ds(0, place.n - 1)
    other = lax.rem(place.line + 1, place.n)
    copy = remote(
        src.at[blocks], dst.at[blocks], send, recv, (lax.div(other, 2), lax.rem(other, 2))
    )
    if sends:
        copy.wait_send()
    else:
        copy.wait_recv()


def text_keys(number, seg_rows, rows, segs, half, ids, mask, row_key, seg_key):
    length = ids.shape[0]
    entry = ids[...].reshape(1, length)
    source = ((entry.astype(F32) + 0.5) * (1.0 / number)).astype(jnp.int32)
    within = entry - source * number
    segment = jnp.zeros_like(entry)
    for h in range(1, segs):
        segment = segment + (within >= h * seg_rows).astype(jnp.int32)
    upper = (source >= half).astype(jnp.int32)
    row_key[...] = (source - half * upper) * rows + within - segment * seg_rows
    seg_key[...] = jnp.where(mask[...].reshape(1, length) != 0, upper * segs + segment, -1)


def text_blocks(length):
    whole = length // TBLOCK
    return whole, length - whole * TBLOCK


def one_hot(keys, depth):
    width = keys.shape[1]
    return (lax.broadcasted_iota(jnp.int32, (depth, width), 0) == keys).astype(F32).astype(BF16)


def scatter_block(start, width, row_ref, seg_ref, cot_ref, acc_ref):
    span = pl.ds(start, width)
    depth, side = acc_ref.shape[0], acc_ref.shape[1] // 2
    seg = seg_ref[:, span]
    cot = cot_ref[:, span].astype(F32)
    spread = jnp.concatenate(
        [jnp.where(seg == q, cot, 0.0).astype(BF16) for q in range(side // cot.shape[0])], axis=0
    )
    for k in range(2):
        hot = one_hot(row_ref[:, span] - k * depth, depth)
        acc_ref[:, k * side : (k + 1) * side] += contract(hot, spread, 1, 1)


class Sweep:
    def __init__(self, length, block):
        self.block, self.done = block, 0
        self.whole, self.tail = text_blocks(length)

    def go(self, low, high):
        last = high == SHARES
        low, high = low * self.whole // SHARES, high * self.whole // SHARES

        def step(i, carry):
            self.block(pl.multiple_of(i * TBLOCK, TBLOCK), TBLOCK)
            return carry

        if high > low:
            lax.fori_loop(low, high, step, 0)
        if last and self.tail:
            self.block(self.whole * TBLOCK, self.tail)


def lookup_block(start, width, row_ref, seg_ref, table_ref, out_ref):
    span = pl.ds(start, width)
    hot = one_hot(row_ref[:, span], table_ref.shape[1])
    seg = seg_ref[:, span]
    wide = jnp.dot(table_ref[...], hot, preferred_element_type=F32)
    feats = out_ref.shape[0]
    found = jnp.zeros((feats, width), F32)
    for q in range(table_ref.shape[0] // feats):
        found = found + jnp.where(seg == q, wide[q * feats : (q + 1) * feats], 0.0)
    out_ref[:, span] = found.astype(BF16)


def cast_pair(value):
    high = value.astype(BF16)
    return high, (value - high.astype(F32)).astype(BF16)


def head_ones():
    head_row = lax.broadcasted_iota(jnp.int32, (4 * HEAD, 4 * HEAD), 0) // HEAD
    head_col = lax.broadcasted_iota(jnp.int32, (4 * HEAD, 4 * HEAD), 1) // HEAD
    return (head_row == head_col).astype(F32).astype(BF16)


def head_sum(value, ones):
    high, low = cast_pair(value)
    step = 4 * HEAD
    return jnp.concatenate(
        [
            jnp.dot(high[:, j : j + step], ones, preferred_element_type=F32)
            + jnp.dot(low[:, j : j + step], ones, preferred_element_type=F32)
            for j in range(0, value.shape[1], step)
        ],
        axis=1,
    )


def flat(ref, low=None, high=None):
    value = ref[...] if low is None else ref[:, :, :, :, :, low:high]
    return value.reshape(-1, value.shape[-1])


def spread_segments(blocks, feats, segs):
    lane = lax.broadcasted_iota(jnp.int32, blocks[0].shape, 1) // feats
    out = []
    for h in range(segs):
        whole = None
        for j in range(segs):
            shift = ((j - h) * feats) % LANES
            moved = blocks[j] if shift == 0 else pltpu.roll(blocks[j], shift, 1)
            whole = moved if whole is None else jnp.where(lane == j, moved, whole)
        out.append(whole)
    return out


class Block:
    def __init__(self, m, segs, seg_rows, rows, feats):
        self.m, self.segs, self.seg_rows, self.rows, self.feats = m, segs, seg_rows, rows, feats
        self.number = m.pieces.shape[1]
        self.width = m.pieces.shape[2]
        self.total = segs * rows

    def pieces_of(self, h):
        return min(self.seg_rows, max(self.number - h * self.seg_rows, 0))

    def column(self, ref):
        line = lax.broadcasted_iota(jnp.int32, (self.total, 1), 0)
        segment, within = line // self.rows, line % self.rows
        entry = jnp.where(within < self.seg_rows, segment * self.seg_rows + within, -1)
        values = ref[...].reshape(1, self.number)
        lane = lax.broadcasted_iota(jnp.int32, (self.total, self.number), 1)
        return jnp.sum(jnp.where(lane == entry, values, 0), axis=1, keepdims=True)

    def load(self):
        m = self.m
        m.length_col[...] = self.column(m.lengths)
        m.group_col[...] = self.column(m.groups)
        for p in range(PIECES):
            value = m.pieces[p].astype(F32)
            for h in range(self.segs):
                low, base, count = h * self.seg_rows, h * self.rows, self.pieces_of(h)
                m.unit[p, base : base + count, :] = value[low : low + count]
                m.unit[p, base + count : base + self.rows, :] = jnp.zeros(
                    (self.rows - count, self.width), F32
                )

    def norm_one(self):
        m, width = self.m, self.width
        small = flat(m.w_out, width, width + LANES).astype(F32).T
        m.small[...] = small[:8]
        start = m.unit[0]
        for g in range(m.n_groups):
            start = start + jnp.where(m.group_col[...] == g, small[2 + g : 3 + g, :], 0.0)
        m.unit[0] = start
        m.hidden[...] = start

        def one(p, carry):
            value = m.unit[p]
            centered = value - jnp.mean(value, axis=1, keepdims=True)
            inv = lax.rsqrt(jnp.mean(centered * centered, axis=1, keepdims=True) + epsilon)
            unit = centered * inv
            m.unit[p] = unit
            m.inv_one[p] = jnp.broadcast_to(inv, (self.total, LANES))
            m.normed[p] = (unit * m.small[0:1, :]).astype(BF16)
            return carry

        lax.fori_loop(0, PIECES, one, 0)

    def project_qkv(self, i):
        m, width = self.m, self.width
        step = width // 2
        if i == 4:
            m.query[...] = jnp.dot(
                m.normed[0], flat(m.w_qkv, 0, width), preferred_element_type=F32
            ).astype(BF16)
            return
        m.key_value[:, :, i * step : (i + 1) * step] = (
            jnp.dot(
                m.normed[...].reshape(PIECES * self.total, width),
                flat(m.w_qkv, width + i * step, width + (i + 1) * step),
                preferred_element_type=F32,
            )
            .astype(BF16)
            .reshape(PIECES, self.total, step)
        )

    def score(self, i):
        m, width = self.m, self.width
        ones = head_ones()

        def score(p, carry):
            product = m.query[...].astype(F32) * m.key_value[p, :, :width].astype(F32)
            m.prob[p] = head_sum(product, ones) * (HEAD**-0.5)
            return carry

        lax.fori_loop(*self.half_of(PIECES, i), score, 0)

    def half_of(self, count, i):
        return i * count // 2, (i + 1) * count // 2

    def soft(self, half):
        m, width = self.m, self.width

        def soft(i, carry):
            span = pl.ds(pl.multiple_of(i * 16, 16), 16)
            length = m.length_col[span, :]
            scores = [
                jnp.where(p < length, m.prob[p, span, :], -1e30) for p in range(PIECES)
            ]
            highest = functools.reduce(jnp.maximum, scores)
            raised = [jnp.exp(s - highest) for s in scores]
            inv = 1.0 / functools.reduce(jnp.add, raised)
            total = jnp.zeros((16, width), F32)
            for p in range(PIECES):
                prob = raised[p] * inv
                m.prob[p, span, :] = prob
                total = total + prob.astype(BF16).astype(F32) * m.key_value[
                    p, span, width:
                ].astype(F32)
            m.attended[span, :] = total.astype(BF16)
            return carry

        lax.fori_loop(*self.half_of(self.total // 16, half), soft, 0)

    def norm_two(self):
        m, width = self.m, self.width
        hidden = m.hidden[...] + jnp.dot(
            m.attended[...], flat(m.w_out, 0, width), preferred_element_type=F32
        )
        m.hidden[...] = hidden
        centered = hidden - jnp.mean(hidden, axis=1, keepdims=True)
        inv = lax.rsqrt(jnp.mean(centered * centered, axis=1, keepdims=True) + epsilon)
        unit = centered * inv
        m.unit_two[...] = unit
        m.inv_two[...] = jnp.broadcast_to(inv, (self.total, LANES))
        m.normed_two[...] = (unit * m.small[1:2, :]).astype(BF16)

    def up(self, i):
        m, step = self.m, 2 * LANES
        tiles = m.activated.shape[1] // step

        def one(j, carry):
            span = pl.ds(pl.multiple_of(j * step, step), step)
            weight = m.w_up[:, :, :, :, :, span].reshape(self.width, step)
            upward = jnp.dot(m.normed_two[...], weight, preferred_element_type=F32)
            normal = 0.5 * (1.0 + lax.erf(upward * (0.5**0.5)))
            m.activated[:, span] = (upward * normal).astype(BF16)
            m.slope[:, span] = normal + upward * (
                jnp.exp(-0.5 * upward * upward) * 0.3989422804014327
            )
            return carry

        lax.fori_loop(i * tiles // 4, (i + 1) * tiles // 4, one, 0)

    def down(self):
        m = self.m
        m.output[...] = (
            m.hidden[...]
            + jnp.dot(m.activated[...], flat(m.w_down), preferred_element_type=F32)
        ).astype(BF16)

    def table(self, i):
        m, segs, rows = self.m, self.segs, self.rows
        step = m.w_proj.shape[-1] // 4
        wide = jnp.dot(
            m.output[...],
            flat(m.w_proj, i * step, (i + 1) * step),
            preferred_element_type=F32,
        )
        for g in range(step // LANES):
            value = wide[:, g * LANES : (g + 1) * LANES]
            parts = [value[h * rows : (h + 1) * rows] for h in range(segs)]
            for j, part in enumerate(spread_segments(parts, self.feats, segs)):
                m.came_grad[i * (step // self.feats) + g * segs + j] = part.astype(BF16)


    def table_back(self, i):
        m, segs, rows = self.m, self.segs, self.rows
        groups = m.grad_table.shape[1] // LANES

        def one(g, carry):
            span = pl.ds(pl.multiple_of(g * LANES, LANES), LANES)
            parts = [m.came_grad[g * segs + j].astype(F32) for j in range(segs)]
            for h, part in enumerate(spread_segments(parts, self.feats, segs)):
                m.grad_table[h * rows : (h + 1) * rows, span] = part.astype(BF16)
            return carry

        lax.fori_loop(*self.half_of(groups, i), one, 0)

    def put(self, ref, value):
        ref[...] = value.astype(BF16).reshape(ref.shape)

    def halves(self, value, i):
        half = value.shape[-1] // 2
        return value[:, i * half : (i + 1) * half]

    def proj_grad(self, i):
        m = self.m
        target = (m.d_proj0, m.d_proj1)[i]
        self.put(target, contract(m.output[...], self.halves(m.grad_table, i), 0, 0))

    def proj_back(self):
        m = self.m
        grad_output = contract(m.grad_table[...], flat(m.w_proj), 1, 1)
        m.grad_output[...] = grad_output
        m.grad_branch[...] = grad_output.astype(BF16)

    def down_grad(self, i):
        m = self.m
        target = (m.d_down0, m.d_down1)[i]
        self.put(target, contract(m.activated[...], self.halves(m.grad_branch, i), 0, 0))

    def down_back(self):
        m = self.m
        grad_act = contract(m.grad_branch[...], flat(m.w_down), 1, 1)
        m.activated[...] = (grad_act * m.slope[...]).astype(BF16)

    def up_grad(self, i):
        m = self.m
        target = (m.d_up0, m.d_up1)[i]
        self.put(target, contract(m.normed_two[...], self.halves(m.activated, i), 0, 0))

    def up_back(self):
        m = self.m
        grad = contract(m.activated[...], flat(m.w_up), 1, 1)
        m.d_small[...] = jnp.zeros_like(m.d_small)
        unit = m.unit_two[...]
        m.d_small[1:2, :] = jnp.sum(grad * unit, axis=0, keepdims=True)
        grad = grad * m.small[1:2, :]
        first = jnp.mean(grad, axis=1, keepdims=True)
        second = jnp.mean(grad * unit, axis=1, keepdims=True)
        hidden = m.grad_output[...] + m.inv_two[:, 0:1] * (grad - first - unit * second)
        m.hidden[...] = hidden
        m.grad_branch[...] = hidden.astype(BF16)

    def out_back(self):
        m, width = self.m, self.width
        m.d_out[:, :, :, :, :, :width] = (
            contract(m.attended[...], m.grad_branch[...], 0, 0)
            .astype(BF16)
            .reshape(m.d_out.shape[:-1] + (width,))
        )
        m.attended[...] = contract(m.grad_branch[...], flat(m.w_out, 0, width), 1, 1).astype(BF16)

    def back_score(self, i):
        m, width = self.m, self.width
        ones = head_ones()

        def score(p, carry):
            product = m.attended[...].astype(F32) * m.key_value[p, :, width:].astype(F32)
            m.grad_prob[p] = head_sum(product, ones)
            return carry

        lax.fori_loop(*self.half_of(PIECES, i), score, 0)

    def back_soft(self, half):
        m, width = self.m, self.width
        scale = HEAD**-0.5

        def soft(i, carry):
            span = pl.ds(pl.multiple_of(i * 16, 16), 16)
            inner = jnp.zeros((16, width), F32)
            for p in range(PIECES):
                inner = inner + m.prob[p, span, :] * m.grad_prob[p, span, :]
            query = m.query[span, :].astype(F32)
            grad_att = m.attended[span, :].astype(F32)
            grad_query = jnp.zeros((16, width), F32)
            for p in range(PIECES):
                prob = m.prob[p, span, :]
                low = prob.astype(BF16).astype(F32)
                grad = (prob * (m.grad_prob[p, span, :] - inner)).astype(BF16).astype(F32)
                grad_query = grad_query + grad * m.key_value[p, span, :width].astype(F32)
                m.key_value[p, span, :width] = (grad * query * scale).astype(BF16)
                m.key_value[p, span, width:] = (low * grad_att).astype(BF16)
            m.query[span, :] = (grad_query * scale).astype(BF16)
            return carry

        lax.fori_loop(*self.half_of(self.total // 16, half), soft, 0)

    def qkv_back(self, i):
        m, width = self.m, self.width
        if i == 4:
            self.put(m.d_q, contract(m.normed[0], m.query[...], 0, 0))
            return
        step = width // 2
        grad = contract(
            m.normed[...].reshape(PIECES * self.total, width),
            m.key_value[:, :, i * step : (i + 1) * step].reshape(PIECES * self.total, step),
            0,
            0,
        )
        target, low = (m.d_k, m.d_v)[i // 2], (i % 2) * step
        target[:, :, :, :, :, low : low + step] = grad.astype(BF16).reshape(
            target.shape[:-1] + (step,)
        )

    def normed_back(self):
        m, width = self.m, self.width
        m.grad_prob[...] = contract(
            m.key_value[...].reshape(PIECES * self.total, 2 * width),
            flat(m.w_qkv, width, 3 * width),
            1,
            1,
        ).reshape(PIECES, self.total, width)
        m.grad_prob[0] += contract(m.query[...], flat(m.w_qkv, 0, width), 1, 1)

    def norm_back(self):
        m, width = self.m, self.width
        gain = m.small[0:1, :]

        def back(p):
            grad = m.grad_prob[p]
            unit = m.unit[p]
            m.d_small[0:1, :] += jnp.sum(grad * unit, axis=0, keepdims=True)
            grad = grad * gain
            first = jnp.mean(grad, axis=1, keepdims=True)
            second = jnp.mean(grad * unit, axis=1, keepdims=True)
            grad = m.inv_one[p][:, 0:1] * (grad - first - unit * second)
            if p == 0:
                grad = grad + m.hidden[...]
                for g in range(m.n_groups):
                    m.d_small[2 + g : 3 + g, :] = jnp.sum(
                        jnp.where(m.group_col[...] == g, grad, 0.0), axis=0, keepdims=True
                    )
            for h in range(self.segs):
                low, base, count = h * self.seg_rows, h * self.rows, self.pieces_of(h)
                m.grad_output[low : low + count, :] = grad[base : base + count]
            m.grad_pieces[p] = m.grad_output[0 : self.number, :].astype(BF16)

        for p in range(PIECES):
            back(p)
        lead = m.d_out.shape[:-1]
        small = jnp.concatenate(
            [m.d_small[...], jnp.zeros((LANES - 8, width), F32)], axis=0
        ).T
        m.d_out[:, :, :, :, :, width:] = small.astype(BF16).reshape(lead + (LANES,))


def block_scratch(n, rows, total, width, hidden, out_width):
    return dict(
        length_col=((total, 1), jnp.int32),
        group_col=((total, 1), jnp.int32),
        unit=((PIECES, total, width), F32),
        inv_one=((PIECES, total, LANES), F32),
        small=((8, width), F32),
        normed=((PIECES, total, width), BF16),
        query=((total, width), BF16),
        key_value=((PIECES, total, 2 * width), BF16),
        prob=((PIECES, total, width), F32),
        attended=((total, width), BF16),
        hidden=((total, width), F32),
        unit_two=((total, width), F32),
        inv_two=((total, LANES), F32),
        normed_two=((total, width), BF16),
        activated=((total, hidden), BF16),
        slope=((total, hidden), F32),
        output=((total, width), BF16),
        grad_table=((total, out_width), BF16),
        grad_output=((total, width), F32),
        grad_branch=((total, width), BF16),
        d_small=((8, width), F32),
        grad_prob=((PIECES, total, width), F32),
    )


NAMES = ("out", "qkv", "up", "down", "proj")


SHARES = 18
SUMS = dict(
    proj0=("proj", 0),
    proj1=("proj", 1),
    down0=("down", 0),
    down1=("down", 1),
    up0=("up", 0),
    up1=("up", 1),
    k=("qkv", 1),
    v=("qkv", 2),
    q=("qkv", 0),
    out=("out", 0),
)


def main_kernel(n_entries, names, segs, seg_rows, rows, *refs):
    m = types.SimpleNamespace(**dict(zip(names, refs)))
    place = Place(n_entries)
    n, half = place.n, place.n // 2
    peers = partners(place)
    barrier = pltpu.get_barrier_semaphore()
    for peer in peers:
        pl.semaphore_signal(barrier, inc=1, device_id=peer, device_id_type=MESH)
    shard = m.ln1_gain.shape[0]
    width = m.i_pieces.shape[2]
    mine = {
        name: getattr(m, "w_" + name).at[place.z, place.x, place.c, place.y] for name in NAMES
    }
    targets = dict(
        i_ln1_gain=m.ln1_gain,
        i_ln2_gain=m.ln2_gain,
        i_group_table=m.group_table,
        i_out=mine["out"].at[:, :width],
        i_qkv=mine["qkv"],
        i_up=mine["up"],
        i_down=mine["down"],
        i_proj=mine["proj"],
        i_text_ids=m.text_ids,
        i_text_mask=m.text_mask,
        i_lengths=m.lengths,
        i_groups=m.groups,
        i_pieces=m.pieces,
        i_grad_embed=m.grad_embed,
    )
    inward = [
        pltpu.make_async_copy(getattr(m, name), target, m.i_sem.at[i])
        for i, (name, target) in enumerate(targets.items())
    ]
    for copy in inward:
        copy.start()
    m.n_groups = m.group_table.shape[0]
    feats = m.grad_embed.shape[0]
    block = Block(m, segs, seg_rows, rows, feats)
    gather, reduce = types.SimpleNamespace(), types.SimpleNamespace()
    for i, name in enumerate(NAMES):
        whole = getattr(m, "w_" + name)
        setattr(gather, name, Gather(place, whole, m.g_send.at[i], m.g_recv.at[i]))
    for i, name in enumerate(SUMS):
        held = [getattr(m, f"{kind}_{name}") for kind in ("d", "core", "one", "two", "along")]
        part = Reduce(place, *held, m.r_send.at[i], m.r_recv.at[i])
        part.stage, part.place_in = getattr(m, "t_" + name), SUMS[name][1]
        part.target = getattr(m, "o_" + SUMS[name][0])
        setattr(reduce, name, part)
    for copy in inward[:3]:
        copy.wait()
    small = jnp.concatenate(
        [
            m.ln1_gain[...].astype(F32).reshape(1, shard),
            m.ln2_gain[...].astype(F32).reshape(1, shard),
            m.group_table[...].astype(F32),
            jnp.zeros((6 - m.n_groups, shard), F32),
        ],
        axis=0,
    )
    small = jnp.concatenate([small, jnp.zeros((8, LANES - shard), F32)], axis=1).T
    small = jnp.concatenate([small[:shard], jnp.zeros((shard, LANES - 8), F32)], axis=1)
    mine["out"][:, width:] = small.astype(BF16)
    for copy in inward[3:8]:
        copy.wait()
    text_len = m.text_ids.shape[0]
    acc = m.grad_prob.reshape(PIECES * block.total, width)
    acc = acc.at[pl.ds(0, half * rows // 2), pl.ds(0, 4 * LANES)]
    scatter = Sweep(
        text_len,
        lambda start, count: scatter_block(
            start, count, m.row_key, m.seg_key, m.grad_embed, acc
        ),
    )
    lookup = Sweep(
        text_len,
        lambda start, count: lookup_block(
            start, count, m.row_key, m.seg_key, m.table, m.found
        ),
    )
    grad_way = (place, m.sent_grad, m.came_grad, m.xg_send, m.xg_recv)
    table_way = (place, m.came_grad, m.came_table, m.xt_send, m.xt_recv)
    going = []

    def send_out(source, target):
        going.append(pltpu.make_async_copy(source, target, m.o_sem.at[len(going)]))
        going[-1].start()

    def keys():
        for copy in inward[8:10]:
            copy.wait()
        text_keys(
            block.number, seg_rows, rows, segs, half, m.text_ids, m.text_mask, m.row_key, m.seg_key
        )
        acc[...] = jnp.zeros(acc.shape, F32)

    def load():
        for copy in inward[10:]:
            copy.wait()
        block.load()

    def pack(i, carry):
        span = pl.ds(pl.multiple_of(i * rows, rows), rows)
        for k in range(4):
            value = acc[span, k * LANES : (k + 1) * LANES]
            m.sent_grad[i + (k // 2) * (half // 2) + (k % 2) * half] = value.astype(BF16)
        return carry

    def scatter_end():
        lax.fori_loop(0, half // 2, pack, 0)

    def norm_back():
        block.norm_back()
        send_out(m.grad_pieces, m.o_pieces)

    def look_prep():
        for side in range(2):
            part = m.came_table[side * half : (side + 1) * half].reshape(half * rows, LANES)
            m.table[side * LANES : (side + 1) * LANES, :] = part.astype(F32).T.astype(BF16)

    def result(part):
        stage = part.stage
        part.z_wait(stage)
        if part is reduce.out:
            small = jnp.concatenate(
                [stage[:, width:], jnp.zeros((LANES - shard, LANES), F32)], axis=0
            ).T
            m.t_ln1[...] = small[0:1, :shard].reshape(shard)
            m.t_ln2[...] = small[1:2, :shard].reshape(shard)
            m.t_group[...] = small[2 : 2 + m.n_groups, :shard]
            send_out(m.t_ln1, m.o_ln1)
            send_out(m.t_ln2, m.o_ln2)
            send_out(m.t_group, m.o_group)
            send_out(stage.at[:, :width], m.o_out)
        else:
            columns = stage.shape[1]
            low = part.place_in * columns
            send_out(stage, part.target.at[:, low : low + columns])

    def sent_all():
        exchange_wait(*grad_way, True)
        for name in NAMES:
            getattr(gather, name).finish()

    pl.semaphore_wait(barrier, len(peers))
    gather.out.start()
    gather.qkv.start()
    gather.up.start()
    keys()
    load()
    scatter.go(0, 5)
    gather.out.one_wait(0)
    gather.out.z_wait(0)
    scatter.go(5, 6)
    gather.out.z_wait(1)
    gather.qkv.one_wait(0)
    gather.out.z_wait(2)
    gather.down.start()
    scatter.go(6, 8)
    gather.qkv.z_wait(0)
    gather.up.one_wait(0)
    scatter.go(8, 10)
    gather.out.one_wait(1)
    scatter.go(10, 11)
    gather.out.one_wait(2)
    gather.qkv.z_wait(1)
    gather.out.one_wait(3)
    scatter.go(11, 13)
    gather.qkv.z_wait(2)
    gather.out.two_wait()
    gather.down.one_wait(0)
    scatter.go(13, 15)
    gather.up.z_wait(0)
    gather.qkv.one_wait(1)
    scatter.go(15, 17)
    gather.qkv.one_wait(2)
    scatter.go(17, 18)
    scatter_end()
    gather.qkv.one_wait(3)
    gather.up.z_wait(1)
    gather.out.three_wait()
    gather.up.z_wait(2)
    gather.up.one_wait(1)
    gather.qkv.two_wait()
    gather.out.core_wait()
    gather.down.z_wait(0)
    exchange(*grad_way)
    gather.proj.start()
    gather.up.one_wait(2)
    gather.up.one_wait(3)
    gather.down.z_wait(1)
    gather.down.one_wait(1)
    gather.down.z_wait(2)
    gather.qkv.three_wait()
    gather.qkv.core_wait()
    block.norm_one()
    gather.up.two_wait()
    block.project_qkv(0)
    block.project_qkv(1)
    block.project_qkv(2)
    block.project_qkv(3)
    block.project_qkv(4)
    block.score(0)
    block.score(1)
    gather.proj.one_wait(0)
    block.soft(0)
    gather.down.one_wait(2)
    block.soft(1)
    block.norm_two()
    gather.down.one_wait(3)
    exchange_wait(*grad_way, False)
    block.table_back(0)
    gather.up.three_wait()
    block.table_back(1)
    gather.proj.z_wait(0)
    gather.down.two_wait()
    gather.up.core_wait()
    block.up(0)
    block.up(1)
    block.up(2)
    gather.proj.z_wait(1)
    block.up(3)
    gather.down.three_wait()
    gather.proj.z_wait(2)
    gather.proj.one_wait(1)
    gather.down.core_wait()
    block.down()
    block.proj_grad(0)
    reduce.proj0.core_start()
    block.proj_grad(1)
    reduce.proj1.core_start()
    gather.proj.one_wait(2)
    reduce.proj0.core_wait()
    gather.proj.one_wait(3)
    gather.proj.two_wait()
    reduce.proj1.core_wait()
    gather.proj.three_wait()
    reduce.proj0.one_wait()
    gather.proj.core_wait()
    reduce.proj0.one_more_wait()
    block.table(0)
    block.table(1)
    block.table(2)
    block.table(3)
    exchange(*table_way)
    reduce.proj1.one_wait()
    block.proj_back()
    block.down_grad(0)
    reduce.down0.core_start()
    block.down_grad(1)
    reduce.down1.core_start()
    reduce.proj0.two_wait()
    block.down_back()
    reduce.proj1.one_more_wait()
    reduce.down0.core_wait()
    block.up_grad(0)
    reduce.up0.core_start()
    block.up_grad(1)
    reduce.up1.core_start()
    block.up_back()
    reduce.down1.core_wait()
    block.out_back()
    block.back_score(0)
    block.back_score(1)
    block.back_soft(0)
    block.back_soft(1)
    block.qkv_back(0)
    reduce.up0.core_wait()
    block.qkv_back(1)
    reduce.k.core_start()
    block.qkv_back(2)
    reduce.proj1.two_wait()
    reduce.down0.one_wait()
    reduce.up1.core_wait()
    block.qkv_back(3)
    reduce.v.core_start()
    reduce.down0.one_more_wait()
    block.qkv_back(4)
    reduce.q.core_start()
    block.normed_back()
    reduce.down1.one_wait()
    exchange_wait(*table_way, False)
    norm_back()
    reduce.out.core_start()
    reduce.down1.one_more_wait()
    reduce.k.core_wait()
    reduce.down0.two_wait()
    look_prep()
    result(reduce.proj0)
    lookup.go(0, 2)
    reduce.up0.one_wait()
    reduce.v.core_wait()
    lookup.go(2, 4)
    reduce.down1.two_wait()
    result(reduce.proj1)
    lookup.go(4, 5)
    reduce.up0.one_more_wait()
    reduce.q.core_wait()
    lookup.go(5, 8)
    reduce.out.core_wait()
    reduce.up1.one_wait()
    result(reduce.down0)
    lookup.go(8, 10)
    reduce.up0.two_wait()
    lookup.go(10, 11)
    reduce.up1.one_more_wait()
    lookup.go(11, 12)
    reduce.k.one_wait()
    result(reduce.down1)
    lookup.go(12, 14)
    reduce.k.one_more_wait()
    lookup.go(14, 16)
    reduce.v.one_wait()
    reduce.up1.two_wait()
    sent_all()
    lookup.go(16, 18)
    send_out(m.found, m.o_found)
    reduce.k.two_wait()
    reduce.v.one_more_wait()
    result(reduce.up0)
    reduce.q.one_wait()
    reduce.q.one_more_wait()
    reduce.v.two_wait()
    reduce.out.one_wait()
    result(reduce.up1)
    reduce.out.one_more_wait()
    reduce.q.two_wait()
    result(reduce.k)
    reduce.out.two_wait()
    result(reduce.v)
    result(reduce.q)
    result(reduce.out)
    exchange_wait(*table_way, True)
    for name in SUMS:
        getattr(reduce, name).finish()
    for copy in going:
        copy.wait()


def copy_kernel(count, *refs):
    ins, outs, held = refs[:count], refs[count : 2 * count], refs[2 * count : 3 * count]
    come, go = refs[3 * count :]
    inward = [pltpu.make_async_copy(ins[i], held[i], come.at[i]) for i in range(count)]
    outward = [pltpu.make_async_copy(held[i], outs[i], go.at[i]) for i in range(count)]
    for copy in inward:
        copy.start()
    for i in range(count):
        inward[i].wait()
        outward[i].start()
    for copy in outward:
        copy.wait()


def full(shape, dtype):
    return jax.ShapeDtypeStruct(shape, dtype)


def body(
    mesh_shape,
    pieces,
    lengths,
    entry_group,
    group_table,
    ln1_gain,
    w_qkv,
    w_out,
    ln2_gain,
    w_up,
    w_down,
    w_proj,
    text_ids,
    text_mask,
    grad_embed,
):
    n_entries = mesh_shape["entries"]
    n = n_entries * mesh_shape["feat"]
    n_z = n_entries // 4
    number, width = pieces.shape[0], pieces.shape[2]
    feats = grad_embed.shape[0]
    text_len = text_ids.shape[0]
    segs = LANES // feats
    seg_rows = -(-number // segs)
    rows = -(-seg_rows // 16) * 16
    half, total = n // 2, segs * rows
    pieces = jnp.transpose(pieces, (1, 0, 2))
    hbm = pl.BlockSpec(memory_space=pl.ANY)
    dma = pltpu.SemaphoreType.DMA

    ins = dict(
        i_pieces=pieces,
        i_lengths=lengths,
        i_groups=entry_group,
        i_group_table=group_table,
        i_ln1_gain=ln1_gain,
        i_qkv=w_qkv,
        i_out=w_out,
        i_ln2_gain=ln2_gain,
        i_up=w_up,
        i_down=w_down,
        i_proj=w_proj,
        i_text_ids=text_ids,
        i_text_mask=text_mask,
        i_grad_embed=grad_embed,
    )
    outs = dict(
        o_found=full((feats, text_len), BF16),
        o_pieces=full(pieces.shape, BF16),
        o_group=full(group_table.shape, F32),
        o_ln1=full(ln1_gain.shape, F32),
        o_qkv=full(w_qkv.shape, F32),
        o_out=full(w_out.shape, F32),
        o_ln2=full(ln2_gain.shape, F32),
        o_up=full(w_up.shape, F32),
        o_down=full(w_down.shape, F32),
        o_proj=full(w_proj.shape, F32),
    )
    scratch = {
        name: VMEM(*item)
        for name, item in block_scratch(
            n, rows, total, width, w_up.shape[1], w_proj.shape[1]
        ).items()
    }
    lead = (n_z, 2, 2, 2)
    shapes = dict(
        out=(w_out.shape[0], width + LANES),
        qkv=w_qkv.shape,
        up=w_up.shape,
        down=w_down.shape,
        proj=w_proj.shape,
    )
    for name, shape in shapes.items():
        scratch["w_" + name] = VMEM(lead + shape, BF16)
    for name, (whole, _) in SUMS.items():
        shape = shapes[whole]
        parts_n = 3 if whole == "qkv" else 1 if whole == "out" else 2
        shape = (shape[0], shape[1] // parts_n)
        scratch["d_" + name] = VMEM(lead + shape, BF16)
        scratch["t_" + name] = VMEM(shape, F32)
        scratch["core_" + name] = VMEM((n_z, 2, 2) + shape, BF16)
        scratch["one_" + name] = VMEM((2, n_z) + shape, BF16)
        scratch["two_" + name] = VMEM((n_z,) + shape, BF16)
        scratch["along_" + name] = VMEM((n_z - 1,) + shape, BF16)
    for name in ("sent_grad", "came_grad", "came_table"):
        scratch[name] = VMEM((n, rows, LANES), BF16)
    scratch.update(
        row_key=VMEM((1, text_len), jnp.int32),
        seg_key=VMEM((1, text_len), jnp.int32),
        table=VMEM((2 * LANES, half * rows), BF16),
        found=VMEM((feats, text_len), BF16),
        grad_pieces=VMEM(pieces.shape, BF16),
        i_sem=dma((len(ins),)),
        t_ln1=VMEM(ln1_gain.shape, F32),
        t_ln2=VMEM(ln2_gain.shape, F32),
        t_group=VMEM(group_table.shape, F32),
        g_send=dma((len(NAMES),)),
        g_recv=dma((len(NAMES), 2 * n_z + 2)),
        r_send=dma((len(SUMS),)),
        r_recv=dma((len(SUMS), 5)),
        xg_send=dma(()),
        xg_recv=dma(()),
        xt_send=dma(()),
        xt_recv=dma(()),
        o_sem=dma((len(SUMS) + 5,)),
    )
    for name in ("pieces", "lengths", "groups", "group_table", "ln1_gain", "ln2_gain"):
        scratch[name] = VMEM(ins["i_" + name].shape, ins["i_" + name].dtype)
    for name in ("text_ids", "text_mask", "grad_embed"):
        scratch[name] = VMEM(ins["i_" + name].shape, ins["i_" + name].dtype)
    results = pl.pallas_call(
        functools.partial(
            main_kernel,
            n_entries,
            tuple(ins) + tuple(outs) + tuple(scratch),
            segs,
            seg_rows,
            rows,
        ),
        out_shape=tuple(outs.values()),
        in_specs=[hbm] * len(ins),
        out_specs=(hbm,) * len(outs),
        scratch_shapes=list(scratch.values()),
        compiler_params=pltpu.CompilerParams(
            collective_id=0, has_side_effects=True, vmem_limit_bytes=VMEM_BYTES
        ),
    )(*ins.values())
    results = pl.pallas_call(
        functools.partial(copy_kernel, len(results)),
        out_shape=tuple(outs.values()),
        in_specs=[hbm] * len(results),
        out_specs=(hbm,) * len(results),
        scratch_shapes=[VMEM(leaf.shape, leaf.dtype) for leaf in outs.values()]
        + [dma((len(results),)), dma((len(results),))],
    )(*results)
    found, grad_pieces, *others = results
    return (found, jnp.transpose(grad_pieces, (1, 0, 2)), *others)


VMEM_BYTES = 63 * 2**20


def solution(mesh):
    both = P(AXES)
    rows = P(AXES, None)
    return jax.shard_map(
        functools.partial(body, dict(mesh.shape)),
        mesh=mesh,
        in_specs=(
            P(AXES, None, None),
            both,
            both,
            P(None, AXES),
            both,
            rows,
            rows,
            both,
            rows,
            rows,
            rows,
            P(),
            P(),
            rows,
        ),
        out_specs=(
            rows,
            P(AXES, None, None),
            P(None, AXES),
            both,
            rows,
            rows,
            both,
            rows,
            rows,
            rows,
        ),
        check_vma=False,
    )
```

```python
import functools
import types

import jax
import jax.numpy as jnp
from jax import lax
from jax.experimental import pallas as pl
from jax.experimental.pallas import tpu as pltpu
from jax.sharding import PartitionSpec as P

HEADS = 8
HEAD = 64
PIECES = 7
LANES = 128
TBLOCK = 512
AXES = ("entries", "feat")
MESH = pl.DeviceIdType.MESH
VMEM = pltpu.VMEM
BF16 = jnp.bfloat16
F32 = jnp.float32

epsilon = 1e-05


def contract(left_side, right_side, left_dim, right_dim):
    return lax.dot_general(
        left_side,
        right_side,
        (((left_dim,), (right_dim,)), ((), ())),
        preferred_element_type=jnp.float32,
    )


class Place:
    def __init__(self, n_entries):
        entry = lax.axis_index("entries")
        self.n_z = n_entries // 4
        self.n = n_entries * 2
        self.y = lax.axis_index("feat")
        self.c = lax.rem(entry, 2)
        self.x = lax.rem(lax.div(entry, 2), 2)
        self.z = lax.div(entry, 4)
        self.line = entry * 2 + self.y
        first = self.c == 0
        self.x1 = jnp.where(first, 1 - self.x, self.x)
        self.y1 = jnp.where(first, self.y, 1 - self.y)
        self.x2 = jnp.where(first, self.x, 1 - self.x)
        self.y2 = jnp.where(first, 1 - self.y, self.y)

    def at(self, z, x, c, y):
        return ((z * 2 + x) * 2 + c, y)

    def along_z(self, step):
        return lax.rem(self.z + step, self.n_z)


def partners(place):
    p = place
    return [p.at(p.along_z(k), p.x, p.c, p.y) for k in range(1, p.n_z)] + [
        p.at(p.z, p.x, 1 - p.c, p.y),
        p.at(p.z, p.x1, p.c, p.y1),
        p.at(p.z, p.x2, p.c, p.y2),
    ]


def remote(src, dst, send, recv, to):
    return pltpu.make_async_remote_copy(
        src_ref=src, dst_ref=dst, send_sem=send, recv_sem=recv, device_id=to, device_id_type=MESH
    )


def thirds(n_z):
    others = list(range(1, n_z))
    return [others[i * len(others) // 3 : (i + 1) * len(others) // 3] for i in range(3)]


class Gather:
    def __init__(self, place, whole, send, recv, source=None):
        p = self.place = place
        nz = p.n_z
        self.groups = thirds(nz)
        to_one = p.at(p.z, p.x1, p.c, p.y1)
        to_two = p.at(p.z, p.x2, p.c, p.y2)
        to_core = p.at(p.z, p.x, 1 - p.c, p.y)

        def shard(k, x, y):
            return whole.at[p.along_z(nz - k), x, p.c, y]

        def copy(ref, index, to):
            return remote(ref, ref, send, recv.at[index], to)

        def first(index, to):
            ref = shard(0, p.x, p.y)
            return remote(ref if source is None else source, ref, send, recv.at[index], to)

        self.along = {
            k: first(k - 1, p.at(p.along_z(k), p.x, p.c, p.y)) for k in range(1, nz)
        }
        self.one = [copy(shard(k, p.x, p.y), nz - 1 + k, to_one) for k in range(nz)]
        self.one[0] = first(nz - 1, to_one)
        base = 2 * nz - 1
        self.two = [copy(shard(k, p.x, p.y), base, to_two) for k in range(nz)]
        self.two[0] = first(base, to_two)
        self.three = [copy(shard(k, p.x1, p.y1), base + 1, to_two) for k in range(nz)]
        cols = [(p.x, p.y), (p.x1, p.y1), (p.x2, p.y2), (1 - p.x, 1 - p.y)]
        self.core = [copy(whole.at[:, x, p.c, y], base + 2, to_core) for x, y in cols]
        self.all_two = copy(whole.at[:, p.x, p.c, p.y], base, to_two)
        self.all_three = copy(whole.at[:, p.x1, p.c, p.y1], base + 1, to_two)
        self.all_core = copy(whole.at[:, :, p.c], base + 2, to_core)
        lines = whole.reshape((p.n,) + whole.shape[4:])
        self.all_sent = copy(lines.at[pl.ds(0, p.n - 1)], base, to_two)

    def start(self):
        for copy in self.along.values():
            copy.start()
        self.one[0].start()
        self.two[0].start()

    def z_wait(self, i):
        for k in self.groups[i]:
            self.along[k].wait_recv()
            self.one[k].start()
            self.two[k].start()
        if i == 2:
            self.core[0].start()

    def one_wait(self, i):
        for k in [0] if i == 0 else self.groups[i - 1]:
            self.one[k].wait_recv()
            self.three[k].start()
        if i == 3:
            self.core[1].start()

    def two_wait(self):
        self.all_two.wait_recv()
        self.core[2].start()

    def three_wait(self):
        self.all_three.wait_recv()
        self.core[3].start()

    def core_wait(self):
        self.all_core.wait_recv()

    def finish(self):
        self.all_sent.wait_send()


class Reduce:
    def __init__(self, place, parts, held_core, held_one, held_two, held_z, send, recv):
        p = self.place = place
        nz = p.n_z
        self.parts, self.held_core = parts, held_core
        self.held_one, self.held_two, self.held_z = held_one, held_two, held_z
        self.cols = [(p.x, p.y), (p.x1, p.y1), (p.x2, p.y2), (1 - p.x, 1 - p.y)]
        to_one = p.at(p.z, p.x1, p.c, p.y1)
        to_two = p.at(p.z, p.x2, p.c, p.y2)
        to_core = p.at(p.z, p.x, 1 - p.c, p.y)

        def col(k):
            return parts.at[:, self.cols[k][0], p.c, self.cols[k][1]]

        self.core = remote(parts.at[:, :, 1 - p.c], held_core, send, recv.at[0], to_core)
        self.one = [
            remote(col(1), held_one.at[0], send, recv.at[1], to_one),
            remote(col(3), held_one.at[1], send, recv.at[2], to_one),
        ]
        self.two = remote(col(2), held_two, send, recv.at[3], to_two)
        self.along = [
            remote(
                parts.at[p.along_z(k), p.x, p.c, p.y],
                held_z.at[k - 1],
                send,
                recv.at[4],
                p.at(p.along_z(k), p.x, p.c, p.y),
            )
            for k in range(1, nz)
        ]

        landed = held_z.at[pl.ds(0, nz - 1)]
        self.all_along = remote(landed, landed, send, recv.at[4], to_two)
        lines = parts.reshape((p.n,) + parts.shape[4:]).at[pl.ds(0, p.n - 1)]
        self.all_sent = remote(lines, lines, send, recv.at[4], to_two)

    def add(self, k, other):
        p, (x, y) = self.place, self.cols[k]
        self.parts[:, x, p.c, y] = (
            self.parts[:, x, p.c, y].astype(F32) + other.astype(F32)
        ).astype(BF16)

    def core_start(self):
        self.core.start()

    def core_wait(self):
        self.core.wait_recv()
        for k in (3, 1, 2, 0):
            x, y = self.cols[k]
            self.add(k, self.held_core[:, x, y])
            if k == 3:
                self.one[1].start()
            if k == 1:
                self.one[0].start()

    def one_wait(self):
        self.one[1].wait_recv()
        self.add(2, self.held_one[1])
        self.two.start()

    def one_more_wait(self):
        self.one[0].wait_recv()
        self.add(0, self.held_one[0])

    def two_wait(self):
        self.two.wait_recv()
        self.add(0, self.held_two[...])
        for copy in self.along:
            copy.start()

    def z_wait(self, out):
        p = self.place
        total = self.parts[p.z, p.x, p.c, p.y].astype(F32)
        self.all_along.wait_recv()
        for k in range(len(self.along)):
            total = total + self.held_z[k].astype(F32)
        out[...] = total

    def finish(self):
        self.all_sent.wait_send()


def exchange(place, src, dst, send, recv):
    dst[place.line] = src[place.line]

    def begin(step, carry):
        turn = lax.rem(step + 3 * place.n // 4 - 1, place.n - 1) + 1
        other = lax.rem(place.line + turn, place.n)
        to = (lax.div(other, 2), lax.rem(other, 2))
        remote(src.at[other], dst.at[place.line], send, recv, to).start()
        return carry

    lax.fori_loop(1, place.n, begin, 0)


def exchange_wait(place, src, dst, send, recv, sends):
    blocks = pl.ds(0, place.n - 1)
    other = lax.rem(place.line + 1, place.n)
    copy = remote(
        src.at[blocks], dst.at[blocks], send, recv, (lax.div(other, 2), lax.rem(other, 2))
    )
    if sends:
        copy.wait_send()
    else:
        copy.wait_recv()


def text_keys(number, seg_rows, rows, segs, half, ids, mask, row_key, seg_key):
    length = ids.shape[0]
    entry = ids[...].reshape(1, length)
    source = ((entry.astype(F32) + 0.5) * (1.0 / number)).astype(jnp.int32)
    within = entry - source * number
    segment = jnp.zeros_like(entry)
    for h in range(1, segs):
        segment = segment + (within >= h * seg_rows).astype(jnp.int32)
    upper = (source >= half).astype(jnp.int32)
    row_key[...] = (source - half * upper) * rows + within - segment * seg_rows
    seg_key[...] = jnp.where(mask[...].reshape(1, length) != 0, upper * segs + segment, -1)


def text_blocks(length):
    whole = length // TBLOCK
    return whole, length - whole * TBLOCK


def one_hot(keys, depth):
    width = keys.shape[1]
    return (lax.broadcasted_iota(jnp.int32, (depth, width), 0) == keys).astype(F32).astype(BF16)


def scatter_block(start, width, row_ref, seg_ref, cot_ref, acc_ref):
    span = pl.ds(start, width)
    depth, side = acc_ref.shape[0], acc_ref.shape[1] // 2
    seg = seg_ref[:, span]
    cot = cot_ref[:, span].astype(F32)
    spread = jnp.concatenate(
        [jnp.where(seg == q, cot, 0.0).astype(BF16) for q in range(side // cot.shape[0])], axis=0
    )
    for k in range(2):
        hot = one_hot(row_ref[:, span] - k * depth, depth)
        acc_ref[:, k * side : (k + 1) * side] += contract(hot, spread, 1, 1)


class Sweep:
    def __init__(self, length, block):
        self.block, self.done = block, 0
        self.whole, self.tail = text_blocks(length)

    def go(self, low, high):
        last = high == SHARES
        low, high = low * self.whole // SHARES, high * self.whole // SHARES

        def step(i, carry):
            self.block(pl.multiple_of(i * TBLOCK, TBLOCK), TBLOCK)
            return carry

        if high > low:
            lax.fori_loop(low, high, step, 0)
        if last and self.tail:
            self.block(self.whole * TBLOCK, self.tail)


def lookup_block(start, width, row_ref, seg_ref, table_ref, out_ref):
    span = pl.ds(start, width)
    hot = one_hot(row_ref[:, span], table_ref.shape[1])
    seg = seg_ref[:, span]
    wide = jnp.dot(table_ref[...], hot, preferred_element_type=F32)
    feats = out_ref.shape[0]
    found = jnp.zeros((feats, width), F32)
    for q in range(table_ref.shape[0] // feats):
        found = found + jnp.where(seg == q, wide[q * feats : (q + 1) * feats], 0.0)
    out_ref[:, span] = found.astype(BF16)


def cast_pair(value):
    high = value.astype(BF16)
    return high, (value - high.astype(F32)).astype(BF16)


def head_ones():
    head_row = lax.broadcasted_iota(jnp.int32, (4 * HEAD, 4 * HEAD), 0) // HEAD
    head_col = lax.broadcasted_iota(jnp.int32, (4 * HEAD, 4 * HEAD), 1) // HEAD
    return (head_row == head_col).astype(F32).astype(BF16)


def head_sum(value, ones):
    high, low = cast_pair(value)
    step = 4 * HEAD
    return jnp.concatenate(
        [
            jnp.dot(high[:, j : j + step], ones, preferred_element_type=F32)
            + jnp.dot(low[:, j : j + step], ones, preferred_element_type=F32)
            for j in range(0, value.shape[1], step)
        ],
        axis=1,
    )


def flat(ref, low=None, high=None):
    value = ref[...] if low is None else ref[:, :, :, :, :, low:high]
    return value.reshape(-1, value.shape[-1])


def spread_segments(blocks, feats, segs):
    lane = lax.broadcasted_iota(jnp.int32, blocks[0].shape, 1) // feats
    out = []
    for h in range(segs):
        whole = None
        for j in range(segs):
            shift = ((j - h) * feats) % LANES
            moved = blocks[j] if shift == 0 else pltpu.roll(blocks[j], shift, 1)
            whole = moved if whole is None else jnp.where(lane == j, moved, whole)
        out.append(whole)
    return out


class Block:
    def __init__(self, m, segs, seg_rows, rows, feats):
        self.m, self.segs, self.seg_rows, self.rows, self.feats = m, segs, seg_rows, rows, feats
        self.number = m.pieces.shape[1]
        self.width = m.pieces.shape[2]
        self.total = segs * rows

    def pieces_of(self, h):
        return min(self.seg_rows, max(self.number - h * self.seg_rows, 0))

    def column(self, ref):
        line = lax.broadcasted_iota(jnp.int32, (self.total, 1), 0)
        segment, within = line // self.rows, line % self.rows
        entry = jnp.where(within < self.seg_rows, segment * self.seg_rows + within, -1)
        values = ref[...].reshape(1, self.number)
        lane = lax.broadcasted_iota(jnp.int32, (self.total, self.number), 1)
        return jnp.sum(jnp.where(lane == entry, values, 0), axis=1, keepdims=True)

    def load(self):
        m = self.m
        m.length_col[...] = self.column(m.lengths)
        m.group_col[...] = self.column(m.groups)
        for p in range(PIECES):
            value = m.pieces[p].astype(F32)
            for h in range(self.segs):
                low, base, count = h * self.seg_rows, h * self.rows, self.pieces_of(h)
                m.unit[p, base : base + count, :] = value[low : low + count]
                m.unit[p, base + count : base + self.rows, :] = jnp.zeros(
                    (self.rows - count, self.width), F32
                )

    def norm_one(self):
        m, width = self.m, self.width
        small = flat(m.w_out, width, width + LANES).astype(F32).T
        m.small[...] = small[:8]
        start = m.unit[0]
        for g in range(m.n_groups):
            start = start + jnp.where(m.group_col[...] == g, small[2 + g : 3 + g, :], 0.0)
        m.unit[0] = start
        m.hidden[...] = start

        def one(p, carry):
            value = m.unit[p]
            centered = value - jnp.mean(value, axis=1, keepdims=True)
            inv = lax.rsqrt(jnp.mean(centered * centered, axis=1, keepdims=True) + epsilon)
            unit = centered * inv
            m.unit[p] = unit
            m.inv_one[p] = jnp.broadcast_to(inv, (self.total, LANES))
            m.normed[p] = (unit * m.small[0:1, :]).astype(BF16)
            return carry

        lax.fori_loop(0, PIECES, one, 0)

    def project_qkv(self, i):
        m, width = self.m, self.width
        step = width // 2
        if i == 4:
            m.query[...] = jnp.dot(
                m.normed[0], flat(m.w_qkv, 0, width), preferred_element_type=F32
            ).astype(BF16)
            return
        m.key_value[:, :, i * step : (i + 1) * step] = (
            jnp.dot(
                m.normed[...].reshape(PIECES * self.total, width),
                flat(m.w_qkv, width + i * step, width + (i + 1) * step),
                preferred_element_type=F32,
            )
            .astype(BF16)
            .reshape(PIECES, self.total, step)
        )

    def score(self, i):
        m, width = self.m, self.width
        ones = head_ones()

        def score(p, carry):
            product = m.query[...].astype(F32) * m.key_value[p, :, :width].astype(F32)
            m.prob[p] = head_sum(product, ones) * (HEAD**-0.5)
            return carry

        lax.fori_loop(*self.half_of(PIECES, i), score, 0)

    def half_of(self, count, i):
        return i * count // 2, (i + 1) * count // 2

    def soft(self, half):
        m, width = self.m, self.width

        def soft(i, carry):
            span = pl.ds(pl.multiple_of(i * 16, 16), 16)
            length = m.length_col[span, :]
            scores = [
                jnp.where(p < length, m.prob[p, span, :], -1e30) for p in range(PIECES)
            ]
            highest = functools.reduce(jnp.maximum, scores)
            raised = [jnp.exp(s - highest) for s in scores]
            inv = 1.0 / functools.reduce(jnp.add, raised)
            total = jnp.zeros((16, width), F32)
            for p in range(PIECES):
                prob = raised[p] * inv
                m.prob[p, span, :] = prob
                total = total + prob.astype(BF16).astype(F32) * m.key_value[
                    p, span, width:
                ].astype(F32)
            m.attended[span, :] = total.astype(BF16)
            return carry

        lax.fori_loop(*self.half_of(self.total // 16, half), soft, 0)

    def norm_two(self):
        m, width = self.m, self.width
        hidden = m.hidden[...] + jnp.dot(
            m.attended[...], flat(m.w_out, 0, width), preferred_element_type=F32
        )
        m.hidden[...] = hidden
        centered = hidden - jnp.mean(hidden, axis=1, keepdims=True)
        inv = lax.rsqrt(jnp.mean(centered * centered, axis=1, keepdims=True) + epsilon)
        unit = centered * inv
        m.unit_two[...] = unit
        m.inv_two[...] = jnp.broadcast_to(inv, (self.total, LANES))
        m.normed_two[...] = (unit * m.small[1:2, :]).astype(BF16)

    def up(self, i):
        m, step = self.m, 2 * LANES
        tiles = m.activated.shape[1] // step

        def one(j, carry):
            span = pl.ds(pl.multiple_of(j * step, step), step)
            weight = m.w_up[:, :, :, :, :, span].reshape(self.width, step)
            upward = jnp.dot(m.normed_two[...], weight, preferred_element_type=F32)
            normal = 0.5 * (1.0 + lax.erf(upward * (0.5**0.5)))
            m.activated[:, span] = (upward * normal).astype(BF16)
            m.slope[:, span] = normal + upward * (
                jnp.exp(-0.5 * upward * upward) * 0.3989422804014327
            )
            return carry

        lax.fori_loop(i * tiles // 4, (i + 1) * tiles // 4, one, 0)

    def down(self):
        m = self.m
        m.output[...] = (
            m.hidden[...]
            + jnp.dot(m.activated[...], flat(m.w_down), preferred_element_type=F32)
        ).astype(BF16)

    def table(self, i):
        m, segs, rows = self.m, self.segs, self.rows
        step = m.w_proj.shape[-1] // 4
        wide = jnp.dot(
            m.output[...],
            flat(m.w_proj, i * step, (i + 1) * step),
            preferred_element_type=F32,
        )
        for g in range(step // LANES):
            value = wide[:, g * LANES : (g + 1) * LANES]
            parts = [value[h * rows : (h + 1) * rows] for h in range(segs)]
            for j, part in enumerate(spread_segments(parts, self.feats, segs)):
                m.came_grad[i * (step // self.feats) + g * segs + j] = part.astype(BF16)


    def table_back(self, i):
        m, segs, rows = self.m, self.segs, self.rows
        groups = m.grad_table.shape[1] // LANES

        def one(g, carry):
            span = pl.ds(pl.multiple_of(g * LANES, LANES), LANES)
            parts = [m.came_grad[g * segs + j].astype(F32) for j in range(segs)]
            for h, part in enumerate(spread_segments(parts, self.feats, segs)):
                m.grad_table[h * rows : (h + 1) * rows, span] = part.astype(BF16)
            return carry

        lax.fori_loop(*self.half_of(groups, i), one, 0)

    def put(self, ref, value):
        ref[...] = value.astype(BF16).reshape(ref.shape)

    def halves(self, value, i):
        half = value.shape[-1] // 2
        return value[:, i * half : (i + 1) * half]

    def proj_grad(self, i):
        m = self.m
        target = (m.d_proj0, m.d_proj1)[i]
        self.put(target, contract(m.output[...], self.halves(m.grad_table, i), 0, 0))

    def proj_back(self):
        m = self.m
        grad_output = contract(m.grad_table[...], flat(m.w_proj), 1, 1)
        m.grad_output[...] = grad_output
        m.grad_branch[...] = grad_output.astype(BF16)

    def down_grad(self, i):
        m = self.m
        target = (m.d_down0, m.d_down1)[i]
        self.put(target, contract(m.activated[...], self.halves(m.grad_branch, i), 0, 0))

    def down_back(self):
        m = self.m
        grad_act = contract(m.grad_branch[...], flat(m.w_down), 1, 1)
        m.activated[...] = (grad_act * m.slope[...]).astype(BF16)

    def up_grad(self, i):
        m = self.m
        target = (m.d_up0, m.d_up1)[i]
        self.put(target, contract(m.normed_two[...], self.halves(m.activated, i), 0, 0))

    def up_back(self):
        m = self.m
        grad = contract(m.activated[...], flat(m.w_up), 1, 1)
        m.d_small[...] = jnp.zeros_like(m.d_small)
        unit = m.unit_two[...]
        m.d_small[1:2, :] = jnp.sum(grad * unit, axis=0, keepdims=True)
        grad = grad * m.small[1:2, :]
        first = jnp.mean(grad, axis=1, keepdims=True)
        second = jnp.mean(grad * unit, axis=1, keepdims=True)
        hidden = m.grad_output[...] + m.inv_two[:, 0:1] * (grad - first - unit * second)
        m.hidden[...] = hidden
        m.grad_branch[...] = hidden.astype(BF16)

    def out_back(self):
        m, width = self.m, self.width
        m.d_out[:, :, :, :, :, :width] = (
            contract(m.attended[...], m.grad_branch[...], 0, 0)
            .astype(BF16)
            .reshape(m.d_out.shape[:-1] + (width,))
        )
        m.attended[...] = contract(m.grad_branch[...], flat(m.w_out, 0, width), 1, 1).astype(BF16)

    def back_score(self, i):
        m, width = self.m, self.width
        ones = head_ones()

        def score(p, carry):
            product = m.attended[...].astype(F32) * m.key_value[p, :, width:].astype(F32)
            m.grad_prob[p] = head_sum(product, ones)
            return carry

        lax.fori_loop(*self.half_of(PIECES, i), score, 0)

    def back_soft(self, half):
        m, width = self.m, self.width
        scale = HEAD**-0.5

        def soft(i, carry):
            span = pl.ds(pl.multiple_of(i * 16, 16), 16)
            inner = jnp.zeros((16, width), F32)
            for p in range(PIECES):
                inner = inner + m.prob[p, span, :] * m.grad_prob[p, span, :]
            query = m.query[span, :].astype(F32)
            grad_att = m.attended[span, :].astype(F32)
            grad_query = jnp.zeros((16, width), F32)
            for p in range(PIECES):
                prob = m.prob[p, span, :]
                low = prob.astype(BF16).astype(F32)
                grad = (prob * (m.grad_prob[p, span, :] - inner)).astype(BF16).astype(F32)
                grad_query = grad_query + grad * m.key_value[p, span, :width].astype(F32)
                m.key_value[p, span, :width] = (grad * query * scale).astype(BF16)
                m.key_value[p, span, width:] = (low * grad_att).astype(BF16)
            m.query[span, :] = (grad_query * scale).astype(BF16)
            return carry

        lax.fori_loop(*self.half_of(self.total // 16, half), soft, 0)

    def qkv_back(self, i):
        m, width = self.m, self.width
        if i == 4:
            self.put(m.d_q, contract(m.normed[0], m.query[...], 0, 0))
            return
        step = width // 2
        grad = contract(
            m.normed[...].reshape(PIECES * self.total, width),
            m.key_value[:, :, i * step : (i + 1) * step].reshape(PIECES * self.total, step),
            0,
            0,
        )
        target, low = (m.d_k, m.d_v)[i // 2], (i % 2) * step
        target[:, :, :, :, :, low : low + step] = grad.astype(BF16).reshape(
            target.shape[:-1] + (step,)
        )

    def normed_back(self):
        m, width = self.m, self.width
        m.grad_prob[...] = contract(
            m.key_value[...].reshape(PIECES * self.total, 2 * width),
            flat(m.w_qkv, width, 3 * width),
            1,
            1,
        ).reshape(PIECES, self.total, width)
        m.grad_prob[0] += contract(m.query[...], flat(m.w_qkv, 0, width), 1, 1)

    def norm_back(self):
        m, width = self.m, self.width
        gain = m.small[0:1, :]

        def back(p):
            grad = m.grad_prob[p]
            unit = m.unit[p]
            m.d_small[0:1, :] += jnp.sum(grad * unit, axis=0, keepdims=True)
            grad = grad * gain
            first = jnp.mean(grad, axis=1, keepdims=True)
            second = jnp.mean(grad * unit, axis=1, keepdims=True)
            grad = m.inv_one[p][:, 0:1] * (grad - first - unit * second)
            if p == 0:
                grad = grad + m.hidden[...]
                for g in range(m.n_groups):
                    m.d_small[2 + g : 3 + g, :] = jnp.sum(
                        jnp.where(m.group_col[...] == g, grad, 0.0), axis=0, keepdims=True
                    )
            for h in range(self.segs):
                low, base, count = h * self.seg_rows, h * self.rows, self.pieces_of(h)
                m.grad_output[low : low + count, :] = grad[base : base + count]
            m.grad_pieces[p] = m.grad_output[0 : self.number, :].astype(BF16)

        for p in range(PIECES):
            back(p)
        lead = m.d_out.shape[:-1]
        small = jnp.concatenate(
            [m.d_small[...], jnp.zeros((LANES - 8, width), F32)], axis=0
        ).T
        m.d_out[:, :, :, :, :, width:] = small.astype(BF16).reshape(lead + (LANES,))


def block_scratch(n, rows, total, width, hidden, out_width):
    return dict(
        length_col=((total, 1), jnp.int32),
        group_col=((total, 1), jnp.int32),
        unit=((PIECES, total, width), F32),
        inv_one=((PIECES, total, LANES), F32),
        small=((8, width), F32),
        normed=((PIECES, total, width), BF16),
        query=((total, width), BF16),
        key_value=((PIECES, total, 2 * width), BF16),
        prob=((PIECES, total, width), F32),
        attended=((total, width), BF16),
        hidden=((total, width), F32),
        unit_two=((total, width), F32),
        inv_two=((total, LANES), F32),
        normed_two=((total, width), BF16),
        activated=((total, hidden), BF16),
        slope=((total, hidden), F32),
        output=((total, width), BF16),
        grad_table=((total, out_width), BF16),
        grad_output=((total, width), F32),
        grad_branch=((total, width), BF16),
        d_small=((8, width), F32),
        grad_prob=((PIECES, total, width), F32),
    )


NAMES = ("out", "qkv", "up", "down", "proj")


SHARES = 18
SUMS = dict(
    proj0=("proj", 0),
    proj1=("proj", 1),
    down0=("down", 0),
    down1=("down", 1),
    up0=("up", 0),
    up1=("up", 1),
    k=("qkv", 1),
    v=("qkv", 2),
    q=("qkv", 0),
    out=("out", 0),
)


def main_kernel(n_entries, names, segs, seg_rows, rows, *refs):
    m = types.SimpleNamespace(**dict(zip(names, refs)))
    place = Place(n_entries)
    n, half = place.n, place.n // 2
    peers = partners(place)
    barrier = pltpu.get_barrier_semaphore()
    for peer in peers:
        pl.semaphore_signal(barrier, inc=1, device_id=peer, device_id_type=MESH)
    shard = m.ln1_gain.shape[0]
    width = m.i_pieces.shape[2]
    mine = {
        name: getattr(m, "w_" + name).at[place.z, place.x, place.c, place.y] for name in NAMES
    }
    targets = dict(
        i_ln1_gain=m.ln1_gain,
        i_ln2_gain=m.ln2_gain,
        i_group_table=m.group_table,
        i_out=mine["out"].at[:, :width],
        i_text_ids=m.text_ids,
        i_text_mask=m.text_mask,
        i_qkv=mine["qkv"],
        i_up=mine["up"],
        i_down=mine["down"],
        i_proj=mine["proj"],
        i_lengths=m.lengths,
        i_groups=m.groups,
        i_pieces=m.pieces,
        i_grad_embed=m.grad_embed,
    )
    inward = [
        pltpu.make_async_copy(getattr(m, name), target, m.i_sem.at[i])
        for i, (name, target) in enumerate(targets.items())
    ]
    for copy in inward:
        copy.start()
    m.n_groups = m.group_table.shape[0]
    feats = m.grad_embed.shape[0]
    block = Block(m, segs, seg_rows, rows, feats)
    gather, reduce = types.SimpleNamespace(), types.SimpleNamespace()
    for i, name in enumerate(NAMES):
        whole = getattr(m, "w_" + name)
        source = None if name == "out" else getattr(m, "i_" + name)
        setattr(gather, name, Gather(place, whole, m.g_send.at[i], m.g_recv.at[i], source))
    for i, name in enumerate(SUMS):
        held = [getattr(m, f"{kind}_{name}") for kind in ("d", "core", "one", "two", "along")]
        part = Reduce(place, *held, m.r_send.at[i], m.r_recv.at[i])
        part.stage, part.place_in = getattr(m, "t_" + name), SUMS[name][1]
        part.target = getattr(m, "o_" + SUMS[name][0])
        setattr(reduce, name, part)
    for copy in inward[:3]:
        copy.wait()
    small = jnp.concatenate(
        [
            m.ln1_gain[...].astype(F32).reshape(1, shard),
            m.ln2_gain[...].astype(F32).reshape(1, shard),
            m.group_table[...].astype(F32),
            jnp.zeros((6 - m.n_groups, shard), F32),
        ],
        axis=0,
    )
    small = jnp.concatenate([small, jnp.zeros((8, LANES - shard), F32)], axis=1).T
    small = jnp.concatenate([small[:shard], jnp.zeros((shard, LANES - 8), F32)], axis=1)
    mine["out"][:, width:] = small.astype(BF16)
    inward[3].wait()
    text_len = m.text_ids.shape[0]
    acc = m.grad_prob.reshape(PIECES * block.total, width)
    acc = acc.at[pl.ds(0, half * rows // 2), pl.ds(0, 4 * LANES)]
    scatter = Sweep(
        text_len,
        lambda start, count: scatter_block(
            start, count, m.row_key, m.seg_key, m.grad_embed, acc
        ),
    )
    lookup = Sweep(
        text_len,
        lambda start, count: lookup_block(
            start, count, m.row_key, m.seg_key, m.table, m.found
        ),
    )
    grad_way = (place, m.sent_grad, m.came_grad, m.xg_send, m.xg_recv)
    table_way = (place, m.came_grad, m.came_table, m.xt_send, m.xt_recv)
    going = []

    def send_out(source, target):
        going.append(pltpu.make_async_copy(source, target, m.o_sem.at[len(going)]))
        going[-1].start()

    def keys():
        for copy in inward[4:10]:
            copy.wait()
        text_keys(
            block.number, seg_rows, rows, segs, half, m.text_ids, m.text_mask, m.row_key, m.seg_key
        )
        acc[...] = jnp.zeros(acc.shape, F32)

    def load():
        for copy in inward[10:]:
            copy.wait()
        block.load()

    def pack(i, carry):
        span = pl.ds(pl.multiple_of(i * rows, rows), rows)
        for k in range(4):
            value = acc[span, k * LANES : (k + 1) * LANES]
            m.sent_grad[i + (k // 2) * (half // 2) + (k % 2) * half] = value.astype(BF16)
        return carry

    def scatter_end():
        lax.fori_loop(0, half // 2, pack, 0)

    def norm_back():
        block.norm_back()
        send_out(m.grad_pieces, m.o_pieces)

    def look_prep():
        for side in range(2):
            part = m.came_table[side * half : (side + 1) * half].reshape(half * rows, LANES)
            m.table[side * LANES : (side + 1) * LANES, :] = part.astype(F32).T.astype(BF16)

    def result(part):
        stage = part.stage
        part.z_wait(stage)
        if part is reduce.out:
            small = jnp.concatenate(
                [stage[:, width:], jnp.zeros((LANES - shard, LANES), F32)], axis=0
            ).T
            m.t_ln1[...] = small[0:1, :shard].reshape(shard)
            m.t_ln2[...] = small[1:2, :shard].reshape(shard)
            m.t_group[...] = small[2 : 2 + m.n_groups, :shard]
            send_out(m.t_ln1, m.o_ln1)
            send_out(m.t_ln2, m.o_ln2)
            send_out(m.t_group, m.o_group)
            send_out(stage.at[:, :width], m.o_out)
        else:
            columns = stage.shape[1]
            low = part.place_in * columns
            send_out(stage, part.target.at[:, low : low + columns])

    def sent_all():
        exchange_wait(*grad_way, True)
        for name in NAMES:
            getattr(gather, name).finish()

    pl.semaphore_wait(barrier, len(peers))
    gather.out.start()
    gather.qkv.start()
    keys()
    load()
    scatter.go(0, 5)
    gather.out.one_wait(0)
    gather.out.z_wait(0)
    scatter.go(5, 6)
    gather.out.z_wait(1)
    gather.qkv.one_wait(0)
    gather.out.z_wait(2)
    gather.up.start()
    scatter.go(6, 8)
    gather.qkv.z_wait(0)
    scatter.go(8, 10)
    gather.out.one_wait(1)
    scatter.go(10, 11)
    gather.out.one_wait(2)
    gather.qkv.z_wait(1)
    gather.out.one_wait(3)
    scatter.go(11, 13)
    gather.qkv.z_wait(2)
    gather.down.start()
    gather.out.two_wait()
    gather.up.one_wait(0)
    scatter.go(13, 15)
    gather.up.z_wait(0)
    gather.qkv.one_wait(1)
    scatter.go(15, 17)
    gather.qkv.one_wait(2)
    scatter.go(17, 18)
    scatter_end()
    gather.qkv.one_wait(3)
    gather.up.z_wait(1)
    gather.out.three_wait()
    gather.down.one_wait(0)
    gather.up.z_wait(2)
    gather.qkv.two_wait()
    gather.out.core_wait()
    exchange(*grad_way)
    gather.proj.start()
    gather.up.one_wait(1)
    gather.down.z_wait(0)
    gather.up.one_wait(2)
    gather.up.one_wait(3)
    gather.down.z_wait(1)
    gather.down.z_wait(2)
    gather.qkv.three_wait()
    gather.qkv.core_wait()
    block.norm_one()
    block.project_qkv(0)
    block.project_qkv(1)
    gather.up.two_wait()
    gather.proj.one_wait(0)
    block.project_qkv(2)
    block.project_qkv(3)
    gather.down.one_wait(1)
    block.project_qkv(4)
    block.score(0)
    gather.down.one_wait(2)
    block.score(1)
    block.soft(0)
    gather.down.one_wait(3)
    block.soft(1)
    block.norm_two()
    exchange_wait(*grad_way, False)
    block.table_back(0)
    block.table_back(1)
    gather.proj.z_wait(0)
    gather.up.three_wait()
    gather.down.two_wait()
    gather.up.core_wait()
    block.up(0)
    block.up(1)
    gather.proj.z_wait(1)
    block.up(2)
    block.up(3)
    gather.proj.z_wait(2)
    gather.proj.one_wait(1)
    gather.down.three_wait()
    gather.down.core_wait()
    block.down()
    gather.proj.one_wait(2)
    block.proj_grad(0)
    reduce.proj0.core_start()
    block.proj_grad(1)
    reduce.proj1.core_start()
    gather.proj.one_wait(3)
    gather.proj.two_wait()
    reduce.proj0.core_wait()
    reduce.proj1.core_wait()
    gather.proj.three_wait()
    gather.proj.core_wait()
    block.table(0)
    reduce.proj0.one_wait()
    block.table(1)
    block.table(2)
    block.table(3)
    exchange(*table_way)
    reduce.proj0.one_more_wait()
    block.proj_back()
    reduce.proj1.one_wait()
    block.down_grad(0)
    reduce.down0.core_start()
    block.down_grad(1)
    reduce.down1.core_start()
    block.down_back()
    block.up_grad(0)
    reduce.up0.core_start()
    reduce.down0.core_wait()
    reduce.proj0.two_wait()
    reduce.proj1.one_more_wait()
    block.up_grad(1)
    reduce.up1.core_start()
    block.up_back()
    block.out_back()
    reduce.down1.core_wait()
    block.back_score(0)
    block.back_score(1)
    block.back_soft(0)
    block.back_soft(1)
    block.qkv_back(0)
    block.qkv_back(1)
    reduce.k.core_start()
    reduce.up0.core_wait()
    block.qkv_back(2)
    block.qkv_back(3)
    reduce.v.core_start()
    block.qkv_back(4)
    reduce.q.core_start()
    reduce.down0.one_wait()
    reduce.proj1.two_wait()
    block.normed_back()
    reduce.down0.one_more_wait()
    exchange_wait(*table_way, False)
    reduce.up1.core_wait()
    norm_back()
    reduce.out.core_start()
    reduce.down1.one_wait()
    look_prep()
    lookup.go(0, 1)
    result(reduce.proj0)
    reduce.k.core_wait()
    reduce.down0.two_wait()
    reduce.down1.one_more_wait()
    lookup.go(1, 4)
    reduce.up0.one_wait()
    reduce.v.core_wait()
    result(reduce.proj1)
    lookup.go(4, 7)
    reduce.down1.two_wait()
    lookup.go(7, 8)
    reduce.up0.one_more_wait()
    reduce.q.core_wait()
    lookup.go(8, 9)
    result(reduce.down0)
    lookup.go(9, 10)
    reduce.out.core_wait()
    lookup.go(10, 11)
    reduce.up1.one_wait()
    lookup.go(11, 12)
    reduce.up0.two_wait()
    lookup.go(12, 13)
    reduce.up1.one_more_wait()
    lookup.go(13, 14)
    reduce.k.one_wait()
    lookup.go(14, 15)
    result(reduce.down1)
    lookup.go(15, 16)
    reduce.k.one_more_wait()
    sent_all()
    lookup.go(16, 18)
    reduce.v.one_wait()
    send_out(m.found, m.o_found)
    reduce.up1.two_wait()
    reduce.v.one_more_wait()
    result(reduce.up0)
    reduce.k.two_wait()
    reduce.q.one_wait()
    reduce.q.one_more_wait()
    reduce.v.two_wait()
    reduce.out.one_wait()
    result(reduce.up1)
    reduce.out.one_more_wait()
    reduce.q.two_wait()
    result(reduce.k)
    reduce.out.two_wait()
    result(reduce.v)
    result(reduce.q)
    result(reduce.out)
    exchange_wait(*table_way, True)
    for name in SUMS:
        getattr(reduce, name).finish()
    for copy in going:
        copy.wait()


def pieces_of_result(ref):
    if ref.shape[0] * ref.shape[-1] < 2**18 and len(ref.shape) < 3:
        return [ref]
    if len(ref.shape) == 3:
        return [ref.at[pl.ds(k, 1)] for k in range(ref.shape[0])]
    steps = max(ref.shape[0] // 16, 1)
    size = ref.shape[0] // steps
    return [ref.at[pl.ds(k * size, size)] for k in range(steps)]


def copy_kernel(count, *refs):
    ins, outs, held = refs[:count], refs[count : 2 * count], refs[2 * count : 3 * count]
    come, go = refs[3 * count :]
    ways = []
    for way in zip(ins, outs, held):
        for source, target, stage in zip(*map(pieces_of_result, way)):
            i = len(ways)
            ways.append(
                (
                    pltpu.make_async_copy(source, stage, come.at[i]),
                    pltpu.make_async_copy(stage, target, go.at[i]),
                )
            )
    for inward, _ in ways:
        inward.start()
    for inward, outward in ways:
        inward.wait()
        outward.start()
    for _, outward in ways:
        outward.wait()


def full(shape, dtype):
    return jax.ShapeDtypeStruct(shape, dtype)


def body(
    mesh_shape,
    pieces,
    lengths,
    entry_group,
    group_table,
    ln1_gain,
    w_qkv,
    w_out,
    ln2_gain,
    w_up,
    w_down,
    w_proj,
    text_ids,
    text_mask,
    grad_embed,
):
    n_entries = mesh_shape["entries"]
    n = n_entries * mesh_shape["feat"]
    n_z = n_entries // 4
    number, width = pieces.shape[0], pieces.shape[2]
    feats = grad_embed.shape[0]
    text_len = text_ids.shape[0]
    segs = LANES // feats
    seg_rows = -(-number // segs)
    rows = -(-seg_rows // 16) * 16
    half, total = n // 2, segs * rows
    pieces = jnp.transpose(pieces, (1, 0, 2))
    hbm = pl.BlockSpec(memory_space=pl.ANY)
    dma = pltpu.SemaphoreType.DMA

    ins = dict(
        i_pieces=pieces,
        i_lengths=lengths,
        i_groups=entry_group,
        i_group_table=group_table,
        i_ln1_gain=ln1_gain,
        i_qkv=w_qkv,
        i_out=w_out,
        i_ln2_gain=ln2_gain,
        i_up=w_up,
        i_down=w_down,
        i_proj=w_proj,
        i_text_ids=text_ids,
        i_text_mask=text_mask,
        i_grad_embed=grad_embed,
    )
    outs = dict(
        o_found=full((feats, text_len), BF16),
        o_pieces=full(pieces.shape, BF16),
        o_group=full(group_table.shape, F32),
        o_ln1=full(ln1_gain.shape, F32),
        o_qkv=full(w_qkv.shape, F32),
        o_out=full(w_out.shape, F32),
        o_ln2=full(ln2_gain.shape, F32),
        o_up=full(w_up.shape, F32),
        o_down=full(w_down.shape, F32),
        o_proj=full(w_proj.shape, F32),
    )
    scratch = {
        name: VMEM(*item)
        for name, item in block_scratch(
            n, rows, total, width, w_up.shape[1], w_proj.shape[1]
        ).items()
    }
    lead = (n_z, 2, 2, 2)
    shapes = dict(
        out=(w_out.shape[0], width + LANES),
        qkv=w_qkv.shape,
        up=w_up.shape,
        down=w_down.shape,
        proj=w_proj.shape,
    )
    for name, shape in shapes.items():
        scratch["w_" + name] = VMEM(lead + shape, BF16)
    for name, (whole, _) in SUMS.items():
        shape = shapes[whole]
        parts_n = 3 if whole == "qkv" else 1 if whole == "out" else 2
        shape = (shape[0], shape[1] // parts_n)
        scratch["d_" + name] = VMEM(lead + shape, BF16)
        scratch["t_" + name] = VMEM(shape, F32)
        scratch["core_" + name] = VMEM((n_z, 2, 2) + shape, BF16)
        scratch["one_" + name] = VMEM((2, n_z) + shape, BF16)
        scratch["two_" + name] = VMEM((n_z,) + shape, BF16)
        scratch["along_" + name] = VMEM((n_z - 1,) + shape, BF16)
    for name in ("sent_grad", "came_grad", "came_table"):
        scratch[name] = VMEM((n, rows, LANES), BF16)
    scratch.update(
        row_key=VMEM((1, text_len), jnp.int32),
        seg_key=VMEM((1, text_len), jnp.int32),
        table=VMEM((2 * LANES, half * rows), BF16),
        found=VMEM((feats, text_len), BF16),
        grad_pieces=VMEM(pieces.shape, BF16),
        i_sem=dma((len(ins),)),
        t_ln1=VMEM(ln1_gain.shape, F32),
        t_ln2=VMEM(ln2_gain.shape, F32),
        t_group=VMEM(group_table.shape, F32),
        g_send=dma((len(NAMES),)),
        g_recv=dma((len(NAMES), 2 * n_z + 2)),
        r_send=dma((len(SUMS),)),
        r_recv=dma((len(SUMS), 5)),
        xg_send=dma(()),
        xg_recv=dma(()),
        xt_send=dma(()),
        xt_recv=dma(()),
        o_sem=dma((len(SUMS) + 5,)),
    )
    for name in ("pieces", "lengths", "groups", "group_table", "ln1_gain", "ln2_gain"):
        scratch[name] = VMEM(ins["i_" + name].shape, ins["i_" + name].dtype)
    for name in ("text_ids", "text_mask", "grad_embed"):
        scratch[name] = VMEM(ins["i_" + name].shape, ins["i_" + name].dtype)
    results = pl.pallas_call(
        functools.partial(
            main_kernel,
            n_entries,
            tuple(ins) + tuple(outs) + tuple(scratch),
            segs,
            seg_rows,
            rows,
        ),
        out_shape=tuple(outs.values()),
        in_specs=[hbm] * len(ins),
        out_specs=(hbm,) * len(outs),
        scratch_shapes=list(scratch.values()),
        compiler_params=pltpu.CompilerParams(
            collective_id=0, has_side_effects=True, vmem_limit_bytes=VMEM_BYTES
        ),
    )(*ins.values())
    results = pl.pallas_call(
        functools.partial(copy_kernel, len(results)),
        out_shape=tuple(outs.values()),
        in_specs=[hbm] * len(results),
        out_specs=(hbm,) * len(results),
        scratch_shapes=[VMEM(leaf.shape, leaf.dtype) for leaf in outs.values()]
        + [dma((32,)), dma((32,))],
    )(*results)
    found, grad_pieces, *others = results
    return (found, jnp.transpose(grad_pieces, (1, 0, 2)), *others)


VMEM_BYTES = 63 * 2**20


def solution(mesh):
    both = P(AXES)
    rows = P(AXES, None)
    return jax.shard_map(
        functools.partial(body, dict(mesh.shape)),
        mesh=mesh,
        in_specs=(
            P(AXES, None, None),
            both,
            both,
            P(None, AXES),
            both,
            rows,
            rows,
            both,
            rows,
            rows,
            rows,
            P(),
            P(),
            rows,
        ),
        out_specs=(
            rows,
            P(AXES, None, None),
            P(None, AXES),
            both,
            rows,
            rows,
            both,
            rows,
            rows,
            rows,
        ),
        check_vma=False,
    )
```

```python
import functools
import types

import jax
import jax.numpy as jnp
from jax import lax
from jax.experimental import pallas as pl
from jax.experimental.pallas import tpu as pltpu
from jax.sharding import PartitionSpec as P

HEADS = 8
HEAD = 64
PIECES = 7
LANES = 128
TBLOCK = 512
AXES = ("entries", "feat")
MESH = pl.DeviceIdType.MESH
VMEM = pltpu.VMEM
BF16 = jnp.bfloat16
F32 = jnp.float32

epsilon = 1e-05


def contract(left_side, right_side, left_dim, right_dim):
    return lax.dot_general(
        left_side,
        right_side,
        (((left_dim,), (right_dim,)), ((), ())),
        preferred_element_type=jnp.float32,
    )


class Place:
    def __init__(self, n_entries):
        entry = lax.axis_index("entries")
        self.n_z = n_entries // 4
        self.n = n_entries * 2
        self.y = lax.axis_index("feat")
        self.c = lax.rem(entry, 2)
        self.x = lax.rem(lax.div(entry, 2), 2)
        self.z = lax.div(entry, 4)
        self.line = entry * 2 + self.y
        first = self.c == 0
        self.x1 = jnp.where(first, 1 - self.x, self.x)
        self.y1 = jnp.where(first, self.y, 1 - self.y)
        self.x2 = jnp.where(first, self.x, 1 - self.x)
        self.y2 = jnp.where(first, 1 - self.y, self.y)

    def at(self, z, x, c, y):
        return ((z * 2 + x) * 2 + c, y)

    def along_z(self, step):
        return lax.rem(self.z + step, self.n_z)


def partners(place):
    p = place
    return [p.at(p.along_z(k), p.x, p.c, p.y) for k in range(1, p.n_z)] + [
        p.at(p.z, p.x, 1 - p.c, p.y),
        p.at(p.z, p.x1, p.c, p.y1),
        p.at(p.z, p.x2, p.c, p.y2),
    ]


def remote(src, dst, send, recv, to):
    return pltpu.make_async_remote_copy(
        src_ref=src, dst_ref=dst, send_sem=send, recv_sem=recv, device_id=to, device_id_type=MESH
    )


def thirds(n_z):
    others = list(range(1, n_z))
    return [others[i * len(others) // 3 : (i + 1) * len(others) // 3] for i in range(3)]


class Gather:
    def __init__(self, place, whole, send, recv, source=None):
        p = self.place = place
        nz = p.n_z
        self.groups = thirds(nz)
        to_one = p.at(p.z, p.x1, p.c, p.y1)
        to_two = p.at(p.z, p.x2, p.c, p.y2)
        to_core = p.at(p.z, p.x, 1 - p.c, p.y)

        def shard(k, x, y):
            return whole.at[p.along_z(nz - k), x, p.c, y]

        def copy(ref, index, to):
            return remote(ref, ref, send, recv.at[index], to)

        def first(index, to):
            ref = shard(0, p.x, p.y)
            return remote(ref if source is None else source, ref, send, recv.at[index], to)

        self.along = {
            k: first(k - 1, p.at(p.along_z(k), p.x, p.c, p.y)) for k in range(1, nz)
        }
        self.one = [copy(shard(k, p.x, p.y), nz - 1 + k, to_one) for k in range(nz)]
        self.one[0] = first(nz - 1, to_one)
        base = 2 * nz - 1
        self.two = [copy(shard(k, p.x, p.y), base, to_two) for k in range(nz)]
        self.two[0] = first(base, to_two)
        self.three = [copy(shard(k, p.x1, p.y1), base + 1, to_two) for k in range(nz)]
        cols = [(p.x, p.y), (p.x1, p.y1), (p.x2, p.y2), (1 - p.x, 1 - p.y)]
        self.core = [copy(whole.at[:, x, p.c, y], base + 2, to_core) for x, y in cols]
        self.all_two = copy(whole.at[:, p.x, p.c, p.y], base, to_two)
        self.all_three = copy(whole.at[:, p.x1, p.c, p.y1], base + 1, to_two)
        self.all_core = copy(whole.at[:, :, p.c], base + 2, to_core)
        lines = whole.reshape((p.n,) + whole.shape[4:])
        self.all_sent = copy(lines.at[pl.ds(0, p.n - 1)], base, to_two)

    def start(self):
        for copy in self.along.values():
            copy.start()
        self.one[0].start()
        self.two[0].start()

    def z_wait(self, i):
        for k in self.groups[i]:
            self.along[k].wait_recv()
            self.one[k].start()
            self.two[k].start()
        if i == 2:
            self.core[0].start()

    def one_wait(self, i):
        for k in [0] if i == 0 else self.groups[i - 1]:
            self.one[k].wait_recv()
            self.three[k].start()
        if i == 3:
            self.core[1].start()

    def two_wait(self):
        self.all_two.wait_recv()
        self.core[2].start()

    def three_wait(self):
        self.all_three.wait_recv()
        self.core[3].start()

    def core_wait(self):
        self.all_core.wait_recv()

    def finish(self):
        self.all_sent.wait_send()


class Reduce:
    def __init__(self, place, parts, held_core, held_one, held_two, held_z, send, recv):
        p = self.place = place
        nz = p.n_z
        self.parts, self.held_core = parts, held_core
        self.held_one, self.held_two, self.held_z = held_one, held_two, held_z
        self.cols = [(p.x, p.y), (p.x1, p.y1), (p.x2, p.y2), (1 - p.x, 1 - p.y)]
        to_one = p.at(p.z, p.x1, p.c, p.y1)
        to_two = p.at(p.z, p.x2, p.c, p.y2)
        to_core = p.at(p.z, p.x, 1 - p.c, p.y)

        def col(k):
            return parts.at[:, self.cols[k][0], p.c, self.cols[k][1]]

        self.core = remote(parts.at[:, :, 1 - p.c], held_core, send, recv.at[0], to_core)
        self.one = [
            remote(col(1), held_one.at[0], send, recv.at[1], to_one),
            remote(col(3), held_one.at[1], send, recv.at[2], to_one),
        ]
        self.two = remote(col(2), held_two, send, recv.at[3], to_two)
        self.along = [
            remote(
                parts.at[p.along_z(k), p.x, p.c, p.y],
                held_z.at[k - 1],
                send,
                recv.at[4],
                p.at(p.along_z(k), p.x, p.c, p.y),
            )
            for k in range(1, nz)
        ]

        landed = held_z.at[pl.ds(0, nz - 1)]
        self.all_along = remote(landed, landed, send, recv.at[4], to_two)
        lines = parts.reshape((p.n,) + parts.shape[4:]).at[pl.ds(0, p.n - 1)]
        self.all_sent = remote(lines, lines, send, recv.at[4], to_two)

    def add(self, k, other):
        p, (x, y) = self.place, self.cols[k]
        self.parts[:, x, p.c, y] = (
            self.parts[:, x, p.c, y].astype(F32) + other.astype(F32)
        ).astype(BF16)

    def core_start(self):
        self.core.start()

    def core_wait(self):
        self.core.wait_recv()
        for k in (3, 1, 2, 0):
            x, y = self.cols[k]
            self.add(k, self.held_core[:, x, y])
            if k == 3:
                self.one[1].start()
            if k == 1:
                self.one[0].start()

    def one_wait(self):
        self.one[1].wait_recv()
        self.add(2, self.held_one[1])
        self.two.start()

    def one_more_wait(self):
        self.one[0].wait_recv()
        self.add(0, self.held_one[0])

    def two_wait(self):
        self.two.wait_recv()
        self.add(0, self.held_two[...])
        for copy in self.along:
            copy.start()

    def z_wait(self, out):
        p = self.place
        total = self.parts[p.z, p.x, p.c, p.y].astype(F32)
        self.all_along.wait_recv()
        for k in range(len(self.along)):
            total = total + self.held_z[k].astype(F32)
        out[...] = total

    def finish(self):
        self.all_sent.wait_send()


def exchange(place, src, dst, send, recv):
    dst[place.line] = src[place.line]

    def begin(step, carry):
        turn = lax.rem(step + 3 * place.n // 4 - 1, place.n - 1) + 1
        other = lax.rem(place.line + turn, place.n)
        to = (lax.div(other, 2), lax.rem(other, 2))
        remote(src.at[other], dst.at[place.line], send, recv, to).start()
        return carry

    lax.fori_loop(1, place.n, begin, 0)


def exchange_wait(place, src, dst, send, recv, sends):
    blocks = pl.ds(0, place.n - 1)
    other = lax.rem(place.line + 1, place.n)
    copy = remote(
        src.at[blocks], dst.at[blocks], send, recv, (lax.div(other, 2), lax.rem(other, 2))
    )
    if sends:
        copy.wait_send()
    else:
        copy.wait_recv()


def text_keys(number, seg_rows, rows, segs, half, ids, mask, row_key, seg_key):
    length = ids.shape[0]
    entry = ids[...].reshape(1, length)
    source = ((entry.astype(F32) + 0.5) * (1.0 / number)).astype(jnp.int32)
    within = entry - source * number
    segment = jnp.zeros_like(entry)
    for h in range(1, segs):
        segment = segment + (within >= h * seg_rows).astype(jnp.int32)
    upper = (source >= half).astype(jnp.int32)
    row_key[...] = (source - half * upper) * rows + within - segment * seg_rows
    seg_key[...] = jnp.where(mask[...].reshape(1, length) != 0, upper * segs + segment, -1)


def text_blocks(length):
    whole = length // TBLOCK
    return whole, length - whole * TBLOCK


def one_hot(keys, depth):
    width = keys.shape[1]
    return (lax.broadcasted_iota(jnp.int32, (depth, width), 0) == keys).astype(F32).astype(BF16)


def scatter_block(start, width, row_ref, seg_ref, cot_ref, acc_ref):
    span = pl.ds(start, width)
    depth, side = acc_ref.shape[0], acc_ref.shape[1] // 2
    seg = seg_ref[:, span]
    cot = cot_ref[:, span].astype(F32)
    spread = jnp.concatenate(
        [jnp.where(seg == q, cot, 0.0).astype(BF16) for q in range(side // cot.shape[0])], axis=0
    )
    for k in range(2):
        hot = one_hot(row_ref[:, span] - k * depth, depth)
        acc_ref[:, k * side : (k + 1) * side] += contract(hot, spread, 1, 1)


class Sweep:
    def __init__(self, length, block):
        self.block, self.done = block, 0
        self.whole, self.tail = text_blocks(length)

    def go(self, low, high):
        last = high == SHARES
        low, high = low * self.whole // SHARES, high * self.whole // SHARES

        def step(i, carry):
            self.block(pl.multiple_of(i * TBLOCK, TBLOCK), TBLOCK)
            return carry

        if high > low:
            lax.fori_loop(low, high, step, 0)
        if last and self.tail:
            self.block(self.whole * TBLOCK, self.tail)


def lookup_block(start, width, row_ref, seg_ref, table_ref, out_ref):
    span = pl.ds(start, width)
    hot = one_hot(row_ref[:, span], table_ref.shape[1])
    seg = seg_ref[:, span]
    wide = jnp.dot(table_ref[...], hot, preferred_element_type=F32)
    feats = out_ref.shape[0]
    found = jnp.zeros((feats, width), F32)
    for q in range(table_ref.shape[0] // feats):
        found = found + jnp.where(seg == q, wide[q * feats : (q + 1) * feats], 0.0)
    out_ref[:, span] = found.astype(BF16)


def cast_pair(value):
    high = value.astype(BF16)
    return high, (value - high.astype(F32)).astype(BF16)


def head_ones():
    head_row = lax.broadcasted_iota(jnp.int32, (4 * HEAD, 4 * HEAD), 0) // HEAD
    head_col = lax.broadcasted_iota(jnp.int32, (4 * HEAD, 4 * HEAD), 1) // HEAD
    return (head_row == head_col).astype(F32).astype(BF16)


def head_sum(value, ones):
    high, low = cast_pair(value)
    step = 4 * HEAD
    return jnp.concatenate(
        [
            jnp.dot(high[:, j : j + step], ones, preferred_element_type=F32)
            + jnp.dot(low[:, j : j + step], ones, preferred_element_type=F32)
            for j in range(0, value.shape[1], step)
        ],
        axis=1,
    )


def flat(ref, low=None, high=None):
    value = ref[...] if low is None else ref[:, :, :, :, :, low:high]
    return value.reshape(-1, value.shape[-1])


def spread_segments(blocks, feats, segs):
    lane = lax.broadcasted_iota(jnp.int32, blocks[0].shape, 1) // feats
    out = []
    for h in range(segs):
        whole = None
        for j in range(segs):
            shift = ((j - h) * feats) % LANES
            moved = blocks[j] if shift == 0 else pltpu.roll(blocks[j], shift, 1)
            whole = moved if whole is None else jnp.where(lane == j, moved, whole)
        out.append(whole)
    return out


class Block:
    def __init__(self, m, segs, seg_rows, rows, feats):
        self.m, self.segs, self.seg_rows, self.rows, self.feats = m, segs, seg_rows, rows, feats
        self.number = m.pieces.shape[1]
        self.width = m.pieces.shape[2]
        self.total = segs * rows

    def pieces_of(self, h):
        return min(self.seg_rows, max(self.number - h * self.seg_rows, 0))

    def column(self, ref):
        line = lax.broadcasted_iota(jnp.int32, (self.total, 1), 0)
        segment, within = line // self.rows, line % self.rows
        entry = jnp.where(within < self.seg_rows, segment * self.seg_rows + within, -1)
        values = ref[...].reshape(1, self.number)
        lane = lax.broadcasted_iota(jnp.int32, (self.total, self.number), 1)
        return jnp.sum(jnp.where(lane == entry, values, 0), axis=1, keepdims=True)

    def load(self):
        m = self.m
        m.length_col[...] = self.column(m.lengths)
        m.group_col[...] = self.column(m.groups)
        for p in range(PIECES):
            value = m.pieces[p].astype(F32)
            for h in range(self.segs):
                low, base, count = h * self.seg_rows, h * self.rows, self.pieces_of(h)
                m.unit[p, base : base + count, :] = value[low : low + count]
                m.unit[p, base + count : base + self.rows, :] = jnp.zeros(
                    (self.rows - count, self.width), F32
                )

    def norm_one(self):
        m, width = self.m, self.width
        small = flat(m.w_out, width, width + LANES).astype(F32).T
        m.small[...] = small[:8]
        start = m.unit[0]
        for g in range(m.n_groups):
            start = start + jnp.where(m.group_col[...] == g, small[2 + g : 3 + g, :], 0.0)
        m.unit[0] = start
        m.hidden[...] = start

        def one(p, carry):
            value = m.unit[p]
            centered = value - jnp.mean(value, axis=1, keepdims=True)
            inv = lax.rsqrt(jnp.mean(centered * centered, axis=1, keepdims=True) + epsilon)
            unit = centered * inv
            m.unit[p] = unit
            m.inv_one[p] = jnp.broadcast_to(inv, (self.total, LANES))
            m.normed[p] = (unit * m.small[0:1, :]).astype(BF16)
            return carry

        lax.fori_loop(0, PIECES, one, 0)

    def project_qkv(self, i):
        m, width = self.m, self.width
        step = width // 2
        if i == 4:
            m.query[...] = jnp.dot(
                m.normed[0], flat(m.w_qkv, 0, width), preferred_element_type=F32
            ).astype(BF16)
            return
        m.key_value[:, :, i * step : (i + 1) * step] = (
            jnp.dot(
                m.normed[...].reshape(PIECES * self.total, width),
                flat(m.w_qkv, width + i * step, width + (i + 1) * step),
                preferred_element_type=F32,
            )
            .astype(BF16)
            .reshape(PIECES, self.total, step)
        )

    def score(self, i):
        m, width = self.m, self.width
        ones = head_ones()

        def score(p, carry):
            product = m.query[...].astype(F32) * m.key_value[p, :, :width].astype(F32)
            m.prob[p] = head_sum(product, ones) * (HEAD**-0.5)
            return carry

        lax.fori_loop(*self.half_of(PIECES, i), score, 0)

    def half_of(self, count, i):
        return i * count // 2, (i + 1) * count // 2

    def soft(self, half):
        m, width = self.m, self.width

        def soft(i, carry):
            span = pl.ds(pl.multiple_of(i * 16, 16), 16)
            length = m.length_col[span, :]
            scores = [
                jnp.where(p < length, m.prob[p, span, :], -1e30) for p in range(PIECES)
            ]
            highest = functools.reduce(jnp.maximum, scores)
            raised = [jnp.exp(s - highest) for s in scores]
            inv = 1.0 / functools.reduce(jnp.add, raised)
            total = jnp.zeros((16, width), F32)
            for p in range(PIECES):
                prob = raised[p] * inv
                m.prob[p, span, :] = prob
                total = total + prob.astype(BF16).astype(F32) * m.key_value[
                    p, span, width:
                ].astype(F32)
            m.attended[span, :] = total.astype(BF16)
            return carry

        lax.fori_loop(*self.half_of(self.total // 16, half), soft, 0)

    def norm_two(self):
        m, width = self.m, self.width
        hidden = m.hidden[...] + jnp.dot(
            m.attended[...], flat(m.w_out, 0, width), preferred_element_type=F32
        )
        m.hidden[...] = hidden
        centered = hidden - jnp.mean(hidden, axis=1, keepdims=True)
        inv = lax.rsqrt(jnp.mean(centered * centered, axis=1, keepdims=True) + epsilon)
        unit = centered * inv
        m.unit_two[...] = unit
        m.inv_two[...] = jnp.broadcast_to(inv, (self.total, LANES))
        m.normed_two[...] = (unit * m.small[1:2, :]).astype(BF16)

    def up(self, i):
        m, step = self.m, 2 * LANES
        tiles = m.activated.shape[1] // step

        def one(j, carry):
            span = pl.ds(pl.multiple_of(j * step, step), step)
            weight = m.w_up[:, :, :, :, :, span].reshape(self.width, step)
            upward = jnp.dot(m.normed_two[...], weight, preferred_element_type=F32)
            normal = 0.5 * (1.0 + lax.erf(upward * (0.5**0.5)))
            m.activated[:, span] = (upward * normal).astype(BF16)
            m.slope[:, span] = normal + upward * (
                jnp.exp(-0.5 * upward * upward) * 0.3989422804014327
            )
            return carry

        lax.fori_loop(i * tiles // 4, (i + 1) * tiles // 4, one, 0)

    def down(self):
        m = self.m
        m.output[...] = (
            m.hidden[...]
            + jnp.dot(m.activated[...], flat(m.w_down), preferred_element_type=F32)
        ).astype(BF16)

    def table(self, i):
        m, segs, rows = self.m, self.segs, self.rows
        step = m.w_proj.shape[-1] // 4
        wide = jnp.dot(
            m.output[...],
            flat(m.w_proj, i * step, (i + 1) * step),
            preferred_element_type=F32,
        )
        for g in range(step // LANES):
            value = wide[:, g * LANES : (g + 1) * LANES]
            parts = [value[h * rows : (h + 1) * rows] for h in range(segs)]
            for j, part in enumerate(spread_segments(parts, self.feats, segs)):
                m.came_grad[i * (step // self.feats) + g * segs + j] = part.astype(BF16)


    def table_back(self, i):
        m, segs, rows = self.m, self.segs, self.rows
        groups = m.grad_table.shape[1] // LANES

        def one(g, carry):
            span = pl.ds(pl.multiple_of(g * LANES, LANES), LANES)
            parts = [m.came_grad[g * segs + j].astype(F32) for j in range(segs)]
            for h, part in enumerate(spread_segments(parts, self.feats, segs)):
                m.grad_table[h * rows : (h + 1) * rows, span] = part.astype(BF16)
            return carry

        lax.fori_loop(*self.half_of(groups, i), one, 0)

    def put(self, ref, value):
        ref[...] = value.astype(BF16).reshape(ref.shape)

    def halves(self, value, i):
        half = value.shape[-1] // 2
        return value[:, i * half : (i + 1) * half]

    def proj_grad(self, i):
        m = self.m
        target = (m.d_proj0, m.d_proj1)[i]
        self.put(target, contract(m.output[...], self.halves(m.grad_table, i), 0, 0))

    def proj_back(self):
        m = self.m
        grad_output = contract(m.grad_table[...], flat(m.w_proj), 1, 1)
        m.grad_output[...] = grad_output
        m.grad_branch[...] = grad_output.astype(BF16)

    def down_grad(self, i):
        m = self.m
        target = (m.d_down0, m.d_down1)[i]
        self.put(target, contract(m.activated[...], self.halves(m.grad_branch, i), 0, 0))

    def down_back(self):
        m = self.m
        grad_act = contract(m.grad_branch[...], flat(m.w_down), 1, 1)
        m.activated[...] = (grad_act * m.slope[...]).astype(BF16)

    def up_grad(self, i):
        m = self.m
        target = (m.d_up0, m.d_up1)[i]
        self.put(target, contract(m.normed_two[...], self.halves(m.activated, i), 0, 0))

    def up_back(self):
        m = self.m
        grad = contract(m.activated[...], flat(m.w_up), 1, 1)
        m.d_small[...] = jnp.zeros_like(m.d_small)
        unit = m.unit_two[...]
        m.d_small[1:2, :] = jnp.sum(grad * unit, axis=0, keepdims=True)
        grad = grad * m.small[1:2, :]
        first = jnp.mean(grad, axis=1, keepdims=True)
        second = jnp.mean(grad * unit, axis=1, keepdims=True)
        hidden = m.grad_output[...] + m.inv_two[:, 0:1] * (grad - first - unit * second)
        m.hidden[...] = hidden
        m.grad_branch[...] = hidden.astype(BF16)

    def out_back(self):
        m, width = self.m, self.width
        m.d_out[:, :, :, :, :, :width] = (
            contract(m.attended[...], m.grad_branch[...], 0, 0)
            .astype(BF16)
            .reshape(m.d_out.shape[:-1] + (width,))
        )
        m.attended[...] = contract(m.grad_branch[...], flat(m.w_out, 0, width), 1, 1).astype(BF16)

    def back_score(self, i):
        m, width = self.m, self.width
        ones = head_ones()

        def score(p, carry):
            product = m.attended[...].astype(F32) * m.key_value[p, :, width:].astype(F32)
            m.grad_prob[p] = head_sum(product, ones)
            return carry

        lax.fori_loop(*self.half_of(PIECES, i), score, 0)

    def back_soft(self, half):
        m, width = self.m, self.width
        scale = HEAD**-0.5

        def soft(i, carry):
            span = pl.ds(pl.multiple_of(i * 16, 16), 16)
            inner = jnp.zeros((16, width), F32)
            for p in range(PIECES):
                inner = inner + m.prob[p, span, :] * m.grad_prob[p, span, :]
            query = m.query[span, :].astype(F32)
            grad_att = m.attended[span, :].astype(F32)
            grad_query = jnp.zeros((16, width), F32)
            for p in range(PIECES):
                prob = m.prob[p, span, :]
                low = prob.astype(BF16).astype(F32)
                grad = (prob * (m.grad_prob[p, span, :] - inner)).astype(BF16).astype(F32)
                grad_query = grad_query + grad * m.key_value[p, span, :width].astype(F32)
                m.key_value[p, span, :width] = (grad * query * scale).astype(BF16)
                m.key_value[p, span, width:] = (low * grad_att).astype(BF16)
            m.query[span, :] = (grad_query * scale).astype(BF16)
            return carry

        lax.fori_loop(*self.half_of(self.total // 16, half), soft, 0)

    def qkv_back(self, i):
        m, width = self.m, self.width
        if i == 4:
            self.put(m.d_q, contract(m.normed[0], m.query[...], 0, 0))
            return
        step = width // 2
        grad = contract(
            m.normed[...].reshape(PIECES * self.total, width),
            m.key_value[:, :, i * step : (i + 1) * step].reshape(PIECES * self.total, step),
            0,
            0,
        )
        target, low = (m.d_k, m.d_v)[i // 2], (i % 2) * step
        target[:, :, :, :, :, low : low + step] = grad.astype(BF16).reshape(
            target.shape[:-1] + (step,)
        )

    def normed_back(self):
        m, width = self.m, self.width
        m.grad_prob[...] = contract(
            m.key_value[...].reshape(PIECES * self.total, 2 * width),
            flat(m.w_qkv, width, 3 * width),
            1,
            1,
        ).reshape(PIECES, self.total, width)
        m.grad_prob[0] += contract(m.query[...], flat(m.w_qkv, 0, width), 1, 1)

    def norm_back(self):
        m, width = self.m, self.width
        gain = m.small[0:1, :]

        def back(p):
            grad = m.grad_prob[p]
            unit = m.unit[p]
            m.d_small[0:1, :] += jnp.sum(grad * unit, axis=0, keepdims=True)
            grad = grad * gain
            first = jnp.mean(grad, axis=1, keepdims=True)
            second = jnp.mean(grad * unit, axis=1, keepdims=True)
            grad = m.inv_one[p][:, 0:1] * (grad - first - unit * second)
            if p == 0:
                grad = grad + m.hidden[...]
                for g in range(m.n_groups):
                    m.d_small[2 + g : 3 + g, :] = jnp.sum(
                        jnp.where(m.group_col[...] == g, grad, 0.0), axis=0, keepdims=True
                    )
            for h in range(self.segs):
                low, base, count = h * self.seg_rows, h * self.rows, self.pieces_of(h)
                m.grad_output[low : low + count, :] = grad[base : base + count]
            m.grad_pieces[p] = m.grad_output[0 : self.number, :].astype(BF16)

        for p in range(PIECES):
            back(p)
        lead = m.d_out.shape[:-1]
        small = jnp.concatenate(
            [m.d_small[...], jnp.zeros((LANES - 8, width), F32)], axis=0
        ).T
        m.d_out[:, :, :, :, :, width:] = small.astype(BF16).reshape(lead + (LANES,))


def block_scratch(n, rows, total, width, hidden, out_width):
    return dict(
        length_col=((total, 1), jnp.int32),
        group_col=((total, 1), jnp.int32),
        unit=((PIECES, total, width), F32),
        inv_one=((PIECES, total, LANES), F32),
        small=((8, width), F32),
        normed=((PIECES, total, width), BF16),
        query=((total, width), BF16),
        key_value=((PIECES, total, 2 * width), BF16),
        prob=((PIECES, total, width), F32),
        attended=((total, width), BF16),
        hidden=((total, width), F32),
        unit_two=((total, width), F32),
        inv_two=((total, LANES), F32),
        normed_two=((total, width), BF16),
        activated=((total, hidden), BF16),
        slope=((total, hidden), F32),
        output=((total, width), BF16),
        grad_table=((total, out_width), BF16),
        grad_output=((total, width), F32),
        grad_branch=((total, width), BF16),
        d_small=((8, width), F32),
        grad_prob=((PIECES, total, width), F32),
    )


NAMES = ("out", "qkv", "up", "down", "proj")


SHARES = 18
SUMS = dict(
    proj0=("proj", 0),
    proj1=("proj", 1),
    down0=("down", 0),
    down1=("down", 1),
    up0=("up", 0),
    up1=("up", 1),
    k=("qkv", 1),
    v=("qkv", 2),
    q=("qkv", 0),
    out=("out", 0),
)


def main_kernel(n_entries, names, segs, seg_rows, rows, *refs):
    m = types.SimpleNamespace(**dict(zip(names, refs)))
    place = Place(n_entries)
    n, half = place.n, place.n // 2
    peers = partners(place)
    barrier = pltpu.get_barrier_semaphore()
    for peer in peers:
        pl.semaphore_signal(barrier, inc=1, device_id=peer, device_id_type=MESH)
    shard = m.ln1_gain.shape[0]
    width = m.i_pieces.shape[2]
    mine = {
        name: getattr(m, "w_" + name).at[place.z, place.x, place.c, place.y] for name in NAMES
    }
    targets = dict(
        i_ln1_gain=m.ln1_gain,
        i_ln2_gain=m.ln2_gain,
        i_group_table=m.group_table,
        i_out=mine["out"].at[:, :width],
        i_text_ids=m.text_ids,
        i_text_mask=m.text_mask,
        i_qkv=mine["qkv"],
        i_up=mine["up"],
        i_down=mine["down"],
        i_proj=mine["proj"],
        i_lengths=m.lengths,
        i_groups=m.groups,
        i_pieces=m.pieces,
        i_grad_embed=m.grad_embed,
    )
    inward = [
        pltpu.make_async_copy(getattr(m, name), target, m.i_sem.at[i])
        for i, (name, target) in enumerate(targets.items())
    ]
    for copy in inward:
        copy.start()
    m.n_groups = m.group_table.shape[0]
    feats = m.grad_embed.shape[0]
    block = Block(m, segs, seg_rows, rows, feats)
    gather, reduce = types.SimpleNamespace(), types.SimpleNamespace()
    for i, name in enumerate(NAMES):
        whole = getattr(m, "w_" + name)
        source = None if name == "out" else getattr(m, "i_" + name)
        setattr(gather, name, Gather(place, whole, m.g_send.at[i], m.g_recv.at[i], source))
    for i, name in enumerate(SUMS):
        held = [getattr(m, f"{kind}_{name}") for kind in ("d", "core", "one", "two", "along")]
        part = Reduce(place, *held, m.r_send.at[i], m.r_recv.at[i])
        part.stage, part.place_in = getattr(m, "t_" + name), SUMS[name][1]
        part.target = getattr(m, "o_" + SUMS[name][0])
        setattr(reduce, name, part)
    for copy in inward[:3]:
        copy.wait()
    small = jnp.concatenate(
        [
            m.ln1_gain[...].astype(F32).reshape(1, shard),
            m.ln2_gain[...].astype(F32).reshape(1, shard),
            m.group_table[...].astype(F32),
            jnp.zeros((6 - m.n_groups, shard), F32),
        ],
        axis=0,
    )
    small = jnp.concatenate([small, jnp.zeros((8, LANES - shard), F32)], axis=1).T
    small = jnp.concatenate([small[:shard], jnp.zeros((shard, LANES - 8), F32)], axis=1)
    mine["out"][:, width:] = small.astype(BF16)
    inward[3].wait()
    text_len = m.text_ids.shape[0]
    acc = m.grad_prob.reshape(PIECES * block.total, width)
    acc = acc.at[pl.ds(0, half * rows // 2), pl.ds(0, 4 * LANES)]
    scatter = Sweep(
        text_len,
        lambda start, count: scatter_block(
            start, count, m.row_key, m.seg_key, m.grad_embed, acc
        ),
    )
    lookup = Sweep(
        text_len,
        lambda start, count: lookup_block(
            start, count, m.row_key, m.seg_key, m.table, m.found
        ),
    )
    grad_way = (place, m.sent_grad, m.came_grad, m.xg_send, m.xg_recv)
    table_way = (place, m.came_grad, m.came_table, m.xt_send, m.xt_recv)
    going = []

    def send_out(source, target):
        going.append(pltpu.make_async_copy(source, target, m.o_sem.at[len(going)]))
        going[-1].start()

    def keys():
        for copy in inward[4:10]:
            copy.wait()
        text_keys(
            block.number, seg_rows, rows, segs, half, m.text_ids, m.text_mask, m.row_key, m.seg_key
        )
        acc[...] = jnp.zeros(acc.shape, F32)

    def load():
        for copy in inward[10:]:
            copy.wait()
        block.load()

    def pack(i, carry):
        span = pl.ds(pl.multiple_of(i * rows, rows), rows)
        for k in range(4):
            value = acc[span, k * LANES : (k + 1) * LANES]
            m.sent_grad[i + (k // 2) * (half // 2) + (k % 2) * half] = value.astype(BF16)
        return carry

    def scatter_end():
        lax.fori_loop(0, half // 2, pack, 0)

    def norm_back():
        block.norm_back()
        send_out(m.grad_pieces, m.o_pieces)

    def look_prep():
        for side in range(2):
            part = m.came_table[side * half : (side + 1) * half].reshape(half * rows, LANES)
            m.table[side * LANES : (side + 1) * LANES, :] = part.astype(F32).T.astype(BF16)

    def result(part):
        stage = part.stage
        if part is reduce.out:
            for name in SUMS:
                if name != "out":
                    getattr(reduce, name).finish()
        part.z_wait(stage)
        if part is reduce.out:
            small = jnp.concatenate(
                [stage[:, width:], jnp.zeros((LANES - shard, LANES), F32)], axis=0
            ).T
            m.t_ln1[...] = small[0:1, :shard].reshape(shard)
            m.t_ln2[...] = small[1:2, :shard].reshape(shard)
            m.t_group[...] = small[2 : 2 + m.n_groups, :shard]
            send_out(m.t_ln1, m.o_ln1)
            send_out(m.t_ln2, m.o_ln2)
            send_out(m.t_group, m.o_group)
            send_out(stage.at[:, :width], m.o_out)
        else:
            columns = stage.shape[1]
            low = part.place_in * columns
            send_out(stage, part.target.at[:, low : low + columns])

    def sent_all():
        exchange_wait(*grad_way, True)
        exchange_wait(*table_way, True)
        for name in NAMES:
            getattr(gather, name).finish()

    pl.semaphore_wait(barrier, len(peers))
    gather.out.start()
    gather.qkv.start()
    keys()
    load()
    scatter.go(0, 5)
    gather.out.one_wait(0)
    gather.out.z_wait(0)
    scatter.go(5, 6)
    gather.out.z_wait(1)
    gather.qkv.one_wait(0)
    gather.out.z_wait(2)
    gather.up.start()
    scatter.go(6, 8)
    gather.qkv.z_wait(0)
    scatter.go(8, 10)
    gather.out.one_wait(1)
    scatter.go(10, 11)
    gather.out.one_wait(2)
    gather.qkv.z_wait(1)
    gather.out.one_wait(3)
    scatter.go(11, 13)
    gather.qkv.z_wait(2)
    gather.down.start()
    gather.out.two_wait()
    gather.up.one_wait(0)
    scatter.go(13, 15)
    gather.up.z_wait(0)
    gather.qkv.one_wait(1)
    scatter.go(15, 17)
    gather.qkv.one_wait(2)
    scatter.go(17, 18)
    scatter_end()
    gather.qkv.one_wait(3)
    gather.up.z_wait(1)
    gather.out.three_wait()
    gather.down.one_wait(0)
    gather.up.z_wait(2)
    gather.qkv.two_wait()
    gather.out.core_wait()
    exchange(*grad_way)
    gather.proj.start()
    gather.up.one_wait(1)
    gather.down.z_wait(0)
    gather.up.one_wait(2)
    gather.up.one_wait(3)
    gather.down.z_wait(1)
    gather.down.z_wait(2)
    gather.qkv.three_wait()
    gather.qkv.core_wait()
    block.norm_one()
    block.project_qkv(0)
    block.project_qkv(1)
    gather.up.two_wait()
    gather.proj.one_wait(0)
    block.project_qkv(2)
    block.project_qkv(3)
    gather.down.one_wait(1)
    block.project_qkv(4)
    block.score(0)
    gather.down.one_wait(2)
    block.score(1)
    block.soft(0)
    gather.down.one_wait(3)
    block.soft(1)
    block.norm_two()
    exchange_wait(*grad_way, False)
    block.table_back(0)
    block.table_back(1)
    gather.proj.z_wait(0)
    gather.up.three_wait()
    gather.down.two_wait()
    gather.up.core_wait()
    block.up(0)
    block.up(1)
    gather.proj.z_wait(1)
    block.up(2)
    block.up(3)
    gather.proj.z_wait(2)
    gather.proj.one_wait(1)
    gather.down.three_wait()
    gather.down.core_wait()
    block.down()
    gather.proj.one_wait(2)
    block.proj_grad(0)
    reduce.proj0.core_start()
    block.proj_grad(1)
    reduce.proj1.core_start()
    gather.proj.one_wait(3)
    gather.proj.two_wait()
    reduce.proj0.core_wait()
    reduce.proj1.core_wait()
    gather.proj.three_wait()
    gather.proj.core_wait()
    block.table(0)
    reduce.proj0.one_wait()
    block.table(1)
    block.table(2)
    block.table(3)
    exchange(*table_way)
    reduce.proj0.one_more_wait()
    block.proj_back()
    reduce.proj1.one_wait()
    block.down_grad(0)
    reduce.down0.core_start()
    block.down_grad(1)
    reduce.down1.core_start()
    block.down_back()
    block.up_grad(0)
    reduce.up0.core_start()
    reduce.down0.core_wait()
    reduce.proj0.two_wait()
    reduce.proj1.one_more_wait()
    block.up_grad(1)
    reduce.up1.core_start()
    block.up_back()
    block.out_back()
    reduce.down1.core_wait()
    block.back_score(0)
    block.back_score(1)
    block.back_soft(0)
    block.back_soft(1)
    block.qkv_back(0)
    block.qkv_back(1)
    reduce.k.core_start()
    reduce.up0.core_wait()
    block.qkv_back(2)
    block.qkv_back(3)
    reduce.v.core_start()
    block.qkv_back(4)
    reduce.q.core_start()
    reduce.down0.one_wait()
    reduce.proj1.two_wait()
    block.normed_back()
    reduce.down0.one_more_wait()
    exchange_wait(*table_way, False)
    reduce.up1.core_wait()
    norm_back()
    reduce.out.core_start()
    reduce.down1.one_wait()
    look_prep()
    lookup.go(0, 1)
    result(reduce.proj0)
    reduce.k.core_wait()
    reduce.down0.two_wait()
    reduce.down1.one_more_wait()
    lookup.go(1, 4)
    reduce.up0.one_wait()
    reduce.v.core_wait()
    result(reduce.proj1)
    lookup.go(4, 7)
    reduce.down1.two_wait()
    lookup.go(7, 8)
    reduce.up0.one_more_wait()
    reduce.q.core_wait()
    lookup.go(8, 9)
    result(reduce.down0)
    lookup.go(9, 10)
    reduce.out.core_wait()
    lookup.go(10, 11)
    reduce.up1.one_wait()
    lookup.go(11, 12)
    reduce.up0.two_wait()
    lookup.go(12, 13)
    reduce.up1.one_more_wait()
    lookup.go(13, 14)
    reduce.k.one_wait()
    lookup.go(14, 15)
    result(reduce.down1)
    lookup.go(15, 16)
    reduce.k.one_more_wait()
    sent_all()
    lookup.go(16, 18)
    reduce.v.one_wait()
    send_out(m.found, m.o_found)
    reduce.up1.two_wait()
    reduce.v.one_more_wait()
    result(reduce.up0)
    reduce.k.two_wait()
    reduce.q.one_wait()
    reduce.q.one_more_wait()
    reduce.v.two_wait()
    reduce.out.one_wait()
    result(reduce.up1)
    reduce.out.one_more_wait()
    reduce.q.two_wait()
    result(reduce.k)
    reduce.out.two_wait()
    result(reduce.v)
    result(reduce.q)
    result(reduce.out)
    reduce.out.finish()
    for copy in going:
        copy.wait()


def pieces_of_result(ref):
    if ref.shape[0] * ref.shape[-1] < 2**18 and len(ref.shape) < 3:
        return [ref]
    if len(ref.shape) == 3:
        return [ref.at[pl.ds(k, 1)] for k in range(ref.shape[0])]
    steps = max(ref.shape[0] // 16, 1)
    size = ref.shape[0] // steps
    return [ref.at[pl.ds(k * size, size)] for k in range(steps)]


def copy_kernel(count, *refs):
    ins, outs, held = refs[:count], refs[count : 2 * count], refs[2 * count : 3 * count]
    come, go = refs[3 * count :]
    ways = []
    for way in zip(ins, outs, held):
        for source, target, stage in zip(*map(pieces_of_result, way)):
            i = len(ways)
            ways.append(
                (
                    pltpu.make_async_copy(source, stage, come.at[i]),
                    pltpu.make_async_copy(stage, target, go.at[i]),
                )
            )
    for inward, _ in ways:
        inward.start()
    for inward, outward in ways:
        inward.wait()
        outward.start()
    for _, outward in ways:
        outward.wait()


def full(shape, dtype):
    return jax.ShapeDtypeStruct(shape, dtype)


def body(
    mesh_shape,
    pieces,
    lengths,
    entry_group,
    group_table,
    ln1_gain,
    w_qkv,
    w_out,
    ln2_gain,
    w_up,
    w_down,
    w_proj,
    text_ids,
    text_mask,
    grad_embed,
):
    n_entries = mesh_shape["entries"]
    n = n_entries * mesh_shape["feat"]
    n_z = n_entries // 4
    number, width = pieces.shape[0], pieces.shape[2]
    feats = grad_embed.shape[0]
    text_len = text_ids.shape[0]
    segs = LANES // feats
    seg_rows = -(-number // segs)
    rows = -(-seg_rows // 16) * 16
    half, total = n // 2, segs * rows
    pieces = jnp.transpose(pieces, (1, 0, 2))
    hbm = pl.BlockSpec(memory_space=pl.ANY)
    dma = pltpu.SemaphoreType.DMA

    ins = dict(
        i_pieces=pieces,
        i_lengths=lengths,
        i_groups=entry_group,
        i_group_table=group_table,
        i_ln1_gain=ln1_gain,
        i_qkv=w_qkv,
        i_out=w_out,
        i_ln2_gain=ln2_gain,
        i_up=w_up,
        i_down=w_down,
        i_proj=w_proj,
        i_text_ids=text_ids,
        i_text_mask=text_mask,
        i_grad_embed=grad_embed,
    )
    outs = dict(
        o_found=full((feats, text_len), BF16),
        o_pieces=full(pieces.shape, BF16),
        o_group=full(group_table.shape, F32),
        o_ln1=full(ln1_gain.shape, F32),
        o_qkv=full(w_qkv.shape, F32),
        o_out=full(w_out.shape, F32),
        o_ln2=full(ln2_gain.shape, F32),
        o_up=full(w_up.shape, F32),
        o_down=full(w_down.shape, F32),
        o_proj=full(w_proj.shape, F32),
    )
    scratch = {
        name: VMEM(*item)
        for name, item in block_scratch(
            n, rows, total, width, w_up.shape[1], w_proj.shape[1]
        ).items()
    }
    lead = (n_z, 2, 2, 2)
    shapes = dict(
        out=(w_out.shape[0], width + LANES),
        qkv=w_qkv.shape,
        up=w_up.shape,
        down=w_down.shape,
        proj=w_proj.shape,
    )
    for name, shape in shapes.items():
        scratch["w_" + name] = VMEM(lead + shape, BF16)
    for name, (whole, _) in SUMS.items():
        shape = shapes[whole]
        parts_n = 3 if whole == "qkv" else 1 if whole == "out" else 2
        shape = (shape[0], shape[1] // parts_n)
        scratch["d_" + name] = VMEM(lead + shape, BF16)
        scratch["t_" + name] = VMEM(shape, F32)
        scratch["core_" + name] = VMEM((n_z, 2, 2) + shape, BF16)
        scratch["one_" + name] = VMEM((2, n_z) + shape, BF16)
        scratch["two_" + name] = VMEM((n_z,) + shape, BF16)
        scratch["along_" + name] = VMEM((n_z - 1,) + shape, BF16)
    for name in ("sent_grad", "came_grad", "came_table"):
        scratch[name] = VMEM((n, rows, LANES), BF16)
    scratch.update(
        row_key=VMEM((1, text_len), jnp.int32),
        seg_key=VMEM((1, text_len), jnp.int32),
        table=VMEM((2 * LANES, half * rows), BF16),
        found=VMEM((feats, text_len), BF16),
        grad_pieces=VMEM(pieces.shape, BF16),
        i_sem=dma((len(ins),)),
        t_ln1=VMEM(ln1_gain.shape, F32),
        t_ln2=VMEM(ln2_gain.shape, F32),
        t_group=VMEM(group_table.shape, F32),
        g_send=dma((len(NAMES),)),
        g_recv=dma((len(NAMES), 2 * n_z + 2)),
        r_send=dma((len(SUMS),)),
        r_recv=dma((len(SUMS), 5)),
        xg_send=dma(()),
        xg_recv=dma(()),
        xt_send=dma(()),
        xt_recv=dma(()),
        o_sem=dma((len(SUMS) + 5,)),
    )
    for name in ("pieces", "lengths", "groups", "group_table", "ln1_gain", "ln2_gain"):
        scratch[name] = VMEM(ins["i_" + name].shape, ins["i_" + name].dtype)
    for name in ("text_ids", "text_mask", "grad_embed"):
        scratch[name] = VMEM(ins["i_" + name].shape, ins["i_" + name].dtype)
    results = pl.pallas_call(
        functools.partial(
            main_kernel,
            n_entries,
            tuple(ins) + tuple(outs) + tuple(scratch),
            segs,
            seg_rows,
            rows,
        ),
        out_shape=tuple(outs.values()),
        in_specs=[hbm] * len(ins),
        out_specs=(hbm,) * len(outs),
        scratch_shapes=list(scratch.values()),
        compiler_params=pltpu.CompilerParams(
            collective_id=0, has_side_effects=True, vmem_limit_bytes=VMEM_BYTES
        ),
    )(*ins.values())
    results = pl.pallas_call(
        functools.partial(copy_kernel, len(results)),
        out_shape=tuple(outs.values()),
        in_specs=[hbm] * len(results),
        out_specs=(hbm,) * len(results),
        scratch_shapes=[VMEM(leaf.shape, leaf.dtype) for leaf in outs.values()]
        + [dma((32,)), dma((32,))],
    )(*results)
    found, grad_pieces, *others = results
    return (found, jnp.transpose(grad_pieces, (1, 0, 2)), *others)


VMEM_BYTES = 63 * 2**20


def solution(mesh):
    both = P(AXES)
    rows = P(AXES, None)
    return jax.shard_map(
        functools.partial(body, dict(mesh.shape)),
        mesh=mesh,
        in_specs=(
            P(AXES, None, None),
            both,
            both,
            P(None, AXES),
            both,
            rows,
            rows,
            both,
            rows,
            rows,
            rows,
            P(),
            P(),
            rows,
        ),
        out_specs=(
            rows,
            P(AXES, None, None),
            P(None, AXES),
            both,
            rows,
            rows,
            both,
            rows,
            rows,
            rows,
        ),
        check_vma=False,
    )
```
